32 devices in a mesh: dom: 8 (over z, y), lvl: 4 (over x, core).
Axes of the slice: x: 2, y: 2, z: 4, core: 2. Of those that a mesh axis runs over, the one named last changes fastest.
Arguments:
- displacement: float32 [3, 131072], P(None, ('dom', 'lvl')), may hold values from -1.8 to 1.8
- velocity: float32 [3, 131072], P(None, ('dom', 'lvl')), may hold values from -6 to 6
- inverse_mass: float32 [131072], P(('dom', 'lvl')), may hold values from 0.5 to 2
- levels: int32 [2048], P(('dom', 'lvl')), may hold values from 0 to 3, as said below
- first_lame: float32 [2048], P(('dom', 'lvl')), may hold values from 0.125 to 32
- shear_modulus: float32 [2048], P(('dom', 'lvl')), may hold values from 0.125 to 32
- connectivity: int32 [125, 2048], P(None, ('dom', 'lvl')), may hold values from 0 to 4607, as said below
- owner_list: int32 [16384], P(('dom', 'lvl')), may hold values from 0 to 4095, as said below
Outputs:
- new_displacement: float32 [3, 131072], P(None, ('dom', 'lvl'))
- new_velocity: float32 [3, 131072], P(None, ('dom', 'lvl'))
The draws below stay inside these ranges and needn't reach their ends.
Inputs may be any that keep to these rules, and one draw needn't show every extreme that they name: `levels`: levels 0 to 3. On each device at most 16 elements have level 3, at most 24 level 2 or more, at most 32 level 1 or more; each of these bounds is met on one device of every row of 4 consecutive devices that share a dom index, and every such row holds exactly 32 elements of level 3. `connectivity`: the 125 entries of an element are distinct and form a conforming hexahedral mesh of slabs 2 elements thick chained from device to device in a loop; entries at least 4096 are ghost slots of the next device. `owner_list`: on each device, distinct owned nodes, matching the ghost slots of the previous device.
All inputs are finite; a program needn't handle non-finite values.
Results may differ from the reference program's by a relative error of at most 0.0001.
Values sent between devices are 32-bit elements; how exact they have to be, the bound alone decides.
A program may use at most 64 MiB of HBM per device.

```python
import math
import jax
import jax.numpy as jnp
import numpy as np
from jax import lax

SLAB_X = 2
SLAB_Y = 4
SLAB_Z = 8
ELEMS_DEV = 64
NODES_DEV = 4096
GHOSTS_DEV = 512
FINE_MOST = 16
MID_MOST = 24
COARSE_MOST = 32
ELEMS = 2048
NODES = 131072
N_LVL = 4
DEVICES = 32


def mesh_tables(key):
    base = jax.random.fold_in(key, 7)
    width_y = 4 * SLAB_Y
    width_z = 4 * SLAB_Z
    plane = width_y * width_z

    def device_perms(device):
        device_key = jax.random.fold_in(base, device)
        node_perm = jax.random.permutation(jax.random.fold_in(device_key, 1), NODES_DEV).astype(jnp.int32)
        ghost_perm = jax.random.permutation(jax.random.fold_in(device_key, 2), GHOSTS_DEV).astype(jnp.int32)
        return (node_perm, ghost_perm)
    node_perms, ghost_perms = jax.vmap(device_perms)(jnp.arange(DEVICES, dtype=jnp.int32))
    local_point = jnp.arange(125, dtype=jnp.int32)
    point_x = local_point // 25
    point_y = local_point // 5 % 5
    point_z = local_point % 5
    element = jnp.arange(ELEMS_DEV, dtype=jnp.int32)
    elem_x = element // (SLAB_Y * SLAB_Z)
    elem_y = element // SLAB_Z % SLAB_Y
    elem_z = element % SLAB_Z
    grid_x = 4 * elem_x[None, :] + point_x[:, None]
    grid_y = (4 * elem_y[None, :] + point_y[:, None]) % width_y
    grid_z = (4 * elem_z[None, :] + point_z[:, None]) % width_z
    plane_index = grid_y * width_z + grid_z
    own_index = jnp.clip(grid_x * plane + plane_index, 0, NODES_DEV - 1)

    def device_connect(node_perm, ghost_perm):
        return jnp.where(grid_x < 4 * SLAB_X, node_perm[own_index], NODES_DEV + ghost_perm[plane_index]).astype(jnp.int32)
    connect_all = jax.vmap(device_connect)(node_perms, ghost_perms)
    connect_all = jnp.transpose(connect_all, (1, 0, 2)).reshape(125, DEVICES * ELEMS_DEV)
    previous_ghost = jnp.roll(ghost_perms, 1, axis=0)

    def device_owner(node_perm, ghost_perm):
        inverse = jnp.zeros((GHOSTS_DEV,), jnp.int32).at[ghost_perm].set(jnp.arange(GHOSTS_DEV, dtype=jnp.int32))
        return node_perm[inverse]
    owner_all = jax.vmap(device_owner)(node_perms, previous_ghost).reshape(DEVICES * GHOSTS_DEV)
    return (connect_all, owner_all)


def draw_connectivity(key, part):
    return mesh_tables(key)[0]


def draw_owner_list(key, part):
    return mesh_tables(key)[1]


def draw_levels(key, part):
    row_count = DEVICES // N_LVL
    slots = jnp.arange(N_LVL, dtype=jnp.int32)

    def one_row(row):
        row_key = jax.random.fold_in(key, row)
        top = jax.random.randint(jax.random.fold_in(row_key, 1), (), 0, N_LVL)
        cuts = jnp.sort(jax.random.randint(jax.random.fold_in(row_key, 2), (N_LVL - 2,), 0, FINE_MOST + 1))
        bounds = jnp.concatenate([jnp.zeros((1,), jnp.int32), cuts.astype(jnp.int32), jnp.full((1,), FINE_MOST, jnp.int32)])
        pieces = bounds[1:] - bounds[:-1]
        other = jnp.clip(slots - (slots > top).astype(jnp.int32), 0, N_LVL - 2)
        fine_counts = jnp.where(slots == top, FINE_MOST, pieces[other])
        extra_mid = jax.random.randint(jax.random.fold_in(row_key, 3), (N_LVL,), 0, MID_MOST - FINE_MOST + 1)
        extra_mid = jnp.where(slots == top, MID_MOST - FINE_MOST, extra_mid)
        extra_coarse = jax.random.randint(jax.random.fold_in(row_key, 4), (N_LVL,), 0, COARSE_MOST - MID_MOST + 1)
        extra_coarse = jnp.where(slots == top, COARSE_MOST - MID_MOST, extra_coarse)
        mid_counts = fine_counts + extra_mid
        coarse_counts = mid_counts + extra_coarse

        def one_device(slot):
            order = jax.random.permutation(jax.random.fold_in(row_key, 10 + slot), ELEMS_DEV).astype(jnp.int32)
            level_of = (order < fine_counts[slot]).astype(jnp.int32) + (order < mid_counts[slot]).astype(jnp.int32) + (order < coarse_counts[slot]).astype(jnp.int32)
            return level_of
        return jax.vmap(one_device)(slots)
    return jax.vmap(one_row)(jnp.arange(row_count, dtype=jnp.int32)).reshape(DEVICES * ELEMS_DEV).astype(jnp.int32)


def level_factor(key, part):
    level_of = draw_levels(key, part)
    return jnp.where(level_of == 0, 0.25, jnp.where(level_of == 1, 1.0, jnp.where(level_of == 2, 4.0, 16.0))).astype(jnp.float32)


def material_unit(key, salt):
    material_key = jax.random.fold_in(jax.random.fold_in(key, 90001), salt)
    return jax.random.uniform(material_key, (ELEMS,), jnp.float32, 0.0, 1.0)


def draw_first_lame(key, part):
    unit = material_unit(key, 1)
    base_value = 0.5 * jnp.exp(unit * jnp.log(4.0))
    return (base_value * level_factor(key, part)).astype(jnp.float32)


def draw_shear_modulus(key, part):
    unit = material_unit(key, 2)
    base_value = 0.5 * jnp.exp(unit * jnp.log(4.0))
    return (base_value * level_factor(key, part)).astype(jnp.float32)


def block_levels(rng, extent, cuts, least, high):
    def one(axis_at, shards_of):
        steps = jax.random.uniform(jax.random.fold_in(jax.random.fold_in(rng, 6), axis_at), (shards_of,), jnp.float32, least / len(cuts), high / len(cuts))
        return jnp.repeat(jnp.exp(steps), extent[axis_at] // shards_of).reshape((-1,) + (1,) * (len(extent) - axis_at - 1))

    factor_of = one(*cuts[0])
    for cut in cuts[1:]:
        factor_of = factor_of * one(*cut)
    return factor_of


def gaussian(key, shape, spread, bound, cuts=(), kind=jnp.bfloat16):
    values = spread * jax.random.normal(key, shape, jnp.float32)
    if cuts:
        values = values * block_levels(key, shape, cuts, -0.22, 0.18)
    return jnp.clip(values, -bound, bound).astype(kind)


def setup_inputs(seed: int = 0) -> dict:
    key_list = jax.random.split(jax.random.key(seed), 9)
    return {
        "displacement": gaussian(key_list[0], (3, NODES), 0.3, 1.8, ((1, 32),), jnp.float32),
        "velocity": gaussian(key_list[1], (3, NODES), 1.0, 6.0, ((1, 32),), jnp.float32),
        "inverse_mass": jnp.clip(jnp.exp(math.log(2.0) - 1.3862944 * jax.random.uniform(key_list[2], (NODES,), jnp.float32) ** block_levels(key_list[2], (NODES,), ((0, 32),), -0.2, 0.2)), 0.5, 2.0),
        "levels": draw_levels(jax.random.fold_in(key_list[8], 71), 0),
        "first_lame": draw_first_lame(jax.random.fold_in(key_list[8], 71), 0),
        "shear_modulus": draw_shear_modulus(jax.random.fold_in(key_list[8], 71), 0),
        "connectivity": draw_connectivity(jax.random.fold_in(key_list[8], 71), 0),
        "owner_list": draw_owner_list(jax.random.fold_in(key_list[8], 71), 0),
    }


substep_length = 0.01

def lobatto_tables():
    points = np.array([-1.0, -np.sqrt(3.0 / 7.0), 0.0, np.sqrt(3.0 / 7.0), 1.0])
    weights = np.array([0.1, 49.0 / 90.0, 32.0 / 45.0, 49.0 / 90.0, 0.1])
    factor = np.array([np.prod([points[i] - points[k] for k in range(5) if k != i]) for i in range(5)])
    matrix = np.zeros((5, 5))
    for i in range(5):
        for j in range(5):
            if i == j:
                matrix[i, j] = sum((1.0 / (points[i] - points[k]) for k in range(5) if k != i))
            else:
                matrix[i, j] = factor[i] / (factor[j] * (points[i] - points[j]))
    cube = weights[:, None, None] * weights[None, :, None] * weights[None, None, :]
    return (jnp.asarray(matrix, jnp.float32), jnp.asarray(cube, jnp.float32))

def element_force(values, lame_first, lame_shear, tables):
    derivative, weight_cube = tables
    highest = lax.Precision.HIGHEST
    field = values.reshape(3, 5, 5, 5, -1)
    along_first = jnp.einsum('pi,cijkb->cpjkb', derivative, field, precision=highest)
    along_second = jnp.einsum('qj,cijkb->ciqkb', derivative, field, precision=highest)
    along_third = jnp.einsum('rk,cijkb->cijrb', derivative, field, precision=highest)
    gradient = jnp.stack([along_first, along_second, along_third], axis=1)
    divergence = along_first[0] + along_second[1] + along_third[2]
    unit_matrix = jnp.eye(3, dtype=jnp.float32)
    stress = lame_shear * (gradient + jnp.swapaxes(gradient, 0, 1)) + lame_first * divergence[None, None] * unit_matrix[:, :, None, None, None, None]
    weighted = stress * weight_cube[None, None, :, :, :, None]
    forces = jnp.einsum('pi,cpjkb->cijkb', derivative, weighted[:, 0], precision=highest)
    forces = forces + jnp.einsum('qj,ciqkb->cijkb', derivative, weighted[:, 1], precision=highest)
    forces = forces + jnp.einsum('rk,cijrb->cijkb', derivative, weighted[:, 2], precision=highest)
    return forces.reshape(3, 125, -1)

def reference(displacement, velocity, inverse_mass, levels, first_lame, shear_modulus, connectivity, owner_list):
    tables = lobatto_tables()
    local_ids = connectivity.reshape(125, DEVICES, ELEMS_DEV)
    device_ids = jnp.arange(DEVICES, dtype=jnp.int32)[None, :, None]
    successor = (device_ids + 1) % DEVICES
    owner_table = owner_list.reshape(DEVICES, GHOSTS_DEV)
    ghost_slot = jnp.clip(local_ids - NODES_DEV, 0, GHOSTS_DEV - 1)
    ghost_node = owner_table[successor, ghost_slot]
    global_ids = jnp.where(local_ids < NODES_DEV, device_ids * NODES_DEV + local_ids, successor * NODES_DEV + ghost_node).astype(jnp.int32)
    global_blocks = jnp.transpose(global_ids, (1, 0, 2))
    period = jnp.where(levels == 0, 8, jnp.where(levels == 1, 4, jnp.where(levels == 2, 2, 1))).astype(jnp.int32)
    lame_blocks = first_lame.reshape(DEVICES, ELEMS_DEV)
    shear_blocks = shear_modulus.reshape(DEVICES, ELEMS_DEV)
    for substep in range(8):
        weight = jnp.where(substep % period == 0, period.astype(jnp.float32), jnp.float32(0.0)).reshape(DEVICES, ELEMS_DEV)
        current = displacement

        def add_block(total, block_item):
            nodes_of, lame_first, lame_shear, weight_row = block_item
            forces = element_force(current[:, nodes_of], lame_first, lame_shear, tables) * weight_row[None, None, :]
            return (total.at[:, nodes_of].add(forces), None)
        assembled = lax.scan(add_block, jnp.zeros((3, NODES), jnp.float32), (global_blocks, lame_blocks, shear_blocks, weight))[0]
        velocity = velocity - substep_length * inverse_mass[None, :] * assembled
        displacement = displacement + substep_length * velocity
    return (displacement, velocity)
```

```python
import functools

import jax
import jax.numpy as jnp
import numpy as np
from jax import lax
from jax.experimental import pallas as pl
from jax.experimental.pallas import tpu as pltpu
from jax.sharding import PartitionSpec as P

substep_length = 0.01
substeps = 8
MESH = pl.DeviceIdType.MESH
f32 = jnp.float32
bf16 = jnp.bfloat16

BLOCK = (
    [(0, 0), (0, 1), (0, 2), (0, 3), (1, 0), (2, 0), (3, 0)]
    + [(b, c) for b in (1, 2, 3) for c in (1, 2, 3)]
)
CENTRE = BLOCK.index((2, 2))
HIGH = [(4, 0), (4, 1), (4, 2), (4, 3), (1, 4), (2, 4), (3, 4), (0, 4)]
PLANES = [(c, a) for c in range(3) for a in range(5)]
MAIN, FACE, TOTAL = 240, 120, 384


def lobatto_tables():
    points = np.array([-1.0, -np.sqrt(3.0 / 7.0), 0.0, np.sqrt(3.0 / 7.0), 1.0])
    weights = np.array([0.1, 49.0 / 90.0, 32.0 / 45.0, 49.0 / 90.0, 0.1])
    factor = np.array(
        [np.prod([points[i] - points[k] for k in range(5) if k != i]) for i in range(5)]
    )
    matrix = np.zeros((5, 5))
    for i in range(5):
        for j in range(5):
            if i == j:
                matrix[i, j] = sum((1.0 / (points[i] - points[k]) for k in range(5) if k != i))
            else:
                matrix[i, j] = factor[i] / (factor[j] * (points[i] - points[j]))
    cube = weights[:, None, None] * weights[None, :, None] * weights[None, None, :]
    return matrix, cube


def element_operator():
    derivative, cube = lobatto_tables()
    one = np.eye(5)
    along = [
        np.kron(np.kron(derivative, one), one),
        np.kron(np.kron(one, derivative), one),
        np.kron(np.kron(one, one), derivative),
    ]
    weight = cube.reshape(125)
    lame = np.zeros((3, 125, 3, 125))
    shear = np.zeros((3, 125, 3, 125))
    for c in range(3):
        for a in range(3):
            lame[c, :, a, :] += along[c].T @ (weight[:, None] * along[a])
            shear[c, :, c, :] += along[a].T @ (weight[:, None] * along[a])
            shear[c, :, a, :] += along[a].T @ (weight[:, None] * along[c])
    rows = []
    for c, a in PLANES:
        rows += [c * 125 + a * 25 + b * 5 + k for b, k in BLOCK]
    for c, a in PLANES:
        rows += [c * 125 + a * 25 + b * 5 + k for b, k in HIGH]
    for c, a in PLANES:
        rows.append(c * 125 + a * 25 + 24)
    rows = np.array(rows)
    full = np.zeros((TOTAL, 2 * TOTAL))
    full[: len(rows), : len(rows)] = lame.reshape(375, 375)[np.ix_(rows, rows)]
    full[: len(rows), TOTAL : TOTAL + len(rows)] = shear.reshape(375, 375)[np.ix_(rows, rows)]
    high = full.astype(jnp.bfloat16)
    low = (full - high.astype(np.float64)).astype(jnp.bfloat16)
    return np.concatenate([high, low], axis=0)


def node_row(a, b, c):
    return a * 25 + b * 5 + c


NAMES = [
    node_row(2, 0, 2), node_row(2, 4, 2),
    node_row(2, 2, 0), node_row(2, 2, 4),
    node_row(2, 0, 0), node_row(2, 4, 4),
    node_row(0, 2, 2), node_row(4, 2, 2),
]


def lanes(shape):
    return lax.broadcasted_iota(jnp.int32, shape, len(shape) - 1)


def sublanes(shape):
    return lax.broadcasted_iota(jnp.int32, shape, len(shape) - 2)


def split_two(x):
    high = x.astype(bf16).astype(f32)
    return jnp.where(lanes(x.shape) < 64, high, x - high).astype(bf16)


def split_three(x):
    high = x.astype(bf16).astype(f32)
    rest = x - high
    middle = rest.astype(bf16).astype(f32)
    first = jnp.where(lanes(x.shape) < 64, high, middle).astype(bf16)
    second = jnp.where(lanes(x.shape) < 64, rest - middle, 0.0).astype(bf16)
    return jnp.concatenate([first, second], axis=1)


def moved(parts, matrix):
    return jnp.dot(parts, matrix, preferred_element_type=f32)


def same(column, row):
    return jnp.where(column == row, 1.0, 0.0).astype(bf16)


def kernel(
    disp_ref, vel_ref, mass_ref, level_ref, lame_ref, shear_ref, conn_ref, owner_ref, oper_ref,
    out_u_ref, out_v_ref,
    conn_s, tile_s, pick_s, hot_hi, hot_lo, u_s, v_s, m_s, f_s, x_s, elem_s,
    low_out, low_in, name_out, name_in, send_buf, recv_buf,
    init_send, init_recv, step_send, step_recv,
):
    dom_size, lvl_size = lax.axis_size("dom"), lax.axis_size("lvl")
    count = dom_size * lvl_size
    me = lax.axis_index("dom") * lvl_size + lax.axis_index("lvl")
    after = lax.rem(me + 1, count)
    before = lax.rem(me + count - 1, count)
    after_id = (after // lvl_size, lax.rem(after, lvl_size))
    before_id = (before // lvl_size, lax.rem(before, lvl_size))

    barrier = pltpu.get_barrier_semaphore()
    for other in (after_id, before_id):
        pl.semaphore_signal(barrier, inc=1, device_id=other, device_id_type=MESH)

    conn_s[:, 0:64] = conn_ref[...]
    conn_s[:, 64:128] = conn_ref[...]
    for row, ref in enumerate((level_ref, lame_ref, shear_ref)):
        elem_s[row : row + 1, 0:64] = ref[...].astype(f32)
        elem_s[row : row + 1, 64:128] = ref[...].astype(f32)

    low_half = lanes((1, 128)) < 64
    for a in range(2):
        for j, (b, c) in enumerate(BLOCK):
            r0, r1 = node_row(a, b, c), node_row(a + 2, b, c)
            pick_s[a * 16 + j : a * 16 + j + 1, :] = jnp.where(
                low_half, conn_s[r0 : r0 + 1, :], conn_s[r1 : r1 + 1, :]
            )
    pick = pick_s[...]
    pick_hi, pick_lo = lax.shift_right_logical(pick, 7), lax.bitwise_and(pick, 127)

    def gather_step(t, kept):
        here = pick_hi == t
        cols = pl.ds(pl.multiple_of(t * 128, 128), 128)
        rows = [disp_ref[c : c + 1, cols] for c in range(3)]
        rows += [vel_ref[c : c + 1, cols] for c in range(3)]
        rows.append(mass_ref[pl.ds(t, 1), :])
        new = []
        for row, old in zip(rows, kept):
            got = jnp.take_along_axis(
                jnp.broadcast_to(row, (32, 128)), pick_lo, axis=1, mode="promise_in_bounds"
            )
            new.append(jnp.where(here, got, old))
        return tuple(new)

    got = lax.fori_loop(
        0, 32, gather_step, tuple(jnp.zeros((32, 128), f32) for _ in range(7)), unroll=4
    )
    half = lanes((32, 128)) < 64
    for k, ref in enumerate([u_s] * 3 + [v_s] * 3 + [m_s]):
        turned = pltpu.roll(got[k], 64, axis=1)
        base = (k % 3) * 80 if k < 6 else 0
        ref[base : base + 32, :] = jnp.where(half, got[k], turned)
        ref[base + 32 : base + 64, :] = jnp.where(half, turned, got[k])
    u_s[MAIN : MAIN + 16, :] = jnp.zeros((16, 128), f32)
    f_s[MAIN : MAIN + 16, :] = jnp.zeros((16, 128), f32)

    tile_s[...] = jnp.zeros((128, 128), f32)
    for k, r in enumerate(NAMES):
        tile_s[k : k + 1, :] = conn_s[r : r + 1, :].astype(f32)
    tile_s[8:12, :] = owner_ref[...].astype(f32)
    columns = jnp.transpose(tile_s[...])
    name_row = [tile_s[k : k + 1, :] for k in range(8)]
    name_col = [columns[:, k : k + 1] for k in range(8)]
    slot_low = jnp.full((1, 128), -9999.0, f32)
    for k in range(4):
        hit = columns[:, 8 + k : 9 + k] == name_row[6]
        number = sublanes((128, 128)).astype(f32) + (k * 128 + 9999)
        slot_low = slot_low + jnp.sum(jnp.where(hit, number, 0.0), axis=0, keepdims=True)
    owned = 4096.0
    slot_high = name_row[7] - owned
    for k in range(3):
        low_out[k * 16 : k * 16 + 16, :] = u_s[k * 80 : k * 80 + 16, :]
        low_out[48 + k * 16 : 64 + k * 16, :] = v_s[k * 80 : k * 80 + 16, :]
    low_out[96:112, :] = m_s[0:16, :]
    low_out[112:120, :] = jnp.broadcast_to(slot_low, (8, 128))
    name_out[...] = jnp.broadcast_to(slot_high, (8, 128))

    pl.semaphore_wait(barrier, 2)
    low_copy = pltpu.make_async_remote_copy(
        src_ref=low_out, dst_ref=low_in, send_sem=init_send.at[0], recv_sem=init_recv.at[0],
        device_id=before_id, device_id_type=MESH,
    )
    name_copy = pltpu.make_async_remote_copy(
        src_ref=name_out, dst_ref=name_in, send_sem=init_send.at[1], recv_sem=init_recv.at[1],
        device_id=after_id, device_id_type=MESH,
    )
    low_copy.start()
    name_copy.start()

    spread = jnp.concatenate(
        [same(name_col[0], name_row[1]), same(name_col[2], name_row[3])], axis=1
    )
    spread = jnp.concatenate([spread, spread], axis=0)
    spread_edge = same(name_col[4], name_row[5])
    spread_edge = jnp.concatenate([spread_edge, spread_edge], axis=0)
    collect = jnp.concatenate(
        [same(name_col[1], name_row[0]), same(name_col[3], name_row[2])], axis=1
    )
    collect_edge = same(name_col[5], name_row[4])
    to_high = same(name_col[6], name_row[7])
    to_low = same(name_col[7], name_row[6])

    row_hi, row_lo = pick_hi, pick_lo
    for r in range(32):
        cols = slice(r * 128, r * 128 + 128)
        hit = row_hi[r : r + 1, :] == sublanes((32, 128))
        hot_hi[0:32, cols] = jnp.where(hit, lanes((32, 128)).astype(f32), 0.0).astype(bf16)
        hot_hi[32:64, cols] = jnp.where(hit, float(r), 0.0).astype(bf16)
        hot_lo[:, cols] = same(sublanes((128, 128)), row_lo[r : r + 1, :])
    place = lax.dot_general(
        hot_hi[...], hot_lo[...], (((1,), (1,)), ((), ())), preferred_element_type=f32
    )
    place_lane = place[0:32].astype(jnp.int32)
    place_row = place[32:64].astype(jnp.int32)

    low_copy.wait()
    name_copy.wait()
    tile_s[0:8, :] = low_in[112:120, :]
    tile_s[8:16, :] = name_in[...]
    columns = jnp.transpose(tile_s[...])
    from_after = same(columns[:, 0:1], slot_high)
    from_before = same(columns[:, 8:9], slot_low)
    to_high_twice = jnp.concatenate([to_high, to_high], axis=0)
    from_after_twice = jnp.concatenate([from_after, from_after], axis=0)
    high = moved(split_three(low_out[0:112, :]), to_high_twice)
    high = high + moved(split_three(low_in[0:112, :]), from_after_twice)
    for k in range(3):
        u_s[k * 80 + 64 : k * 80 + 80, :] = high[k * 16 : k * 16 + 16]
        v_s[k * 80 + 64 : k * 80 + 80, :] = high[48 + k * 16 : 64 + k * 16]
    m_s[64:80, :] = high[96:112]

    level = elem_s[0:1, :]
    period = jnp.where(level == 0.0, 8, jnp.where(level == 1.0, 4, jnp.where(level == 2.0, 2, 1)))
    row8 = sublanes((15, 8, 128))

    def advance(rows, force):
        c_rows = pl.ds(rows[0] * 80 + rows[1] * 16, 16)
        mass = m_s[pl.ds(rows[1] * 16, 16), :]
        speed = v_s[c_rows, :] - substep_length * mass * force
        v_s[c_rows, :] = speed
        u_s[c_rows, :] = u_s[c_rows, :] + substep_length * speed

    def substep(s, carry):
        u = u_s[0:MAIN, :].reshape(15, 16, 128)
        faces = moved(split_three(u[:, 0:8].reshape(FACE, 128)), spread)
        along_y = faces[:, 0:128].reshape(15, 8, 128)
        along_z = faces[:, 128:256].reshape(15, 8, 128)
        face = jnp.where(
            row8 < 4, along_y, jnp.where(row8 < 7, along_z, pltpu.roll(along_z, 7, axis=1))
        )
        edge = moved(split_three(u_s[pl.ds(0, 16, stride=16), :]), spread_edge)
        centres = [
            u_s[c * 80 + 32 + CENTRE : c * 80 + 33 + CENTRE, :] for c in range(3)
        ]
        row16 = sublanes((16, 128))
        edge = edge - jnp.where(
            row16 < 5, centres[0], jnp.where(row16 < 10, centres[1], centres[2])
        )
        edge = jnp.where(row16 < 15, edge, 0.0)
        active = lax.rem(jnp.full((1, 128), s, jnp.int32), period) == 0
        weight = jnp.where(active, period.astype(f32), 0.0)
        for part, value in enumerate((elem_s[1:2, :] * weight, elem_s[2:3, :] * weight)):
            at = part * TOTAL
            for c in range(3):
                main = (u[c * 5 : c * 5 + 5].reshape(80, 128) - centres[c]) * value
                x_s[at + c * 80 : at + c * 80 + 80, :] = split_two(main)
            both = [
                (face[c * 5 : c * 5 + 5].reshape(40, 128) - centres[c]) * value for c in range(3)
            ]
            both += [edge * value, jnp.zeros((8, 128), f32)]
            x_s[at + MAIN : at + TOTAL, :] = split_two(jnp.concatenate(both, axis=0))
        product = jnp.dot(oper_ref[...], x_s[...], preferred_element_type=f32)
        force = product[0:TOTAL] + product[TOTAL : 2 * TOTAL]
        force = force + pltpu.roll(force, 64, axis=1)

        face = moved(split_two(force[MAIN : MAIN + FACE]), collect)
        along_y = face[:, 0:128].reshape(15, 8, 128)
        along_z = face[:, 128:256].reshape(15, 8, 128)
        low = jnp.where(row8 < 4, along_y, jnp.where(row8 < 7, along_z, 0.0))
        low = low + jnp.where(row8 == 0, pltpu.roll(along_z, 1, axis=1), 0.0)
        main = force[0:MAIN].reshape(15, 2, 8, 128)
        main = jnp.concatenate([main[:, 0:1] + low[:, None], main[:, 1:2]], axis=1)
        f_s[0:MAIN, :] = main.reshape(MAIN, 128)
        edge = moved(split_two(force[MAIN + FACE : MAIN + FACE + 16]), collect_edge)
        f_s[pl.ds(0, 16, stride=16), :] = f_s[pl.ds(0, 16, stride=16), :] + edge

        low_x = jnp.concatenate([f_s[c * 80 : c * 80 + 16, :] for c in range(3)], axis=0)
        high_x = jnp.concatenate([f_s[c * 80 + 64 : c * 80 + 80, :] for c in range(3)], axis=0)
        send_buf[s, 0] = low_x
        send_buf[s, 1] = high_x
        copies = [
            pltpu.make_async_remote_copy(
                src_ref=send_buf.at[s, way], dst_ref=recv_buf.at[s, way],
                send_sem=step_send.at[s, way], recv_sem=step_recv.at[s, way],
                device_id=other, device_id_type=MESH,
            )
            for way, other in enumerate((before_id, after_id))
        ]
        copies[1].start()
        copies[0].start()
        low_sum = low_x + moved(split_two(high_x), to_low)
        high_sum = high_x + moved(split_two(low_x), to_high)
        for c in range(3):
            for a in (1, 2, 3):
                advance((c, a), f_s[c * 80 + a * 16 : c * 80 + a * 16 + 16, :])
        copies[1].wait()
        copies[0].wait()
        low_sum = low_sum + moved(split_two(recv_buf[s, 1]), from_before)
        high_sum = high_sum + moved(split_two(recv_buf[s, 0]), from_after)
        for c in range(3):
            advance((c, 0), low_sum[c * 16 : c * 16 + 16])
            advance((c, 4), high_sum[c * 16 : c * 16 + 16])
        return carry

    lax.fori_loop(0, substeps, substep, 0)

    for ref in (u_s, v_s):
        for c in range(3):
            first = ref[c * 80 : c * 80 + 32, :]
            second = ref[c * 80 + 32 : c * 80 + 64, :]
            at = (0 if ref is u_s else 96) + c * 32
            f_s[at : at + 32, :] = jnp.where(half, first, second)

    def scatter_step(t, kept):
        here = place_row == t
        new = []
        for k in range(6):
            row = f_s[pl.ds(k * 32 + t, 1), :]
            got = jnp.take_along_axis(
                jnp.broadcast_to(row, (32, 128)), place_lane, axis=1, mode="promise_in_bounds"
            )
            new.append(jnp.where(here, got, kept[k]))
        return tuple(new)

    done = lax.fori_loop(
        0, 32, scatter_step, tuple(jnp.zeros((32, 128), f32) for _ in range(6)), unroll=4
    )
    for k in range(6):
        ref = out_u_ref if k < 3 else out_v_ref
        for t in range(32):
            ref[k % 3 : k % 3 + 1, t * 128 : t * 128 + 128] = done[k][t : t + 1]


def per_device(
    displacement, velocity, inverse_mass, levels, first_lame, shear_modulus, connectivity, owner_list
):
    operator = jnp.asarray(element_operator())
    nodes = displacement.shape[1]
    vmem = pl.BlockSpec(memory_space=pltpu.VMEM)
    shape = jax.ShapeDtypeStruct((3, nodes), f32)
    V, S = pltpu.VMEM, pltpu.SemaphoreType.DMA
    return pl.pallas_call(
        kernel,
        out_shape=(shape, shape),
        in_specs=[vmem] * 9,
        out_specs=(vmem, vmem),
        scratch_shapes=[
            V((125, 128), jnp.int32), V((128, 128), f32), V((32, 128), jnp.int32),
            V((64, 4096), bf16), V((128, 4096), bf16),
            V((256, 128), f32), V((256, 128), f32), V((80, 128), f32), V((256, 128), f32),
            V((2 * TOTAL, 128), bf16), V((8, 128), f32),
            V((120, 128), f32), V((120, 128), f32), V((8, 128), f32), V((8, 128), f32),
            V((substeps, 2, 48, 128), f32), V((substeps, 2, 48, 128), f32),
            S((2,)), S((2,)), S((substeps, 2)), S((substeps, 2)),
        ],
        compiler_params=pltpu.CompilerParams(
            collective_id=0, has_side_effects=True, vmem_limit_bytes=32 * 1024 * 1024
        ),
    )(
        displacement, velocity, inverse_mass.reshape(32, 128),
        levels.reshape(1, 64), first_lame.reshape(1, 64), shear_modulus.reshape(1, 64),
        connectivity, owner_list.reshape(4, 128), operator,
    )


def solution(mesh):
    in_specs = (
        P(None, ("dom", "lvl")),
        P(None, ("dom", "lvl")),
        P(("dom", "lvl")),
        P(("dom", "lvl")),
        P(("dom", "lvl")),
        P(("dom", "lvl")),
        P(None, ("dom", "lvl")),
        P(("dom", "lvl")),
    )
    out_specs = (P(None, ("dom", "lvl")), P(None, ("dom", "lvl")))
    return jax.shard_map(
        per_device, mesh=mesh, in_specs=in_specs, out_specs=out_specs, check_vma=False
    )
```

```python
import functools

import jax
import jax.numpy as jnp
import numpy as np
from jax import lax
from jax.experimental import pallas as pl
from jax.experimental.pallas import tpu as pltpu
from jax.sharding import PartitionSpec as P

substep_length = 0.01
substeps = 8
MESH = pl.DeviceIdType.MESH
f32 = jnp.float32
bf16 = jnp.bfloat16

BLOCK = (
    [(0, 0), (0, 1), (0, 2), (0, 3), (1, 0), (2, 0), (3, 0)]
    + [(b, c) for b in (1, 2, 3) for c in (1, 2, 3)]
)
CENTRE = BLOCK.index((2, 2))
HIGH = [(4, 0), (4, 1), (4, 2), (4, 3), (1, 4), (2, 4), (3, 4), (0, 4)]
PLANES = [(c, a) for c in range(3) for a in range(5)]
MAIN, FACE, TOTAL = 240, 120, 384


def lobatto_tables():
    points = np.array([-1.0, -np.sqrt(3.0 / 7.0), 0.0, np.sqrt(3.0 / 7.0), 1.0])
    weights = np.array([0.1, 49.0 / 90.0, 32.0 / 45.0, 49.0 / 90.0, 0.1])
    factor = np.array(
        [np.prod([points[i] - points[k] for k in range(5) if k != i]) for i in range(5)]
    )
    matrix = np.zeros((5, 5))
    for i in range(5):
        for j in range(5):
            if i == j:
                matrix[i, j] = sum((1.0 / (points[i] - points[k]) for k in range(5) if k != i))
            else:
                matrix[i, j] = factor[i] / (factor[j] * (points[i] - points[j]))
    cube = weights[:, None, None] * weights[None, :, None] * weights[None, None, :]
    return matrix, cube


def element_operator():
    derivative, cube = lobatto_tables()
    one = np.eye(5)
    along = [
        np.kron(np.kron(derivative, one), one),
        np.kron(np.kron(one, derivative), one),
        np.kron(np.kron(one, one), derivative),
    ]
    weight = cube.reshape(125)
    lame = np.zeros((3, 125, 3, 125))
    shear = np.zeros((3, 125, 3, 125))
    for c in range(3):
        for a in range(3):
            lame[c, :, a, :] += along[c].T @ (weight[:, None] * along[a])
            shear[c, :, c, :] += along[a].T @ (weight[:, None] * along[a])
            shear[c, :, a, :] += along[a].T @ (weight[:, None] * along[c])
    rows = []
    for c, a in PLANES:
        rows += [c * 125 + a * 25 + b * 5 + k for b, k in BLOCK]
    for c, a in PLANES:
        rows += [c * 125 + a * 25 + b * 5 + k for b, k in HIGH]
    for c, a in PLANES:
        rows.append(c * 125 + a * 25 + 24)
    rows = np.array(rows)
    full = np.zeros((TOTAL, 2 * TOTAL))
    full[: len(rows), : len(rows)] = lame.reshape(375, 375)[np.ix_(rows, rows)]
    full[: len(rows), TOTAL : TOTAL + len(rows)] = shear.reshape(375, 375)[np.ix_(rows, rows)]
    high = full.astype(jnp.bfloat16)
    low = (full - high.astype(np.float64)).astype(jnp.bfloat16)
    return np.concatenate([high, low], axis=0)


def node_row(a, b, c):
    return a * 25 + b * 5 + c


NAMES = [
    node_row(2, 0, 2), node_row(2, 4, 2),
    node_row(2, 2, 0), node_row(2, 2, 4),
    node_row(2, 0, 0), node_row(2, 4, 4),
    node_row(0, 2, 2), node_row(4, 2, 2),
]


def lanes(shape):
    return lax.broadcasted_iota(jnp.int32, shape, len(shape) - 1)


def sublanes(shape):
    return lax.broadcasted_iota(jnp.int32, shape, len(shape) - 2)


def split_two(x):
    high = x.astype(bf16).astype(f32)
    return jnp.where(lanes(x.shape) < 64, high, x - high).astype(bf16)


def split_three(x):
    high = x.astype(bf16).astype(f32)
    rest = x - high
    middle = rest.astype(bf16).astype(f32)
    first = jnp.where(lanes(x.shape) < 64, high, middle).astype(bf16)
    second = jnp.where(lanes(x.shape) < 64, rest - middle, 0.0).astype(bf16)
    return jnp.concatenate([first, second], axis=1)


def moved(parts, matrix):
    return jnp.dot(parts, matrix, preferred_element_type=f32)


def same(column, row):
    return jnp.where(column == row, 1.0, 0.0).astype(bf16)


FOLDED = [5, 1, 3, 2, 0, 4, 6, 7, 11, 10, 8, 12, 14, 15, 13, 9]
STATE, NAMED, ROWS = 224, 232, 240


def looked_up(index, table):
    found = jnp.int32(table[0])
    for k, value in enumerate(table[1:], 1):
        found = jnp.where(index == k, jnp.int32(value), found)
    return found


def kernel(
    folded, disp_hbm, vel_hbm, mass_hbm, level_hbm, lame_hbm, shear_hbm, conn_hbm, owner_hbm, oper_hbm,
    out_u_ref, out_v_ref,
    disp_ref, vel_ref, mass_ref, level_ref, lame_ref, shear_ref, conn_ref, owner_ref, oper_ref, load_sem,
    conn_s, tile_s, pick_s, hot_hi, hot_lo, u_s, v_s, m_s, f_s, x_s, elem_s,
    pack_out, pack_in, back_out, back_in,
    low_out, low_in, name_out, name_in, send_buf, recv_buf,
    init_send, init_recv, step_send, step_recv, bulk_send, bulk_recv,
):
    dom_size, lvl_size = lax.axis_size("dom"), lax.axis_size("lvl")
    count = dom_size * lvl_size
    me = lax.axis_index("dom") * lvl_size + lax.axis_index("lvl")

    loads = [
        pltpu.make_async_copy(src, dst, load_sem.at[k])
        for k, (src, dst) in enumerate([
            (conn_hbm, conn_ref), (disp_hbm, disp_ref), (vel_hbm, vel_ref), (mass_hbm, mass_ref),
            (owner_hbm, owner_ref), (level_hbm, level_ref), (lame_hbm, lame_ref),
            (shear_hbm, shear_ref), (oper_hbm, oper_ref),
        ])
    ]
    for load in loads:
        load.start()

    def device(index):
        return (index // lvl_size, lax.rem(index, lvl_size))

    if folded:
        chips = count // 2
        chip, core = me // 2, lax.rem(me, 2)
        order = [FOLDED.index(k) for k in range(chips)]
        host = looked_up(chip, FOLDED) * 2 + core
        home = looked_up(chip, order) * 2 + core
        after_chip = looked_up(chip, [FOLDED[(k + 1) % chips] for k in order])
        before_chip = looked_up(chip, [FOLDED[k - 1] for k in order])
        after = jnp.where(core == 1, after_chip * 2, me + 1)
        before = jnp.where(core == 1, me - 1, before_chip * 2 + 1)
        host_id, home_id = device(host), device(home)
        away = host != me
    else:
        after = lax.rem(me + 1, count)
        before = lax.rem(me + count - 1, count)
    after_id, before_id = device(after), device(before)

    barrier = pltpu.get_barrier_semaphore()
    for other in (after_id, before_id):
        pl.semaphore_signal(barrier, inc=1, device_id=other, device_id_type=MESH)
    if folded:

        @pl.when(away)
        def _():
            for other in (host_id, home_id):
                pl.semaphore_signal(barrier, inc=1, device_id=other, device_id_type=MESH)

    def bulk(src, dst, k, other):
        return pltpu.make_async_remote_copy(
            src_ref=src, dst_ref=dst, send_sem=bulk_send.at[k], recv_sem=bulk_recv.at[k],
            device_id=other, device_id_type=MESH,
        )

    loads[0].wait()
    tile_s[...] = jnp.zeros((128, 128), f32)
    for k in range(2):
        tile_s[k * 64 : k * 64 + 64, 0:125] = conn_ref[...].astype(f32)
    conn_s[...] = jnp.transpose(tile_s[...])

    low_half = lanes((1, 128)) < 64
    for a in range(2):
        for j, (b, c) in enumerate(BLOCK):
            r0, r1 = node_row(a, b, c), node_row(a + 2, b, c)
            pick_s[a * 16 + j : a * 16 + j + 1, :] = jnp.where(
                low_half, conn_s[r0 : r0 + 1, :], conn_s[r1 : r1 + 1, :]
            ).astype(jnp.int32)
    pick = pick_s[...]
    pick_hi, pick_lo = lax.shift_right_logical(pick, 7), lax.bitwise_and(pick, 127)

    for load in loads[1:8]:
        load.wait()

    def gather_step(t, kept):
        here = pick_hi == t
        cols = pl.ds(pl.multiple_of(t * 128, 128), 128)
        rows = [disp_ref[c : c + 1, cols] for c in range(3)]
        rows += [vel_ref[c : c + 1, cols] for c in range(3)]
        rows.append(mass_ref[pl.ds(t, 1), :])
        new = []
        for row, old in zip(rows, kept):
            got = jnp.take_along_axis(
                jnp.broadcast_to(row, (32, 128)), pick_lo, axis=1, mode="promise_in_bounds"
            )
            new.append(jnp.where(here, got, old))
        return tuple(new)

    got = lax.fori_loop(
        0, 32, gather_step, tuple(jnp.zeros((32, 128), f32) for _ in range(7)), unroll=4
    )
    half = lanes((32, 128)) < 64
    for k in range(7):
        pack_out[k * 32 : k * 32 + 32, :] = got[k]

    for k, r in enumerate(NAMES):
        pack_out[STATE + k : STATE + k + 1, :] = conn_s[r : r + 1, :]
    tile_s[0:8, :] = jnp.zeros((8, 128), f32)
    tile_s[0:4, :] = owner_ref[...].astype(f32)
    columns = jnp.transpose(tile_s[...])
    low_name = conn_s[NAMES[6] : NAMES[6] + 1, :]
    slot_low = jnp.full((1, 128), -9999.0, f32)
    for k in range(4):
        hit = columns[:, k : k + 1] == low_name
        number = sublanes((128, 128)).astype(f32) + (k * 128 + 9999)
        slot_low = slot_low + jnp.sum(jnp.where(hit, number, 0.0), axis=0, keepdims=True)
    pack_out[NAMED : NAMED + 8, :] = jnp.zeros((8, 128), f32)
    pack_out[NAMED : NAMED + 1, :] = slot_low
    for k, ref in enumerate((level_ref, lame_ref, shear_ref), 1):
        for at in (0, 64):
            pack_out[NAMED + k : NAMED + k + 1, at : at + 64] = ref[...].astype(f32)

    if folded:

        @pl.when(away)
        def _():
            pl.semaphore_wait(barrier, 4)
            bulk(pack_out, pack_in, 0, host_id).start()

        @pl.when(jnp.logical_not(away))
        def _():
            pl.semaphore_wait(barrier, 2)
    else:
        pl.semaphore_wait(barrier, 2)

    def find_places():
        for r in range(32):
            cols = slice(r * 128, r * 128 + 128)
            hit = pick_hi[r : r + 1, :] == sublanes((32, 128))
            hot_hi[0:32, cols] = jnp.where(hit, lanes((32, 128)).astype(f32), 0.0).astype(bf16)
            hot_hi[32:64, cols] = jnp.where(hit, float(r), 0.0).astype(bf16)
            hot_lo[:, cols] = same(sublanes((128, 128)), pick_lo[r : r + 1, :])
        place = lax.dot_general(
            hot_hi[...], hot_lo[...], (((1,), (1,)), ((), ())), preferred_element_type=f32
        )
        return place[0:32].astype(jnp.int32), place[32:64].astype(jnp.int32)

    if folded:
        place_lane, place_row = find_places()

        @pl.when(away)
        def _():
            bulk(pack_out, pack_in, 0, host_id).wait()

        @pl.when(jnp.logical_not(away))
        def _():
            pack_in[...] = pack_out[...]

    held = pack_in if folded else pack_out
    for k, ref in enumerate([u_s] * 3 + [v_s] * 3 + [m_s]):
        packed = held[k * 32 : k * 32 + 32, :]
        turned = pltpu.roll(packed, 64, axis=1)
        base = (k % 3) * 80 if k < 6 else 0
        ref[base : base + 32, :] = jnp.where(half, packed, turned)
        ref[base + 32 : base + 64, :] = jnp.where(half, turned, packed)
    u_s[MAIN : MAIN + 16, :] = jnp.zeros((16, 128), f32)
    f_s[MAIN : MAIN + 16, :] = jnp.zeros((16, 128), f32)
    elem_s[...] = held[NAMED : NAMED + 8, :]
    slot_low = elem_s[0:1, :]
    name_row = [held[STATE + k : STATE + k + 1, :] for k in range(8)]
    owned = float(disp_ref.shape[1])
    slot_high = name_row[7] - owned

    for k in range(3):
        low_out[k * 16 : k * 16 + 16, :] = u_s[k * 80 : k * 80 + 16, :]
        low_out[48 + k * 16 : 64 + k * 16, :] = v_s[k * 80 : k * 80 + 16, :]
    low_out[96:112, :] = m_s[0:16, :]
    low_out[112:120, :] = jnp.broadcast_to(slot_low, (8, 128))
    name_out[...] = jnp.broadcast_to(slot_high, (8, 128))
    low_copy = pltpu.make_async_remote_copy(
        src_ref=low_out, dst_ref=low_in, send_sem=init_send.at[0], recv_sem=init_recv.at[0],
        device_id=before_id, device_id_type=MESH,
    )
    name_copy = pltpu.make_async_remote_copy(
        src_ref=name_out, dst_ref=name_in, send_sem=init_send.at[1], recv_sem=init_recv.at[1],
        device_id=after_id, device_id_type=MESH,
    )
    low_copy.start()
    name_copy.start()

    tile_s[0:8, :] = held[STATE : STATE + 8, :]
    columns = jnp.transpose(tile_s[...])
    name_col = [columns[:, k : k + 1] for k in range(8)]
    spread = jnp.concatenate(
        [same(name_col[0], name_row[1]), same(name_col[2], name_row[3])], axis=1
    )
    spread = jnp.concatenate([spread, spread], axis=0)
    spread_edge = same(name_col[4], name_row[5])
    spread_edge = jnp.concatenate([spread_edge, spread_edge], axis=0)
    collect = jnp.concatenate(
        [same(name_col[1], name_row[0]), same(name_col[3], name_row[2])], axis=1
    )
    collect_edge = same(name_col[5], name_row[4])
    to_high = same(name_col[6], name_row[7])
    to_low = same(name_col[7], name_row[6])
    if not folded:
        place_lane, place_row = find_places()

    low_copy.wait()
    name_copy.wait()
    tile_s[0:8, :] = low_in[112:120, :]
    tile_s[8:16, :] = name_in[...]
    columns = jnp.transpose(tile_s[...])
    from_after = same(columns[:, 0:1], slot_high)
    from_before = same(columns[:, 8:9], slot_low)
    to_high_twice = jnp.concatenate([to_high, to_high], axis=0)
    from_after_twice = jnp.concatenate([from_after, from_after], axis=0)
    high = moved(split_three(low_out[0:112, :]), to_high_twice)
    high = high + moved(split_three(low_in[0:112, :]), from_after_twice)
    for k in range(3):
        u_s[k * 80 + 64 : k * 80 + 80, :] = high[k * 16 : k * 16 + 16]
        v_s[k * 80 + 64 : k * 80 + 80, :] = high[48 + k * 16 : 64 + k * 16]
    m_s[64:80, :] = high[96:112]
    loads[8].wait()

    level = elem_s[1:2, :]
    period = jnp.where(level == 0.0, 8, jnp.where(level == 1.0, 4, jnp.where(level == 2.0, 2, 1)))
    row8 = sublanes((15, 8, 128))

    def advance(rows, force):
        c_rows = pl.ds(rows[0] * 80 + rows[1] * 16, 16)
        mass = m_s[pl.ds(rows[1] * 16, 16), :]
        speed = v_s[c_rows, :] - substep_length * mass * force
        v_s[c_rows, :] = speed
        u_s[c_rows, :] = u_s[c_rows, :] + substep_length * speed

    def substep(s, carry):
        u = u_s[0:MAIN, :].reshape(15, 16, 128)
        faces = moved(split_three(u[:, 0:8].reshape(FACE, 128)), spread)
        along_y = faces[:, 0:128].reshape(15, 8, 128)
        along_z = faces[:, 128:256].reshape(15, 8, 128)
        face = jnp.where(
            row8 < 4, along_y, jnp.where(row8 < 7, along_z, pltpu.roll(along_z, 7, axis=1))
        )
        edge = moved(split_three(u_s[pl.ds(0, 16, stride=16), :]), spread_edge)
        centres = [
            u_s[c * 80 + 32 + CENTRE : c * 80 + 33 + CENTRE, :] for c in range(3)
        ]
        row16 = sublanes((16, 128))
        edge = edge - jnp.where(
            row16 < 5, centres[0], jnp.where(row16 < 10, centres[1], centres[2])
        )
        edge = jnp.where(row16 < 15, edge, 0.0)
        active = lax.rem(jnp.full((1, 128), s, jnp.int32), period) == 0
        weight = jnp.where(active, period.astype(f32), 0.0)
        for part, value in enumerate((elem_s[2:3, :] * weight, elem_s[3:4, :] * weight)):
            at = part * TOTAL
            for c in range(3):
                main = (u[c * 5 : c * 5 + 5].reshape(80, 128) - centres[c]) * value
                x_s[at + c * 80 : at + c * 80 + 80, :] = split_two(main)
            both = [
                (face[c * 5 : c * 5 + 5].reshape(40, 128) - centres[c]) * value for c in range(3)
            ]
            both += [edge * value, jnp.zeros((8, 128), f32)]
            x_s[at + MAIN : at + TOTAL, :] = split_two(jnp.concatenate(both, axis=0))
        product = jnp.dot(oper_ref[...], x_s[...], preferred_element_type=f32)
        force = product[0:TOTAL] + product[TOTAL : 2 * TOTAL]
        force = force + pltpu.roll(force, 64, axis=1)

        face = moved(split_two(force[MAIN : MAIN + FACE]), collect)
        along_y = face[:, 0:128].reshape(15, 8, 128)
        along_z = face[:, 128:256].reshape(15, 8, 128)
        low = jnp.where(row8 < 4, along_y, jnp.where(row8 < 7, along_z, 0.0))
        low = low + jnp.where(row8 == 0, pltpu.roll(along_z, 1, axis=1), 0.0)
        main = force[0:MAIN].reshape(15, 2, 8, 128)
        main = jnp.concatenate([main[:, 0:1] + low[:, None], main[:, 1:2]], axis=1)
        f_s[0:MAIN, :] = main.reshape(MAIN, 128)
        edge = moved(split_two(force[MAIN + FACE : MAIN + FACE + 16]), collect_edge)
        f_s[pl.ds(0, 16, stride=16), :] = f_s[pl.ds(0, 16, stride=16), :] + edge

        low_x = jnp.concatenate([f_s[c * 80 : c * 80 + 16, :] for c in range(3)], axis=0)
        high_x = jnp.concatenate([f_s[c * 80 + 64 : c * 80 + 80, :] for c in range(3)], axis=0)
        half24 = lanes((24, 128)) < 64
        send_buf[s, 0] = jnp.where(half24, low_x[0:24], low_x[24:48])
        send_buf[s, 1] = jnp.where(half24, high_x[0:24], high_x[24:48])
        copies = [
            pltpu.make_async_remote_copy(
                src_ref=send_buf.at[s, way], dst_ref=recv_buf.at[s, way],
                send_sem=step_send.at[s, way], recv_sem=step_recv.at[s, way],
                device_id=other, device_id_type=MESH,
            )
            for way, other in enumerate((before_id, after_id))
        ]
        copies[1].start()
        copies[0].start()
        low_sum = low_x + moved(split_two(high_x), to_low)
        high_sum = high_x + moved(split_two(low_x), to_high)
        for c in range(3):
            for a in (1, 2, 3):
                advance((c, a), f_s[c * 80 + a * 16 : c * 80 + a * 16 + 16, :])
        copies[1].wait()
        copies[0].wait()

        def unpacked(packed):
            turned = pltpu.roll(packed, 64, axis=1)
            return jnp.concatenate(
                [jnp.where(half24, packed, turned), jnp.where(half24, turned, packed)], axis=0
            )

        low_sum = low_sum + moved(split_two(unpacked(recv_buf[s, 1])), from_before)
        high_sum = high_sum + moved(split_two(unpacked(recv_buf[s, 0])), from_after)
        for c in range(3):
            advance((c, 0), low_sum[c * 16 : c * 16 + 16])
            advance((c, 4), high_sum[c * 16 : c * 16 + 16])
        return carry

    lax.fori_loop(0, substeps, substep, 0)

    for ref in (u_s, v_s):
        for c in range(3):
            first = ref[c * 80 : c * 80 + 32, :]
            second = ref[c * 80 + 32 : c * 80 + 64, :]
            at = (0 if ref is u_s else 96) + c * 32
            back_out[at : at + 32, :] = jnp.where(half, first, second)
    if folded:

        @pl.when(away)
        def _():
            back = bulk(back_out, back_in, 1, home_id)
            back.start()
            back.wait()

        @pl.when(jnp.logical_not(away))
        def _():
            back_in[...] = back_out[...]

    final = back_in if folded else back_out

    def scatter_step(t, kept):
        here = place_row == t
        new = []
        for k in range(6):
            row = final[pl.ds(k * 32 + t, 1), :]
            got = jnp.take_along_axis(
                jnp.broadcast_to(row, (32, 128)), place_lane, axis=1, mode="promise_in_bounds"
            )
            new.append(jnp.where(here, got, kept[k]))
        return tuple(new)

    done = lax.fori_loop(
        0, 32, scatter_step, tuple(jnp.zeros((32, 128), f32) for _ in range(6)), unroll=4
    )
    for k in range(6):
        ref = out_u_ref if k < 3 else out_v_ref
        for t in range(32):
            ref[k % 3 : k % 3 + 1, t * 128 : t * 128 + 128] = done[k][t : t + 1]


def per_device(
    displacement, velocity, inverse_mass, levels, first_lame, shear_modulus, connectivity, owner_list
):
    operator = jnp.asarray(element_operator())
    nodes = displacement.shape[1]
    vmem = pl.BlockSpec(memory_space=pltpu.VMEM)
    hbm = pl.BlockSpec(memory_space=pltpu.HBM)
    shape = jax.ShapeDtypeStruct((3, nodes), f32)
    V, S = pltpu.VMEM, pltpu.SemaphoreType.DMA
    operands = (
        displacement, velocity, inverse_mass.reshape(32, 128),
        levels.reshape(1, 64), first_lame.reshape(1, 64), shear_modulus.reshape(1, 64),
        connectivity.T, owner_list.reshape(4, 128), operator,
    )
    folded = lax.axis_size("dom") == 8 and lax.axis_size("lvl") == 4
    return pl.pallas_call(
        functools.partial(kernel, folded),
        out_shape=(shape, shape),
        in_specs=[hbm] * 9,
        out_specs=(vmem, vmem),
        scratch_shapes=[V(x.shape, x.dtype) for x in operands] + [S((9,))] + [
            V((128, 128), f32), V((128, 128), f32), V((32, 128), jnp.int32),
            V((64, 4096), bf16), V((128, 4096), bf16),
            V((256, 128), f32), V((256, 128), f32), V((80, 128), f32), V((256, 128), f32),
            V((2 * TOTAL, 128), bf16), V((8, 128), f32),
            V((ROWS, 128), f32), V((ROWS, 128), f32), V((192, 128), f32), V((192, 128), f32),
            V((120, 128), f32), V((120, 128), f32), V((8, 128), f32), V((8, 128), f32),
            V((substeps, 2, 24, 128), f32), V((substeps, 2, 24, 128), f32),
            S((2,)), S((2,)), S((substeps, 2)), S((substeps, 2)), S((2,)), S((2,)),
        ],
        compiler_params=pltpu.CompilerParams(
            collective_id=0, has_side_effects=True, vmem_limit_bytes=63 * 1024 * 1024
        ),
    )(*operands)


def solution(mesh):
    in_specs = (
        P(None, ("dom", "lvl")),
        P(None, ("dom", "lvl")),
        P(("dom", "lvl")),
        P(("dom", "lvl")),
        P(("dom", "lvl")),
        P(("dom", "lvl")),
        P(None, ("dom", "lvl")),
        P(("dom", "lvl")),
    )
    out_specs = (P(None, ("dom", "lvl")), P(None, ("dom", "lvl")))
    return jax.shard_map(
        per_device, mesh=mesh, in_specs=in_specs, out_specs=out_specs, check_vma=False
    )
```

```python
import functools

import jax
import jax.numpy as jnp
import numpy as np
from jax import lax
from jax.experimental import pallas as pl
from jax.experimental.pallas import tpu as pltpu
from jax.sharding import PartitionSpec as P

substep_length = 0.01
substeps = 8
MESH = pl.DeviceIdType.MESH
f32 = jnp.float32
bf16 = jnp.bfloat16

BLOCK = (
    [(0, 0), (0, 1), (0, 2), (0, 3), (1, 0), (2, 0), (3, 0)]
    + [(b, c) for b in (1, 2, 3) for c in (1, 2, 3)]
)
CENTRE = BLOCK.index((2, 2))
HIGH = [(4, 0), (4, 1), (4, 2), (4, 3), (1, 4), (2, 4), (3, 4), (0, 4)]
PLANES = [(c, a) for a in (0, 4) for c in range(3)] + [(c, a) for c in range(3) for a in (1, 2, 3)]
MAIN, FACE, TOTAL = 240, 120, 384
SHARED, OUTER, INNER = 6, 160, 240


def lobatto_tables():
    points = np.array([-1.0, -np.sqrt(3.0 / 7.0), 0.0, np.sqrt(3.0 / 7.0), 1.0])
    weights = np.array([0.1, 49.0 / 90.0, 32.0 / 45.0, 49.0 / 90.0, 0.1])
    factor = np.array(
        [np.prod([points[i] - points[k] for k in range(5) if k != i]) for i in range(5)]
    )
    matrix = np.zeros((5, 5))
    for i in range(5):
        for j in range(5):
            if i == j:
                matrix[i, j] = sum((1.0 / (points[i] - points[k]) for k in range(5) if k != i))
            else:
                matrix[i, j] = factor[i] / (factor[j] * (points[i] - points[j]))
    cube = weights[:, None, None] * weights[None, :, None] * weights[None, None, :]
    return matrix, cube


def element_operator():
    derivative, cube = lobatto_tables()
    one = np.eye(5)
    along = [
        np.kron(np.kron(derivative, one), one),
        np.kron(np.kron(one, derivative), one),
        np.kron(np.kron(one, one), derivative),
    ]
    weight = cube.reshape(125)
    lame = np.zeros((3, 125, 3, 125))
    shear = np.zeros((3, 125, 3, 125))
    for c in range(3):
        for a in range(3):
            lame[c, :, a, :] += along[c].T @ (weight[:, None] * along[a])
            shear[c, :, c, :] += along[a].T @ (weight[:, None] * along[a])
            shear[c, :, a, :] += along[a].T @ (weight[:, None] * along[c])

    def ordered(planes):
        rows = [c * 125 + a * 25 + b * 5 + k for c, a in planes for b, k in BLOCK]
        rows += [c * 125 + a * 25 + b * 5 + k for c, a in planes for b, k in HIGH]
        return np.array(rows + [c * 125 + a * 25 + 24 for c, a in planes])

    taken = ordered(PLANES)
    parts = []
    for planes, size in ((PLANES[:SHARED], OUTER), (PLANES[SHARED:], INNER)):
        given = ordered(planes)
        part = np.zeros((size, 2 * TOTAL))
        part[: len(given), : len(taken)] = lame.reshape(375, 375)[np.ix_(given, taken)]
        part[: len(given), TOTAL : TOTAL + len(taken)] = shear.reshape(375, 375)[np.ix_(given, taken)]
        high = part.astype(jnp.bfloat16)
        parts += [high, (part - high.astype(np.float64)).astype(jnp.bfloat16)]
    return np.concatenate(parts, axis=0)


def block_at(c, a):
    return PLANES.index((c, a)) * 16


def node_row(a, b, c):
    return a * 25 + b * 5 + c


NAMES = [
    node_row(2, 0, 2), node_row(2, 4, 2),
    node_row(2, 2, 0), node_row(2, 2, 4),
    node_row(2, 0, 0), node_row(2, 4, 4),
    node_row(0, 2, 2), node_row(4, 2, 2),
]


def lanes(shape):
    return lax.broadcasted_iota(jnp.int32, shape, len(shape) - 1)


def sublanes(shape):
    return lax.broadcasted_iota(jnp.int32, shape, len(shape) - 2)


def split_two(x):
    high = x.astype(bf16).astype(f32)
    return jnp.where(lanes(x.shape) < 64, high, x - high).astype(bf16)


def split_three(x):
    high = x.astype(bf16).astype(f32)
    rest = x - high
    middle = rest.astype(bf16).astype(f32)
    first = jnp.where(lanes(x.shape) < 64, high, middle).astype(bf16)
    second = jnp.where(lanes(x.shape) < 64, rest - middle, 0.0).astype(bf16)
    return jnp.concatenate([first, second], axis=1)


def moved(parts, matrix):
    return jnp.dot(parts, matrix, preferred_element_type=f32)


def same(column, row):
    return jnp.where(column == row, 1.0, 0.0).astype(bf16)


FOLDED = [5, 1, 3, 2, 0, 4, 6, 7, 11, 10, 14, 15, 13, 12, 8, 9]
STATE, NAMED, ROWS = 224, 232, 240


def looked_up(index, table):
    found = jnp.int32(table[0])
    for k, value in enumerate(table[1:], 1):
        found = jnp.where(index == k, jnp.int32(value), found)
    return found


def kernel(
    folded, disp_hbm, vel_hbm, mass_hbm, level_hbm, lame_hbm, shear_hbm, conn_hbm, owner_hbm, oper_hbm,
    final_ref, place_ref,
    disp_ref, vel_ref, mass_ref, level_ref, lame_ref, shear_ref, conn_ref, owner_ref, oper_ref, load_sem,
    conn_s, tile_s, pick_s, hot_hi, hot_lo, u_s, v_s, m_s, f_s, x_s, elem_s,
    pack_out, pack_in, back_out, back_in,
    low_out, low_in, name_out, name_in, send_buf, recv_buf,
    init_send, init_recv, step_send, step_recv, bulk_send, bulk_recv,
):
    dom_size, lvl_size = lax.axis_size("dom"), lax.axis_size("lvl")
    count = dom_size * lvl_size
    me = lax.axis_index("dom") * lvl_size + lax.axis_index("lvl")

    loads = [
        pltpu.make_async_copy(src, dst, load_sem.at[k])
        for k, (src, dst) in enumerate([
            (conn_hbm, conn_ref), (disp_hbm, disp_ref), (vel_hbm, vel_ref), (mass_hbm, mass_ref),
            (owner_hbm, owner_ref), (level_hbm, level_ref), (lame_hbm, lame_ref),
            (shear_hbm, shear_ref), (oper_hbm, oper_ref),
        ])
    ]
    for load in loads:
        load.start()

    def device(index):
        return (index // lvl_size, lax.rem(index, lvl_size))

    def step(index, distance):
        return lax.rem(index + count + distance, count)

    if folded:
        order = [FOLDED.index(k) for k in range(count // 2)]

        def host_of(index):
            return looked_up(index // 2, FOLDED) * 2 + lax.rem(index, 2)

        home = looked_up(me // 2, order) * 2 + lax.rem(me, 2)
        host = host_of(me)
        away = host != me
        after, before = host_of(step(home, 1)), host_of(step(home, -1))
        low_to, name_to = host_of(step(me, -1)), host_of(step(me, 1))
        peers = [after, before, low_to, name_to, step(home, 1), step(home, -1)]
        host_id, home_id = device(host), device(home)
    else:
        after, before = step(me, 1), step(me, -1)
        low_to, name_to = before, after
        peers = [after, before]
    after_id, before_id = device(after), device(before)

    barrier = pltpu.get_barrier_semaphore()
    for other in peers:
        pl.semaphore_signal(barrier, inc=1, device_id=device(other), device_id_type=MESH)
    if folded:

        @pl.when(away)
        def _():
            for other in (host_id, home_id):
                pl.semaphore_signal(barrier, inc=1, device_id=other, device_id_type=MESH)

    def bulk(src, dst, k, other):
        return pltpu.make_async_remote_copy(
            src_ref=src, dst_ref=dst, send_sem=bulk_send.at[k], recv_sem=bulk_recv.at[k],
            device_id=other, device_id_type=MESH,
        )

    loads[0].wait()
    tile_s[...] = jnp.zeros((128, 128), f32)
    for k in range(2):
        tile_s[k * 64 : k * 64 + 64, 0:125] = conn_ref[...].astype(f32)
    conn_s[...] = jnp.transpose(tile_s[...])

    low_half = lanes((1, 128)) < 64
    for a in range(2):
        for j, (b, c) in enumerate(BLOCK):
            r0, r1 = node_row(a, b, c), node_row(a + 2, b, c)
            pick_s[a * 16 + j : a * 16 + j + 1, :] = jnp.where(
                low_half, conn_s[r0 : r0 + 1, :], conn_s[r1 : r1 + 1, :]
            ).astype(jnp.int32)
    pick = pick_s[...]
    pick_hi, pick_lo = lax.shift_right_logical(pick, 7), lax.bitwise_and(pick, 127)

    for load in loads[1:8]:
        load.wait()

    def gather_step(t, kept):
        here = pick_hi == t
        cols = pl.ds(pl.multiple_of(t * 128, 128), 128)
        rows = [disp_ref[c : c + 1, cols] for c in range(3)]
        rows += [vel_ref[c : c + 1, cols] for c in range(3)]
        rows.append(mass_ref[pl.ds(t, 1), :])
        new = []
        for row, old in zip(rows, kept):
            got = jnp.take_along_axis(
                jnp.broadcast_to(row, (32, 128)), pick_lo, axis=1, mode="promise_in_bounds"
            )
            new.append(jnp.where(here, got, old))
        return tuple(new)

    got = lax.fori_loop(
        0, 32, gather_step, tuple(jnp.zeros((32, 128), f32) for _ in range(7)), unroll=4
    )
    half = lanes((32, 128)) < 64
    for k in range(7):
        pack_out[k * 32 : k * 32 + 32, :] = got[k]

    for k, r in enumerate(NAMES):
        pack_out[STATE + k : STATE + k + 1, :] = conn_s[r : r + 1, :]
    tile_s[0:8, :] = jnp.zeros((8, 128), f32)
    tile_s[0:4, :] = owner_ref[...].astype(f32)
    columns = jnp.transpose(tile_s[...])
    low_name = conn_s[NAMES[6] : NAMES[6] + 1, :]
    slot_low = jnp.full((1, 128), -9999.0, f32)
    for k in range(4):
        hit = columns[:, k : k + 1] == low_name
        number = sublanes((128, 128)).astype(f32) + (k * 128 + 9999)
        slot_low = slot_low + jnp.sum(jnp.where(hit, number, 0.0), axis=0, keepdims=True)
    pack_out[NAMED : NAMED + 8, :] = jnp.zeros((8, 128), f32)
    pack_out[NAMED : NAMED + 1, :] = slot_low
    for k, ref in enumerate((level_ref, lame_ref, shear_ref), 1):
        for at in (0, 64):
            pack_out[NAMED + k : NAMED + k + 1, at : at + 64] = ref[...].astype(f32)

    half16 = lanes((16, 128)) < 64
    for k in range(4):
        other = got[min(2 * k + 1, 6)][0:16]
        low_out[k * 16 : k * 16 + 16, :] = jnp.where(
            half16, got[2 * k][0:16], pltpu.roll(other, 64, axis=1)
        )
    low_out[64:72, :] = jnp.broadcast_to(slot_low, (8, 128))
    owned = float(disp_ref.shape[1])
    name_out[...] = jnp.broadcast_to(conn_s[NAMES[7] : NAMES[7] + 1, :] - owned, (8, 128))
    low_copy = pltpu.make_async_remote_copy(
        src_ref=low_out, dst_ref=low_in, send_sem=init_send.at[0], recv_sem=init_recv.at[0],
        device_id=device(low_to), device_id_type=MESH,
    )
    name_copy = pltpu.make_async_remote_copy(
        src_ref=name_out, dst_ref=name_in, send_sem=init_send.at[1], recv_sem=init_recv.at[1],
        device_id=device(name_to), device_id_type=MESH,
    )
    if folded:

        @pl.when(away)
        def _():
            pl.semaphore_wait(barrier, 8)
            bulk(pack_out, pack_in, 0, host_id).start()

        @pl.when(jnp.logical_not(away))
        def _():
            pl.semaphore_wait(barrier, 6)
    else:
        pl.semaphore_wait(barrier, 2)
    low_copy.start()
    name_copy.start()

    def find_places():
        for r in range(32):
            cols = slice(r * 128, r * 128 + 128)
            hit = pick_hi[r : r + 1, :] == sublanes((32, 128))
            hot_hi[0:32, cols] = jnp.where(hit, lanes((32, 128)).astype(f32), 0.0).astype(bf16)
            hot_hi[32:64, cols] = jnp.where(hit, float(r), 0.0).astype(bf16)
            hot_lo[:, cols] = same(sublanes((128, 128)), pick_lo[r : r + 1, :])
        place = lax.dot_general(
            hot_hi[...], hot_lo[...], (((1,), (1,)), ((), ())), preferred_element_type=f32
        )
        return place[0:32].astype(jnp.int32), place[32:64].astype(jnp.int32)

    place_lane, place_row = find_places()
    place_ref[0:32, :] = place_lane
    place_ref[32:64, :] = place_row
    if folded:

        @pl.when(away)
        def _():
            bulk(pack_out, pack_in, 0, host_id).wait()

        @pl.when(jnp.logical_not(away))
        def _():
            pack_in[...] = pack_out[...]

    held = pack_in if folded else pack_out
    for k, ref in enumerate([u_s] * 3 + [v_s] * 3 + [m_s]):
        packed = held[k * 32 : k * 32 + 32, :]
        turned = pltpu.roll(packed, 64, axis=1)
        low, high = jnp.where(half, packed, turned), jnp.where(half, turned, packed)
        for a in range(4):
            at = block_at(k % 3, a) if k < 6 else a * 16
            ref[at : at + 16, :] = (low if a < 2 else high)[a % 2 * 16 : a % 2 * 16 + 16]
    u_s[MAIN : MAIN + 16, :] = jnp.zeros((16, 128), f32)
    f_s[MAIN : MAIN + 16, :] = jnp.zeros((16, 128), f32)
    elem_s[...] = held[NAMED : NAMED + 8, :]
    slot_low = elem_s[0:1, :]
    name_row = [held[STATE + k : STATE + k + 1, :] for k in range(8)]
    slot_high = name_row[7] - owned

    tile_s[0:8, :] = held[STATE : STATE + 8, :]
    columns = jnp.transpose(tile_s[...])
    name_col = [columns[:, k : k + 1] for k in range(8)]
    spread = jnp.concatenate(
        [same(name_col[0], name_row[1]), same(name_col[2], name_row[3])], axis=1
    )
    spread = jnp.concatenate([spread, spread], axis=0)
    spread_edge = same(name_col[4], name_row[5])
    spread_edge = jnp.concatenate([spread_edge, spread_edge], axis=0)
    collect = jnp.concatenate(
        [same(name_col[1], name_row[0]), same(name_col[3], name_row[2])], axis=1
    )
    collect_edge = same(name_col[5], name_row[4])
    to_high = same(name_col[6], name_row[7])
    to_low = same(name_col[7], name_row[6])

    low_copy.wait()
    name_copy.wait()
    tile_s[0:8, :] = low_in[64:72, :]
    tile_s[8:16, :] = name_in[...]
    columns = jnp.transpose(tile_s[...])
    from_after = same(columns[:, 0:1], slot_high)
    from_before = same(columns[:, 8:9], slot_low)
    to_high_twice = jnp.concatenate([to_high, to_high], axis=0)
    from_after_twice = jnp.concatenate([from_after, from_after], axis=0)
    theirs = []
    for k in range(7):
        packed = low_in[k // 2 * 16 : k // 2 * 16 + 16, :]
        turned = pltpu.roll(packed, 64, axis=1)
        theirs.append(jnp.where(half16 if k % 2 == 0 else jnp.logical_not(half16), packed, turned))
    ours = jnp.concatenate([u_s[0:48, :], v_s[0:48, :], m_s[0:16, :]], axis=0)
    high = moved(split_three(ours), to_high_twice)
    high = high + moved(split_three(jnp.concatenate(theirs, axis=0)), from_after_twice)
    u_s[48:96, :] = high[0:48]
    v_s[48:96, :] = high[48:96]
    m_s[64:80, :] = high[96:112]
    loads[8].wait()

    level = elem_s[1:2, :]
    period = jnp.where(level == 0.0, 8, jnp.where(level == 1.0, 4, jnp.where(level == 2.0, 2, 1)))
    row8 = sublanes((15, 8, 128))
    row16 = sublanes((16, 128))
    in_first = (row16 == 0) | (row16 == 3) | ((row16 >= 6) & (row16 < 9))
    in_second = (row16 == 1) | (row16 == 4) | ((row16 >= 9) & (row16 < 12))
    half24 = lanes((24, 128)) < 64

    def advance(first, size, mass, force):
        rows = pl.ds(first, size)
        speed = v_s[rows, :] - substep_length * mass * force
        v_s[rows, :] = speed
        u_s[rows, :] = u_s[rows, :] + substep_length * speed

    def mass_of(first, size):
        one = m_s[first : first + size, :]
        return jnp.concatenate([one, one, one], axis=0)

    def summed(product, size, planes, first):
        force = product[0:size] + product[size : 2 * size]
        force = force + pltpu.roll(force, 64, axis=1)
        main, faces = planes * 16, planes * 24
        moved_face = moved(split_two(force[main:faces]), collect)
        along_y = moved_face[:, 0:128].reshape(planes, 8, 128)
        along_z = moved_face[:, 128:256].reshape(planes, 8, 128)
        row = row8[0:planes]
        low = jnp.where(row < 4, along_y, jnp.where(row < 7, along_z, 0.0))
        low = low + jnp.where(row == 0, pltpu.roll(along_z, 1, axis=1), 0.0)
        both = force[0:main].reshape(planes, 2, 8, 128)
        both = jnp.concatenate([both[:, 0:1] + low[:, None], both[:, 1:2]], axis=1)
        f_s[first : first + main, :] = both.reshape(main, 128)
        edge = moved(split_two(force[faces:size]), collect_edge)[0:planes]
        at = pl.ds(first, planes, stride=16)
        f_s[at, :] = f_s[at, :] + edge

    def unpacked(packed):
        turned = pltpu.roll(packed, 64, axis=1)
        return jnp.concatenate(
            [jnp.where(half24, packed, turned), jnp.where(half24, turned, packed)], axis=0
        )

    def substep(s, carry):
        u = u_s[0:MAIN, :].reshape(15, 16, 128)
        faces = moved(split_three(u[:, 0:8].reshape(FACE, 128)), spread)
        along_y = faces[:, 0:128].reshape(15, 8, 128)
        along_z = faces[:, 128:256].reshape(15, 8, 128)
        face = jnp.where(
            row8 < 4, along_y, jnp.where(row8 < 7, along_z, pltpu.roll(along_z, 7, axis=1))
        )
        edge = moved(split_three(u_s[pl.ds(0, 16, stride=16), :]), spread_edge)
        centres = []
        for c in range(3):
            at = block_at(c, 2) + CENTRE
            centres.append(u_s[at : at + 1, :])
        edge = edge - jnp.where(in_first, centres[0], jnp.where(in_second, centres[1], centres[2]))
        edge = jnp.where(row16 < 15, edge, 0.0)
        active = lax.rem(jnp.full((1, 128), s, jnp.int32), period) == 0
        weight = jnp.where(active, period.astype(f32), 0.0)
        main = [u[k] - centres[c] for k, (c, _) in enumerate(PLANES)]
        face = [face[k] - centres[c] for k, (c, _) in enumerate(PLANES)]
        values = jnp.concatenate(main + face + [edge, jnp.zeros((8, 128), f32)], axis=0)
        x_s[0:TOTAL, :] = split_two(values * (elem_s[2:3, :] * weight))
        x_s[TOTAL : 2 * TOTAL, :] = split_two(values * (elem_s[3:4, :] * weight))

        x = x_s[...]
        product = jnp.dot(oper_ref[0 : 2 * OUTER, :], x, preferred_element_type=f32)
        summed(product, OUTER, SHARED, 0)
        low_x, high_x = f_s[0:48, :], f_s[48:96, :]
        send_buf[s, 0] = jnp.where(half24, low_x[0:24], low_x[24:48])
        send_buf[s, 1] = jnp.where(half24, high_x[0:24], high_x[24:48])
        copies = [
            pltpu.make_async_remote_copy(
                src_ref=send_buf.at[s, way], dst_ref=recv_buf.at[s, way],
                send_sem=step_send.at[s, way], recv_sem=step_recv.at[s, way],
                device_id=other, device_id_type=MESH,
            )
            for way, other in enumerate((before_id, after_id))
        ]
        copies[1].start()
        copies[0].start()
        product = jnp.dot(oper_ref[2 * OUTER :, :], x, preferred_element_type=f32)
        summed(product, INNER, 15 - SHARED, 96)
        low_sum = low_x + moved(split_two(high_x), to_low)
        high_sum = high_x + moved(split_two(low_x), to_high)
        advance(96, 144, mass_of(16, 48), f_s[96:240, :])
        copies[1].wait()
        copies[0].wait()
        low_sum = low_sum + moved(split_two(unpacked(recv_buf[s, 1])), from_before)
        high_sum = high_sum + moved(split_two(unpacked(recv_buf[s, 0])), from_after)
        advance(0, 48, mass_of(0, 16), low_sum)
        advance(48, 48, mass_of(64, 16), high_sum)
        return carry

    lax.fori_loop(0, substeps, substep, 0)

    for ref in (u_s, v_s):
        for c in range(3):
            at = (0 if ref is u_s else 96) + c * 32
            for a in range(2):
                one, two = block_at(c, a), block_at(c, a + 2)
                back_out[at + a * 16 : at + a * 16 + 16, :] = jnp.where(
                    half16, ref[one : one + 16, :], ref[two : two + 16, :]
                )
    if folded:

        @pl.when(away)
        def _():
            back = bulk(back_out, back_in, 1, home_id)
            back.start()
            back.wait()

        @pl.when(jnp.logical_not(away))
        def _():
            back_in[...] = back_out[...]

    final_ref[...] = (back_in if folded else back_out)[...]


def reorder(final_ref, place_ref, out_u_ref, out_v_ref):
    place_lane, place_row = place_ref[0:32, :], place_ref[32:64, :]

    def scatter_step(t, kept):
        here = place_row == t
        new = []
        for k in range(6):
            row = final_ref[pl.ds(k * 32 + t, 1), :]
            got = jnp.take_along_axis(
                jnp.broadcast_to(row, (32, 128)), place_lane, axis=1, mode="promise_in_bounds"
            )
            new.append(jnp.where(here, got, kept[k]))
        return tuple(new)

    done = lax.fori_loop(
        0, 32, scatter_step, tuple(jnp.zeros((32, 128), f32) for _ in range(6)), unroll=4
    )
    for k in range(6):
        ref = out_u_ref if k < 3 else out_v_ref
        for t in range(32):
            ref[k % 3 : k % 3 + 1, t * 128 : t * 128 + 128] = done[k][t : t + 1]


def per_device(
    displacement, velocity, inverse_mass, levels, first_lame, shear_modulus, connectivity, owner_list
):
    operator = jnp.asarray(element_operator())
    nodes = displacement.shape[1]
    vmem = pl.BlockSpec(memory_space=pltpu.VMEM)
    hbm = pl.BlockSpec(memory_space=pltpu.HBM)
    shape = jax.ShapeDtypeStruct((3, nodes), f32)
    V, S = pltpu.VMEM, pltpu.SemaphoreType.DMA
    operands = (
        displacement, velocity, inverse_mass.reshape(32, 128),
        levels.reshape(1, 64), first_lame.reshape(1, 64), shear_modulus.reshape(1, 64),
        connectivity.T, owner_list.reshape(4, 128), operator,
    )
    folded = lax.axis_size("dom") == 8 and lax.axis_size("lvl") == 4
    held = (jax.ShapeDtypeStruct((192, 128), f32), jax.ShapeDtypeStruct((64, 128), jnp.int32))
    final, place = pl.pallas_call(
        functools.partial(kernel, folded),
        out_shape=held,
        in_specs=[hbm] * 9,
        out_specs=(vmem, vmem),
        scratch_shapes=[V(x.shape, x.dtype) for x in operands] + [S((9,))] + [
            V((128, 128), f32), V((128, 128), f32), V((32, 128), jnp.int32),
            V((64, 4096), bf16), V((128, 4096), bf16),
            V((256, 128), f32), V((256, 128), f32), V((80, 128), f32), V((256, 128), f32),
            V((2 * TOTAL, 128), bf16), V((8, 128), f32),
            V((ROWS, 128), f32), V((ROWS, 128), f32), V((192, 128), f32), V((192, 128), f32),
            V((72, 128), f32), V((72, 128), f32), V((8, 128), f32), V((8, 128), f32),
            V((substeps, 2, 24, 128), f32), V((substeps, 2, 24, 128), f32),
            S((2,)), S((2,)), S((substeps, 2)), S((substeps, 2)), S((2,)), S((2,)),
        ],
        compiler_params=pltpu.CompilerParams(
            collective_id=0, has_side_effects=True, vmem_limit_bytes=63 * 1024 * 1024
        ),
    )(*operands)
    return pl.pallas_call(
        reorder,
        out_shape=(shape, shape),
        in_specs=[vmem] * 2,
        out_specs=(vmem, vmem),
        compiler_params=pltpu.CompilerParams(vmem_limit_bytes=63 * 1024 * 1024),
    )(final, place)


def solution(mesh):
    in_specs = (
        P(None, ("dom", "lvl")),
        P(None, ("dom", "lvl")),
        P(("dom", "lvl")),
        P(("dom", "lvl")),
        P(("dom", "lvl")),
        P(("dom", "lvl")),
        P(None, ("dom", "lvl")),
        P(("dom", "lvl")),
    )
    out_specs = (P(None, ("dom", "lvl")), P(None, ("dom", "lvl")))
    return jax.shard_map(
        per_device, mesh=mesh, in_specs=in_specs, out_specs=out_specs, check_vma=False
    )
```

```python
import functools

import jax
import jax.numpy as jnp
import numpy as np
from jax import lax
from jax.experimental import pallas as pl
from jax.experimental.pallas import tpu as pltpu
from jax.sharding import PartitionSpec as P

substep_length = 0.01
substeps = 8
MESH = pl.DeviceIdType.MESH
f32 = jnp.float32
bf16 = jnp.bfloat16

BLOCK = (
    [(0, 0), (0, 1), (0, 2), (0, 3), (1, 0), (2, 0), (3, 0)]
    + [(b, c) for b in (1, 2, 3) for c in (1, 2, 3)]
)
CENTRE = BLOCK.index((2, 2))
HIGH = [(4, 0), (4, 1), (4, 2), (4, 3), (1, 4), (2, 4), (3, 4), (0, 4)]
PLANES = [(c, a) for a in (0, 4) for c in range(3)] + [(c, a) for c in range(3) for a in (1, 2, 3)]
MAIN, FACE, TOTAL = 240, 120, 384
SHARED, OUTER, INNER, DELTA = 6, 160, 240, 192


def lobatto_tables():
    points = np.array([-1.0, -np.sqrt(3.0 / 7.0), 0.0, np.sqrt(3.0 / 7.0), 1.0])
    weights = np.array([0.1, 49.0 / 90.0, 32.0 / 45.0, 49.0 / 90.0, 0.1])
    factor = np.array(
        [np.prod([points[i] - points[k] for k in range(5) if k != i]) for i in range(5)]
    )
    matrix = np.zeros((5, 5))
    for i in range(5):
        for j in range(5):
            if i == j:
                matrix[i, j] = sum((1.0 / (points[i] - points[k]) for k in range(5) if k != i))
            else:
                matrix[i, j] = factor[i] / (factor[j] * (points[i] - points[j]))
    cube = weights[:, None, None] * weights[None, :, None] * weights[None, None, :]
    return matrix, cube


def element_operator():
    derivative, cube = lobatto_tables()
    one = np.eye(5)
    along = [
        np.kron(np.kron(derivative, one), one),
        np.kron(np.kron(one, derivative), one),
        np.kron(np.kron(one, one), derivative),
    ]
    weight = cube.reshape(125)
    lame = np.zeros((3, 125, 3, 125))
    shear = np.zeros((3, 125, 3, 125))
    for c in range(3):
        for a in range(3):
            lame[c, :, a, :] += along[c].T @ (weight[:, None] * along[a])
            shear[c, :, c, :] += along[a].T @ (weight[:, None] * along[a])
            shear[c, :, a, :] += along[a].T @ (weight[:, None] * along[c])

    def ordered(planes):
        rows = [c * 125 + a * 25 + b * 5 + k for c, a in planes for b, k in BLOCK]
        rows += [c * 125 + a * 25 + b * 5 + k for c, a in planes for b, k in HIGH]
        return np.array(rows + [c * 125 + a * 25 + 24 for c, a in planes])

    taken = ordered(PLANES)
    shared = ordered(PLANES[:SHARED])
    spots = np.concatenate([np.arange(SHARED * 24), SHARED * 24 + 8 * np.arange(SHARED)])
    parts = []
    for planes, size in ((PLANES[:SHARED], OUTER), (PLANES[SHARED:], INNER)):
        given = ordered(planes)
        part = np.zeros((size, 2 * TOTAL + 2 * DELTA))
        for k, table in enumerate((lame.reshape(375, 375), shear.reshape(375, 375))):
            part[: len(given), k * TOTAL : k * TOTAL + len(taken)] = table[np.ix_(given, taken)]
            at = 2 * TOTAL + k * DELTA
            part[: len(given), at + spots] = table[np.ix_(given, shared)]
        high = part.astype(jnp.bfloat16)
        parts += [high, (part - high.astype(np.float64)).astype(jnp.bfloat16)]
    return np.concatenate(parts, axis=0)


def block_at(c, a):
    return PLANES.index((c, a)) * 16


def node_row(a, b, c):
    return a * 25 + b * 5 + c


NAMES = [
    node_row(2, 0, 2), node_row(2, 4, 2),
    node_row(2, 2, 0), node_row(2, 2, 4),
    node_row(2, 0, 0), node_row(2, 4, 4),
    node_row(0, 2, 2), node_row(4, 2, 2),
]


def lanes(shape):
    return lax.broadcasted_iota(jnp.int32, shape, len(shape) - 1)


def sublanes(shape):
    return lax.broadcasted_iota(jnp.int32, shape, len(shape) - 2)


def split_two(x):
    high = x.astype(bf16).astype(f32)
    return jnp.where(lanes(x.shape) < 64, high, x - high).astype(bf16)


def split_three(x):
    high = x.astype(bf16).astype(f32)
    rest = x - high
    middle = rest.astype(bf16).astype(f32)
    first = jnp.where(lanes(x.shape) < 64, high, middle).astype(bf16)
    second = jnp.where(lanes(x.shape) < 64, rest - middle, 0.0).astype(bf16)
    return jnp.concatenate([first, second], axis=1)


def moved(parts, matrix):
    return jnp.dot(parts, matrix, preferred_element_type=f32)


def same(column, row):
    return jnp.where(column == row, 1.0, 0.0).astype(bf16)


FOLDED = [5, 1, 3, 2, 0, 4, 6, 7, 11, 10, 14, 15, 13, 12, 8, 9]
NAMES_AT, PARAMS_AT, SPEED_AT, MASS_AT, ROWS = 96, 104, 112, 208, 240


def looked_up(index, table):
    found = jnp.int32(table[0])
    for k, value in enumerate(table[1:], 1):
        found = jnp.where(index == k, jnp.int32(value), found)
    return found


def kernel(
    folded, disp_hbm, vel_hbm, mass_hbm, level_hbm, lame_hbm, shear_hbm, conn_hbm, owner_hbm, oper_hbm,
    final_ref, place_ref,
    disp_ref, vel_ref, mass_ref, level_ref, lame_ref, shear_ref, conn_ref, owner_ref, oper_ref, load_sem,
    conn_s, tile_s, pick_s, hot_hi, hot_lo, u_s, v_s, m_s, f_s, x_s, elem_s, known_s, change_s, rate_s,
    pack_out, pack_in, back_out, back_in,
    low_out, low_in, name_out, name_in, send_buf, recv_buf,
    init_send, init_recv, step_send, step_recv, bulk_send, bulk_recv,
):
    dom_size, lvl_size = lax.axis_size("dom"), lax.axis_size("lvl")
    count = dom_size * lvl_size
    me = lax.axis_index("dom") * lvl_size + lax.axis_index("lvl")

    loads = [
        pltpu.make_async_copy(src, dst, load_sem.at[k])
        for k, (src, dst) in enumerate([
            (conn_hbm, conn_ref), (disp_hbm, disp_ref), (vel_hbm, vel_ref), (mass_hbm, mass_ref),
            (owner_hbm, owner_ref), (level_hbm, level_ref), (lame_hbm, lame_ref),
            (shear_hbm, shear_ref), (oper_hbm, oper_ref),
        ])
    ]
    for load in loads:
        load.start()

    def device(index):
        return (index // lvl_size, lax.rem(index, lvl_size))

    def step(index, distance):
        return lax.rem(index + count + distance, count)

    if folded:
        order = [FOLDED.index(k) for k in range(count // 2)]

        def host_of(index):
            return looked_up(index // 2, FOLDED) * 2 + lax.rem(index, 2)

        home = looked_up(me // 2, order) * 2 + lax.rem(me, 2)
        host = host_of(me)
        away = host != me
        after, before = host_of(step(home, 1)), host_of(step(home, -1))
        low_to, name_to = host_of(step(me, -1)), host_of(step(me, 1))
        peers = [after, before, low_to, name_to, step(home, 1), step(home, -1)]
        host_id, home_id = device(host), device(home)
    else:
        after, before = step(me, 1), step(me, -1)
        low_to, name_to = before, after
        peers = [after, before]
    after_id, before_id = device(after), device(before)

    barrier = pltpu.get_barrier_semaphore()
    for other in peers:
        pl.semaphore_signal(barrier, inc=1, device_id=device(other), device_id_type=MESH)
    if folded:

        @pl.when(away)
        def _():
            for other in (host_id, home_id):
                pl.semaphore_signal(barrier, inc=1, device_id=other, device_id_type=MESH)

    def bulk(src, dst, k, other):
        return pltpu.make_async_remote_copy(
            src_ref=src, dst_ref=dst, send_sem=bulk_send.at[k], recv_sem=bulk_recv.at[k],
            device_id=other, device_id_type=MESH,
        )

    loads[0].wait()
    tile_s[...] = jnp.zeros((128, 128), f32)
    for k in range(2):
        tile_s[k * 64 : k * 64 + 64, 0:125] = conn_ref[...].astype(f32)
    conn_s[...] = jnp.transpose(tile_s[...])

    low_half = lanes((1, 128)) < 64
    for a in range(2):
        for j, (b, c) in enumerate(BLOCK):
            r0, r1 = node_row(a, b, c), node_row(a + 2, b, c)
            pick_s[a * 16 + j : a * 16 + j + 1, :] = jnp.where(
                low_half, conn_s[r0 : r0 + 1, :], conn_s[r1 : r1 + 1, :]
            ).astype(jnp.int32)
    pick = pick_s[...]
    pick_hi, pick_lo = lax.shift_right_logical(pick, 7), lax.bitwise_and(pick, 127)

    def gathered(refs, singles):
        def gather_step(t, kept):
            here = pick_hi == t
            cols = pl.ds(pl.multiple_of(t * 128, 128), 128)
            rows = [ref[c : c + 1, cols] for ref in refs for c in range(3)]
            rows += [ref[pl.ds(t, 1), :] for ref in singles]
            new = []
            for row, old in zip(rows, kept):
                got = jnp.take_along_axis(
                    jnp.broadcast_to(row, (32, 128)), pick_lo, axis=1, mode="promise_in_bounds"
                )
                new.append(jnp.where(here, got, old))
            return tuple(new)

        start = tuple(jnp.zeros((32, 128), f32) for _ in range(3 * len(refs) + len(singles)))
        return list(lax.fori_loop(0, 32, gather_step, start, unroll=4))

    for load in loads[1:8]:
        load.wait()
    got = gathered([disp_ref], [])
    half = lanes((32, 128)) < 64
    for k in range(3):
        pack_out[k * 32 : k * 32 + 32, :] = got[k]

    for k, r in enumerate(NAMES):
        pack_out[NAMES_AT + k : NAMES_AT + k + 1, :] = conn_s[r : r + 1, :]
    tile_s[0:8, :] = jnp.zeros((8, 128), f32)
    tile_s[0:4, :] = owner_ref[...].astype(f32)
    columns = jnp.transpose(tile_s[...])
    low_name = conn_s[NAMES[6] : NAMES[6] + 1, :]
    slot_low = jnp.full((1, 128), -9999.0, f32)
    for k in range(4):
        hit = columns[:, k : k + 1] == low_name
        number = sublanes((128, 128)).astype(f32) + (k * 128 + 9999)
        slot_low = slot_low + jnp.sum(jnp.where(hit, number, 0.0), axis=0, keepdims=True)
    pack_out[PARAMS_AT : PARAMS_AT + 8, :] = jnp.zeros((8, 128), f32)
    pack_out[PARAMS_AT : PARAMS_AT + 1, :] = slot_low
    for k, ref in enumerate((level_ref, lame_ref, shear_ref), 1):
        for at in (0, 64):
            pack_out[PARAMS_AT + k : PARAMS_AT + k + 1, at : at + 64] = ref[...].astype(f32)

    def first_move():
        return bulk(pack_out.at[0:SPEED_AT], pack_in.at[0:SPEED_AT], 0, host_id)

    def second_move():
        return bulk(pack_out.at[SPEED_AT:ROWS], pack_in.at[SPEED_AT:ROWS], 1, host_id)

    if folded:

        @pl.when(away)
        def _():
            pl.semaphore_wait(barrier, 8)
            first_move().start()

        @pl.when(jnp.logical_not(away))
        def _():
            pl.semaphore_wait(barrier, 6)
    else:
        pl.semaphore_wait(barrier, 2)
    got = got + gathered([vel_ref], [mass_ref])
    for k in range(3, 7):
        at = SPEED_AT + (k - 3) * 32
        pack_out[at : at + 32, :] = got[k]
    if folded:

        @pl.when(away)
        def _():
            second_move().start()

    half16 = lanes((16, 128)) < 64
    for k in range(4):
        other = got[min(2 * k + 1, 6)][0:16]
        low_out[k * 16 : k * 16 + 16, :] = jnp.where(
            half16, got[2 * k][0:16], pltpu.roll(other, 64, axis=1)
        )
    low_out[64:72, :] = jnp.broadcast_to(slot_low, (8, 128))
    owned = float(disp_ref.shape[1])
    name_out[...] = jnp.broadcast_to(conn_s[NAMES[7] : NAMES[7] + 1, :] - owned, (8, 128))
    low_copy = pltpu.make_async_remote_copy(
        src_ref=low_out, dst_ref=low_in, send_sem=init_send.at[0], recv_sem=init_recv.at[0],
        device_id=device(low_to), device_id_type=MESH,
    )
    name_copy = pltpu.make_async_remote_copy(
        src_ref=name_out, dst_ref=name_in, send_sem=init_send.at[1], recv_sem=init_recv.at[1],
        device_id=device(name_to), device_id_type=MESH,
    )
    low_copy.start()
    name_copy.start()

    def find_places():
        for r in range(32):
            cols = slice(r * 128, r * 128 + 128)
            hit = pick_hi[r : r + 1, :] == sublanes((32, 128))
            hot_hi[0:32, cols] = jnp.where(hit, lanes((32, 128)).astype(f32), 0.0).astype(bf16)
            hot_hi[32:64, cols] = jnp.where(hit, float(r), 0.0).astype(bf16)
            hot_lo[:, cols] = same(sublanes((128, 128)), pick_lo[r : r + 1, :])
        place = lax.dot_general(
            hot_hi[...], hot_lo[...], (((1,), (1,)), ((), ())), preferred_element_type=f32
        )
        return place[0:32].astype(jnp.int32), place[32:64].astype(jnp.int32)

    place_lane, place_row = find_places()
    place_ref[0:32, :] = place_lane
    place_ref[32:64, :] = place_row
    if folded:

        @pl.when(away)
        def _():
            first_move().wait()
            second_move().wait()

        @pl.when(jnp.logical_not(away))
        def _():
            pack_in[...] = pack_out[...]

    held = pack_in if folded else pack_out
    for k, ref in enumerate([u_s] * 3 + [v_s] * 3 + [m_s]):
        at = k * 32 if k < 3 else SPEED_AT + (k - 3) * 32
        packed = held[at : at + 32, :]
        turned = pltpu.roll(packed, 64, axis=1)
        low, high = jnp.where(half, packed, turned), jnp.where(half, turned, packed)
        for a in range(4):
            at = block_at(k % 3, a) if k < 6 else a * 16
            ref[at : at + 16, :] = (low if a < 2 else high)[a % 2 * 16 : a % 2 * 16 + 16]
    u_s[MAIN : MAIN + 16, :] = jnp.zeros((16, 128), f32)
    f_s[MAIN : MAIN + 16, :] = jnp.zeros((16, 128), f32)
    elem_s[...] = held[PARAMS_AT : PARAMS_AT + 8, :]
    slot_low = elem_s[0:1, :]
    name_row = [held[NAMES_AT + k : NAMES_AT + k + 1, :] for k in range(8)]
    slot_high = name_row[7] - owned

    tile_s[0:8, :] = held[NAMES_AT : NAMES_AT + 8, :]
    columns = jnp.transpose(tile_s[...])
    name_col = [columns[:, k : k + 1] for k in range(8)]
    to_y, to_z = same(name_col[0], name_row[1]), same(name_col[2], name_row[3])
    to_edge = same(name_col[4], name_row[5])
    spread = jnp.concatenate([to_y, to_z], axis=1)
    spread = jnp.concatenate([spread, spread], axis=0)
    spread_edge = jnp.concatenate([to_edge, to_edge], axis=0)
    collect = jnp.concatenate(
        [same(name_col[1], name_row[0]), same(name_col[3], name_row[2])], axis=1
    )
    collect_edge = same(name_col[5], name_row[4])
    to_high = same(name_col[6], name_row[7])
    to_low = same(name_col[7], name_row[6])

    low_copy.wait()
    name_copy.wait()
    tile_s[0:8, :] = low_in[64:72, :]
    tile_s[8:16, :] = name_in[...]
    columns = jnp.transpose(tile_s[...])
    from_after = same(columns[:, 0:1], slot_high)
    from_before = same(columns[:, 8:9], slot_low)
    to_high_twice = jnp.concatenate([to_high, to_high], axis=0)
    from_after_twice = jnp.concatenate([from_after, from_after], axis=0)
    theirs = []
    for k in range(7):
        packed = low_in[k // 2 * 16 : k // 2 * 16 + 16, :]
        turned = pltpu.roll(packed, 64, axis=1)
        theirs.append(jnp.where(half16 if k % 2 == 0 else jnp.logical_not(half16), packed, turned))
    ours = jnp.concatenate([u_s[0:48, :], v_s[0:48, :], m_s[0:16, :]], axis=0)
    high = moved(split_three(ours), to_high_twice)
    high = high + moved(split_three(jnp.concatenate(theirs, axis=0)), from_after_twice)
    u_s[48:96, :] = high[0:48]
    v_s[48:96, :] = high[48:96]
    m_s[64:80, :] = high[96:112]
    loads[8].wait()

    level = elem_s[1:2, :]
    period = jnp.where(level == 0.0, 8, jnp.where(level == 1.0, 4, jnp.where(level == 2.0, 2, 1)))
    row8 = sublanes((15, 8, 128))
    row16 = sublanes((16, 128))
    in_first = (row16 == 0) | (row16 == 3) | ((row16 >= 6) & (row16 < 9))
    in_second = (row16 == 1) | (row16 == 4) | ((row16 >= 9) & (row16 < 12))
    half24 = lanes((24, 128)) < 64

    def face_of(along_y, along_z):
        row = row8[0 : along_y.shape[0]]
        turned = pltpu.roll(along_z, 7, axis=1)
        return jnp.where(row < 4, along_y, jnp.where(row < 7, along_z, turned))

    def passed_on(matrix):
        onward = jnp.concatenate([to_y, to_z, to_edge], axis=1)
        return jnp.concatenate([matrix, (0.5 * moved(matrix, onward)).astype(bf16)], axis=1)

    onto_low, onto_high = passed_on(from_before), passed_on(from_after)

    def thrice(x):
        return jnp.concatenate([x, x, x], axis=0)

    for k, at in enumerate((0, 64)):
        block = m_s[at : at + 16, :]
        top = split_three(block[0:8])
        faces = moved(top, spread)
        face = face_of(faces[:, 0:128].reshape(1, 8, 128), faces[:, 128:256].reshape(1, 8, 128))
        edge = moved(top, spread_edge)
        rate_s[k * 48 : k * 48 + 48, :] = -substep_length * thrice(block)
        rate_s[96 + k * 24 : 120 + k * 24, :] = -substep_length * thrice(face.reshape(8, 128))
        rate_s[144 + k * 24 : 168 + k * 24, :] = -substep_length * thrice(edge)

    def advance(first, size, mass, force):
        rows = pl.ds(first, size)
        speed = v_s[rows, :] - substep_length * mass * force
        v_s[rows, :] = speed
        u_s[rows, :] = u_s[rows, :] + substep_length * speed

    def summed(force, planes, first):
        force = force + pltpu.roll(force, 64, axis=1)
        main, faces = planes * 16, planes * 24
        moved_face = moved(split_two(force[main:faces]), collect)
        along_y = moved_face[:, 0:128].reshape(planes, 8, 128)
        along_z = moved_face[:, 128:256].reshape(planes, 8, 128)
        row = row8[0:planes]
        low = jnp.where(row < 4, along_y, jnp.where(row < 7, along_z, 0.0))
        low = low + jnp.where(row == 0, pltpu.roll(along_z, 1, axis=1), 0.0)
        both = force[0:main].reshape(planes, 2, 8, 128)
        both = jnp.concatenate([both[:, 0:1] + low[:, None], both[:, 1:2]], axis=1)
        f_s[first : first + main, :] = both.reshape(main, 128)
        edge = moved(split_two(force[faces:]), collect_edge)[0:planes]
        at = pl.ds(first, planes, stride=16)
        f_s[at, :] = f_s[at, :] + edge

    def unpacked(packed):
        turned = pltpu.roll(packed, 64, axis=1)
        return jnp.concatenate(
            [jnp.where(half24, packed, turned), jnp.where(half24, turned, packed)], axis=0
        )

    def weights(s):
        active = lax.rem(jnp.full((1, 128), s, jnp.int32), period) == 0
        weight = jnp.where(active, period.astype(f32), 0.0)
        return elem_s[2:3, :] * weight, elem_s[3:4, :] * weight

    def exchange(s):
        return [
            pltpu.make_async_remote_copy(
                src_ref=send_buf.at[s, way], dst_ref=recv_buf.at[s, way],
                send_sem=step_send.at[s, way], recv_sem=step_recv.at[s, way],
                device_id=other, device_id_type=MESH,
            )
            for way, other in enumerate((before_id, after_id))
        ]

    def know(s):
        u = u_s[0:MAIN, :].reshape(15, 16, 128)
        faces = moved(split_three(u[:, 0:8].reshape(FACE, 128)), spread)
        face = face_of(faces[:, 0:128].reshape(15, 8, 128), faces[:, 128:256].reshape(15, 8, 128))
        edge = moved(split_three(u_s[pl.ds(0, 16, stride=16), :]), spread_edge)
        centres = []
        for c in range(3):
            at = block_at(c, 2) + CENTRE
            centres.append(u_s[at : at + 1, :])
        edge = edge - jnp.where(in_first, centres[0], jnp.where(in_second, centres[1], centres[2]))
        edge = jnp.where(row16 < 15, edge, 0.0)
        main = [u[k] - centres[c] for k, (c, _) in enumerate(PLANES)]
        face = [face[k] - centres[c] for k, (c, _) in enumerate(PLANES)]
        values = jnp.concatenate(main + face + [edge, jnp.zeros((8, 128), f32)], axis=0)
        for k, weight in enumerate(weights(s)):
            x_s[k * TOTAL : (k + 1) * TOTAL, :] = split_two(values * weight)
        x = x_s[...]
        for first, size in ((0, OUTER), (OUTER, INNER)):
            rows = slice(2 * first, 2 * (first + size))
            product = jnp.dot(oper_ref[rows, 0 : 2 * TOTAL], x, preferred_element_type=f32)
            known_s[first : first + size, :] = product[0:size] + product[size:]

    def arrived(s):
        for copy in exchange(s)[::-1]:
            copy.wait()
        both = [
            moved(split_two(unpacked(recv_buf[s, way])), matrix)
            for way, matrix in ((1, onto_low), (0, onto_high))
        ]
        main = jnp.concatenate([x[:, 0:128] for x in both], axis=0) * rate_s[0:96, :]
        v_s[0:96, :] = v_s[0:96, :] + main
        main = substep_length * main
        u_s[0:96, :] = u_s[0:96, :] + main
        tops = [
            jnp.concatenate(
                [x[:, k * 128 : k * 128 + 128].reshape(3, 16, 128)[:, 0:8] for x in both], axis=0
            )
            for k in (1, 2, 3)
        ]
        rest = jnp.concatenate(
            [face_of(tops[0], tops[1]).reshape(48, 128), tops[2].reshape(48, 128)], axis=0
        )
        return jnp.concatenate([main, substep_length * rest * rate_s[96:192, :]], axis=0)

    def changed(first, size):
        rows = slice(2 * first, 2 * (first + size))
        product = jnp.dot(oper_ref[rows, 2 * TOTAL :], change_s[...], preferred_element_type=f32)
        return product[0:size] + product[size:]

    def substep(s, follow):
        if follow:
            change = arrived(s - 1)
            for k, weight in enumerate(weights(s)):
                change_s[k * DELTA : (k + 1) * DELTA, :] = split_two(change * weight)
        force = known_s[0:OUTER, :]
        summed(force + changed(0, OUTER) if follow else force, SHARED, 0)
        low_x, high_x = f_s[0:48, :], f_s[48:96, :]
        send_buf[s, 0] = jnp.where(half24, low_x[0:24], low_x[24:48])
        send_buf[s, 1] = jnp.where(half24, high_x[0:24], high_x[24:48])
        for copy in exchange(s)[::-1]:
            copy.start()
        force = known_s[OUTER : OUTER + INNER, :]
        summed(force + changed(OUTER, INNER) if follow else force, 15 - SHARED, 96)
        low_sum = low_x + moved(split_two(high_x), to_low)
        high_sum = high_x + moved(split_two(low_x), to_high)
        advance(96, 144, thrice(m_s[16:64, :]), f_s[96:240, :])
        advance(0, 48, thrice(m_s[0:16, :]), low_sum)
        advance(48, 48, thrice(m_s[64:80, :]), high_sum)

    def follow_on(s, carry):
        substep(s, True)
        know(s + 1)
        return carry

    know(0)
    substep(0, False)
    know(1)
    lax.fori_loop(1, substeps - 1, follow_on, 0)
    substep(substeps - 1, True)

    def back(part):
        rows = slice(part * 96, part * 96 + 96)
        return bulk(back_out.at[rows], back_in.at[rows], 2 + part, home_id)

    for part, a in enumerate((1, 0)):
        if part == 1:
            arrived(substeps - 1)
        for k in range(6):
            ref, at = (u_s if k < 3 else v_s), part * 96 + k * 16
            one, two = block_at(k % 3, a), block_at(k % 3, a + 2)
            back_out[at : at + 16, :] = jnp.where(
                half16, ref[one : one + 16, :], ref[two : two + 16, :]
            )
        if folded:

            @pl.when(away)
            def _():
                back(part).start()

    if folded:

        @pl.when(away)
        def _():
            for part in range(2):
                back(part).wait()
            final_ref[...] = back_in[...]

        @pl.when(jnp.logical_not(away))
        def _():
            final_ref[...] = back_out[...]
    else:
        final_ref[...] = back_out[...]


def reorder(final_ref, place_ref, out_u_ref, out_v_ref):
    place_lane, place_row = place_ref[0:32, :], place_ref[32:64, :]

    def scatter_step(t, kept):
        here = place_row == t
        first = jnp.where(t < 16, t + 96, t - 16)
        new = []
        for k in range(6):
            row = final_ref[pl.ds(k * 16 + first, 1), :]
            got = jnp.take_along_axis(
                jnp.broadcast_to(row, (32, 128)), place_lane, axis=1, mode="promise_in_bounds"
            )
            new.append(jnp.where(here, got, kept[k]))
        return tuple(new)

    done = lax.fori_loop(
        0, 32, scatter_step, tuple(jnp.zeros((32, 128), f32) for _ in range(6)), unroll=4
    )
    for k in range(6):
        ref = out_u_ref if k < 3 else out_v_ref
        for t in range(32):
            ref[k % 3 : k % 3 + 1, t * 128 : t * 128 + 128] = done[k][t : t + 1]


def per_device(
    displacement, velocity, inverse_mass, levels, first_lame, shear_modulus, connectivity, owner_list
):
    operator = jnp.asarray(element_operator())
    nodes = displacement.shape[1]
    vmem = pl.BlockSpec(memory_space=pltpu.VMEM)
    hbm = pl.BlockSpec(memory_space=pltpu.HBM)
    shape = jax.ShapeDtypeStruct((3, nodes), f32)
    V, S = pltpu.VMEM, pltpu.SemaphoreType.DMA
    operands = (
        displacement, velocity, inverse_mass.reshape(32, 128),
        levels.reshape(1, 64), first_lame.reshape(1, 64), shear_modulus.reshape(1, 64),
        connectivity.T, owner_list.reshape(4, 128), operator,
    )
    folded = lax.axis_size("dom") == 8 and lax.axis_size("lvl") == 4
    held = (jax.ShapeDtypeStruct((192, 128), f32), jax.ShapeDtypeStruct((64, 128), jnp.int32))
    final, place = pl.pallas_call(
        functools.partial(kernel, folded),
        out_shape=held,
        in_specs=[hbm] * 9,
        out_specs=(vmem, vmem),
        scratch_shapes=[V(x.shape, x.dtype) for x in operands] + [S((9,))] + [
            V((128, 128), f32), V((128, 128), f32), V((32, 128), jnp.int32),
            V((64, 4096), bf16), V((128, 4096), bf16),
            V((256, 128), f32), V((256, 128), f32), V((80, 128), f32), V((256, 128), f32),
            V((2 * TOTAL, 128), bf16), V((8, 128), f32),
            V((OUTER + INNER, 128), f32), V((2 * DELTA, 128), bf16), V((DELTA, 128), f32),
            V((ROWS, 128), f32), V((ROWS, 128), f32), V((192, 128), f32), V((192, 128), f32),
            V((72, 128), f32), V((72, 128), f32), V((8, 128), f32), V((8, 128), f32),
            V((substeps, 2, 24, 128), f32), V((substeps, 2, 24, 128), f32),
            S((2,)), S((2,)), S((substeps, 2)), S((substeps, 2)), S((4,)), S((4,)),
        ],
        compiler_params=pltpu.CompilerParams(
            collective_id=0, has_side_effects=True, vmem_limit_bytes=63 * 1024 * 1024
        ),
    )(*operands)
    return pl.pallas_call(
        reorder,
        out_shape=(shape, shape),
        in_specs=[vmem] * 2,
        out_specs=(vmem, vmem),
        compiler_params=pltpu.CompilerParams(vmem_limit_bytes=63 * 1024 * 1024),
    )(final, place)


def solution(mesh):
    in_specs = (
        P(None, ("dom", "lvl")),
        P(None, ("dom", "lvl")),
        P(("dom", "lvl")),
        P(("dom", "lvl")),
        P(("dom", "lvl")),
        P(("dom", "lvl")),
        P(None, ("dom", "lvl")),
        P(("dom", "lvl")),
    )
    out_specs = (P(None, ("dom", "lvl")), P(None, ("dom", "lvl")))
    return jax.shard_map(
        per_device, mesh=mesh, in_specs=in_specs, out_specs=out_specs, check_vma=False
    )
```

```python
import functools

import jax
import jax.numpy as jnp
import numpy as np
from jax import lax
from jax.experimental import pallas as pl
from jax.experimental.pallas import tpu as pltpu
from jax.sharding import PartitionSpec as P

substep_length = 0.01
substeps = 8
MESH = pl.DeviceIdType.MESH
f32 = jnp.float32
bf16 = jnp.bfloat16

BLOCK = (
    [(0, 0), (0, 1), (0, 2), (0, 3), (1, 0), (2, 0), (3, 0)]
    + [(b, c) for b in (1, 2, 3) for c in (1, 2, 3)]
)
CENTRE = BLOCK.index((2, 2))
HIGH = [(4, 0), (4, 1), (4, 2), (4, 3), (1, 4), (2, 4), (3, 4), (0, 4)]
PLANES = [(c, a) for a in (0, 4) for c in range(3)] + [(c, a) for c in range(3) for a in (1, 2, 3)]
MAIN, FACE, TOTAL = 240, 120, 384
SHARED, OUTER, INNER, DELTA = 6, 160, 240, 192


def lobatto_tables():
    points = np.array([-1.0, -np.sqrt(3.0 / 7.0), 0.0, np.sqrt(3.0 / 7.0), 1.0])
    weights = np.array([0.1, 49.0 / 90.0, 32.0 / 45.0, 49.0 / 90.0, 0.1])
    factor = np.array(
        [np.prod([points[i] - points[k] for k in range(5) if k != i]) for i in range(5)]
    )
    matrix = np.zeros((5, 5))
    for i in range(5):
        for j in range(5):
            if i == j:
                matrix[i, j] = sum((1.0 / (points[i] - points[k]) for k in range(5) if k != i))
            else:
                matrix[i, j] = factor[i] / (factor[j] * (points[i] - points[j]))
    cube = weights[:, None, None] * weights[None, :, None] * weights[None, None, :]
    return matrix, cube


def element_operator():
    derivative, cube = lobatto_tables()
    one = np.eye(5)
    along = [
        np.kron(np.kron(derivative, one), one),
        np.kron(np.kron(one, derivative), one),
        np.kron(np.kron(one, one), derivative),
    ]
    weight = cube.reshape(125)
    lame = np.zeros((3, 125, 3, 125))
    shear = np.zeros((3, 125, 3, 125))
    for c in range(3):
        for a in range(3):
            lame[c, :, a, :] += along[c].T @ (weight[:, None] * along[a])
            shear[c, :, c, :] += along[a].T @ (weight[:, None] * along[a])
            shear[c, :, a, :] += along[a].T @ (weight[:, None] * along[c])

    def ordered(planes):
        rows = [c * 125 + a * 25 + b * 5 + k for c, a in planes for b, k in BLOCK]
        rows += [c * 125 + a * 25 + b * 5 + k for c, a in planes for b, k in HIGH]
        return np.array(rows + [c * 125 + a * 25 + 24 for c, a in planes])

    taken = ordered(PLANES)
    shared = ordered(PLANES[:SHARED])
    spots = np.concatenate([np.arange(SHARED * 24), SHARED * 24 + 8 * np.arange(SHARED)])
    parts = []
    for planes, size in ((PLANES[:SHARED], OUTER), (PLANES[SHARED:], INNER)):
        given = ordered(planes)
        part = np.zeros((size, 2 * TOTAL + 2 * DELTA))
        for k, table in enumerate((lame.reshape(375, 375), shear.reshape(375, 375))):
            part[: len(given), k * TOTAL : k * TOTAL + len(taken)] = table[np.ix_(given, taken)]
            at = 2 * TOTAL + k * DELTA
            part[: len(given), at + spots] = table[np.ix_(given, shared)]
        high = part.astype(jnp.bfloat16)
        parts += [high, (part - high.astype(np.float64)).astype(jnp.bfloat16)]
    return np.concatenate(parts, axis=0)


def block_at(c, a):
    return PLANES.index((c, a)) * 16


def node_row(a, b, c):
    return a * 25 + b * 5 + c


NAMES = [
    node_row(2, 0, 2), node_row(2, 4, 2),
    node_row(2, 2, 0), node_row(2, 2, 4),
    node_row(2, 0, 0), node_row(2, 4, 4),
    node_row(0, 2, 2), node_row(4, 2, 2),
]


def lanes(shape):
    return lax.broadcasted_iota(jnp.int32, shape, len(shape) - 1)


def sublanes(shape):
    return lax.broadcasted_iota(jnp.int32, shape, len(shape) - 2)


def split_two(x):
    high = x.astype(bf16).astype(f32)
    return jnp.where(lanes(x.shape) < 64, high, x - high).astype(bf16)


def split_three(x):
    high = x.astype(bf16).astype(f32)
    rest = x - high
    middle = rest.astype(bf16).astype(f32)
    first = jnp.where(lanes(x.shape) < 64, high, middle).astype(bf16)
    second = jnp.where(lanes(x.shape) < 64, rest - middle, 0.0).astype(bf16)
    return jnp.concatenate([first, second], axis=1)


def moved(parts, matrix):
    return jnp.dot(parts, matrix, preferred_element_type=f32)


def same(column, row):
    return jnp.where(column == row, 1.0, 0.0).astype(bf16)


FOLDED = [5, 1, 3, 2, 0, 4, 6, 7, 11, 10, 14, 15, 13, 12, 8, 9]
NAMES_AT, PARAMS_AT, SPEED_AT, MASS_AT, ROWS = 96, 104, 112, 208, 240


def looked_up(index, table):
    found = jnp.int32(table[0])
    for k, value in enumerate(table[1:], 1):
        found = jnp.where(index == k, jnp.int32(value), found)
    return found


def kernel(
    folded, disp_hbm, vel_hbm, mass_hbm, level_hbm, lame_hbm, shear_hbm, conn_hbm, owner_hbm, oper_hbm,
    final_ref, place_ref,
    disp_ref, vel_ref, mass_ref, level_ref, lame_ref, shear_ref, conn_ref, owner_ref, oper_ref, load_sem,
    conn_s, tile_s, pick_s, hot_hi, hot_lo, u_s, v_s, m_s, f_s, x_s, elem_s, known_s, change_s, rate_s, value_s, edge_s,
    pack_out, pack_in, back_out, back_in,
    low_out, low_in, name_out, name_in, send_buf, recv_buf,
    init_send, init_recv, step_send, step_recv, bulk_send, bulk_recv,
):
    dom_size, lvl_size = lax.axis_size("dom"), lax.axis_size("lvl")
    count = dom_size * lvl_size
    me = lax.axis_index("dom") * lvl_size + lax.axis_index("lvl")

    loads = [
        pltpu.make_async_copy(src, dst, load_sem.at[k])
        for k, (src, dst) in enumerate([
            (conn_hbm, conn_ref), (disp_hbm, disp_ref), (vel_hbm, vel_ref), (mass_hbm, mass_ref),
            (owner_hbm, owner_ref), (level_hbm, level_ref), (lame_hbm, lame_ref),
            (shear_hbm, shear_ref), (oper_hbm, oper_ref),
        ])
    ]
    for load in loads:
        load.start()

    def device(index):
        return (index // lvl_size, lax.rem(index, lvl_size))

    def step(index, distance):
        return lax.rem(index + count + distance, count)

    if folded:
        order = [FOLDED.index(k) for k in range(count // 2)]

        def host_of(index):
            return looked_up(index // 2, FOLDED) * 2 + lax.rem(index, 2)

        home = looked_up(me // 2, order) * 2 + lax.rem(me, 2)
        host = host_of(me)
        away = host != me
        after, before = host_of(step(home, 1)), host_of(step(home, -1))
        low_to, name_to = host_of(step(me, -1)), host_of(step(me, 1))
        peers = [after, before, low_to, name_to, step(home, 1), step(home, -1)]
        host_id, home_id = device(host), device(home)
    else:
        after, before = step(me, 1), step(me, -1)
        low_to, name_to = before, after
        peers = [after, before]
    after_id, before_id = device(after), device(before)

    barrier = pltpu.get_barrier_semaphore()
    for other in peers:
        pl.semaphore_signal(barrier, inc=1, device_id=device(other), device_id_type=MESH)
    if folded:

        @pl.when(away)
        def _():
            for other in (host_id, home_id):
                pl.semaphore_signal(barrier, inc=1, device_id=other, device_id_type=MESH)

    def bulk(src, dst, k, other):
        return pltpu.make_async_remote_copy(
            src_ref=src, dst_ref=dst, send_sem=bulk_send.at[k], recv_sem=bulk_recv.at[k],
            device_id=other, device_id_type=MESH,
        )

    loads[0].wait()
    tile_s[...] = jnp.zeros((128, 128), f32)
    for k in range(2):
        tile_s[k * 64 : k * 64 + 64, 0:125] = conn_ref[...].astype(f32)
    conn_s[...] = jnp.transpose(tile_s[...])

    low_half = lanes((1, 128)) < 64
    for a in range(2):
        for j, (b, c) in enumerate(BLOCK):
            r0, r1 = node_row(a, b, c), node_row(a + 2, b, c)
            pick_s[a * 16 + j : a * 16 + j + 1, :] = jnp.where(
                low_half, conn_s[r0 : r0 + 1, :], conn_s[r1 : r1 + 1, :]
            ).astype(jnp.int32)
    pick = pick_s[...]
    pick_hi, pick_lo = lax.shift_right_logical(pick, 7), lax.bitwise_and(pick, 127)

    def gathered(refs, singles):
        def gather_step(t, kept):
            here = pick_hi == t
            cols = pl.ds(pl.multiple_of(t * 128, 128), 128)
            rows = [ref[c : c + 1, cols] for ref in refs for c in range(3)]
            rows += [ref[pl.ds(t, 1), :] for ref in singles]
            new = []
            for row, old in zip(rows, kept):
                got = jnp.take_along_axis(
                    jnp.broadcast_to(row, (32, 128)), pick_lo, axis=1, mode="promise_in_bounds"
                )
                new.append(jnp.where(here, got, old))
            return tuple(new)

        start = tuple(jnp.zeros((32, 128), f32) for _ in range(3 * len(refs) + len(singles)))
        return list(lax.fori_loop(0, 32, gather_step, start, unroll=32))

    for load in loads[1:8]:
        load.wait()
    got = gathered([disp_ref], [])
    half = lanes((32, 128)) < 64
    for k in range(3):
        pack_out[k * 32 : k * 32 + 32, :] = got[k]

    for k, r in enumerate(NAMES):
        pack_out[NAMES_AT + k : NAMES_AT + k + 1, :] = conn_s[r : r + 1, :]
    tile_s[0:8, :] = jnp.zeros((8, 128), f32)
    tile_s[0:4, :] = owner_ref[...].astype(f32)
    columns = jnp.transpose(tile_s[...])
    low_name = conn_s[NAMES[6] : NAMES[6] + 1, :]
    slot_low = jnp.full((1, 128), -9999.0, f32)
    for k in range(4):
        hit = columns[:, k : k + 1] == low_name
        number = sublanes((128, 128)).astype(f32) + (k * 128 + 9999)
        slot_low = slot_low + jnp.sum(jnp.where(hit, number, 0.0), axis=0, keepdims=True)
    pack_out[PARAMS_AT : PARAMS_AT + 8, :] = jnp.zeros((8, 128), f32)
    pack_out[PARAMS_AT : PARAMS_AT + 1, :] = slot_low
    for k, ref in enumerate((level_ref, lame_ref, shear_ref), 1):
        for at in (0, 64):
            pack_out[PARAMS_AT + k : PARAMS_AT + k + 1, at : at + 64] = ref[...].astype(f32)

    def first_move():
        return bulk(pack_out.at[0:SPEED_AT], pack_in.at[0:SPEED_AT], 0, host_id)

    def second_move():
        return bulk(pack_out.at[SPEED_AT:ROWS], pack_in.at[SPEED_AT:ROWS], 1, host_id)

    if folded:

        @pl.when(away)
        def _():
            pl.semaphore_wait(barrier, 8)
            first_move().start()

        @pl.when(jnp.logical_not(away))
        def _():
            pl.semaphore_wait(barrier, 6)
    else:
        pl.semaphore_wait(barrier, 2)
    got = got + gathered([vel_ref], [mass_ref])
    for k in range(3, 7):
        at = SPEED_AT + (k - 3) * 32
        pack_out[at : at + 32, :] = got[k]
    if folded:

        @pl.when(away)
        def _():
            second_move().start()

    half16 = lanes((16, 128)) < 64
    for k in range(4):
        other = got[min(2 * k + 1, 6)][0:16]
        low_out[k * 16 : k * 16 + 16, :] = jnp.where(
            half16, got[2 * k][0:16], pltpu.roll(other, 64, axis=1)
        )
    low_out[64:72, :] = jnp.broadcast_to(slot_low, (8, 128))
    owned = float(disp_ref.shape[1])
    name_out[...] = jnp.broadcast_to(conn_s[NAMES[7] : NAMES[7] + 1, :] - owned, (8, 128))
    low_copy = pltpu.make_async_remote_copy(
        src_ref=low_out, dst_ref=low_in, send_sem=init_send.at[0], recv_sem=init_recv.at[0],
        device_id=device(low_to), device_id_type=MESH,
    )
    name_copy = pltpu.make_async_remote_copy(
        src_ref=name_out, dst_ref=name_in, send_sem=init_send.at[1], recv_sem=init_recv.at[1],
        device_id=device(name_to), device_id_type=MESH,
    )
    low_copy.start()
    name_copy.start()

    def find_places():
        for r in range(32):
            cols = slice(r * 128, r * 128 + 128)
            hit = pick_hi[r : r + 1, :] == sublanes((32, 128))
            hot_hi[0:32, cols] = jnp.where(hit, lanes((32, 128)).astype(f32), 0.0).astype(bf16)
            hot_hi[32:64, cols] = jnp.where(hit, float(r), 0.0).astype(bf16)
            hot_lo[:, cols] = same(sublanes((128, 128)), pick_lo[r : r + 1, :])
        place = lax.dot_general(
            hot_hi[...], hot_lo[...], (((1,), (1,)), ((), ())), preferred_element_type=f32
        )
        return place[0:32].astype(jnp.int32), place[32:64].astype(jnp.int32)

    place_lane, place_row = find_places()
    place_ref[0:32, :] = place_lane
    place_ref[32:64, :] = place_row
    if folded:

        @pl.when(away)
        def _():
            first_move().wait()
            second_move().wait()

        @pl.when(jnp.logical_not(away))
        def _():
            pack_in[...] = pack_out[...]

    held = pack_in if folded else pack_out
    for k, ref in enumerate([u_s] * 3 + [v_s] * 3 + [m_s]):
        at = k * 32 if k < 3 else SPEED_AT + (k - 3) * 32
        packed = held[at : at + 32, :]
        turned = pltpu.roll(packed, 64, axis=1)
        low, high = jnp.where(half, packed, turned), jnp.where(half, turned, packed)
        for a in range(4):
            at = block_at(k % 3, a) if k < 6 else a * 16
            ref[at : at + 16, :] = (low if a < 2 else high)[a % 2 * 16 : a % 2 * 16 + 16]
    u_s[MAIN : MAIN + 16, :] = jnp.zeros((16, 128), f32)
    f_s[MAIN : MAIN + 16, :] = jnp.zeros((16, 128), f32)
    edge_s[...] = jnp.zeros((64, 128), f32)
    elem_s[...] = held[PARAMS_AT : PARAMS_AT + 8, :]
    slot_low = elem_s[0:1, :]
    name_row = [held[NAMES_AT + k : NAMES_AT + k + 1, :] for k in range(8)]
    slot_high = name_row[7] - owned

    tile_s[0:8, :] = held[NAMES_AT : NAMES_AT + 8, :]
    columns = jnp.transpose(tile_s[...])
    name_col = [columns[:, k : k + 1] for k in range(8)]
    to_y, to_z = same(name_col[0], name_row[1]), same(name_col[2], name_row[3])
    to_edge = same(name_col[4], name_row[5])
    spread = jnp.concatenate([to_y, to_z], axis=1)
    spread = jnp.concatenate([spread, spread], axis=0)
    spread_edge = jnp.concatenate([to_edge, to_edge], axis=0)
    collect = jnp.concatenate(
        [same(name_col[1], name_row[0]), same(name_col[3], name_row[2])], axis=1
    )
    collect_edge = same(name_col[5], name_row[4])
    to_high = same(name_col[6], name_row[7])
    to_low = same(name_col[7], name_row[6])

    low_copy.wait()
    name_copy.wait()
    tile_s[0:8, :] = low_in[64:72, :]
    tile_s[8:16, :] = name_in[...]
    columns = jnp.transpose(tile_s[...])
    from_after = same(columns[:, 0:1], slot_high)
    from_before = same(columns[:, 8:9], slot_low)
    to_high_twice = jnp.concatenate([to_high, to_high], axis=0)
    from_after_twice = jnp.concatenate([from_after, from_after], axis=0)
    theirs = []
    for k in range(7):
        packed = low_in[k // 2 * 16 : k // 2 * 16 + 16, :]
        turned = pltpu.roll(packed, 64, axis=1)
        theirs.append(jnp.where(half16 if k % 2 == 0 else jnp.logical_not(half16), packed, turned))
    ours = jnp.concatenate([u_s[0:48, :], v_s[0:48, :], m_s[0:16, :]], axis=0)
    high = moved(split_three(ours), to_high_twice)
    high = high + moved(split_three(jnp.concatenate(theirs, axis=0)), from_after_twice)
    u_s[48:96, :] = high[0:48]
    v_s[48:96, :] = high[48:96]
    m_s[64:80, :] = high[96:112]
    loads[8].wait()

    level = elem_s[1:2, :]
    period = jnp.where(level == 0.0, 8, jnp.where(level == 1.0, 4, jnp.where(level == 2.0, 2, 1)))
    row8 = sublanes((15, 8, 128))
    row16 = sublanes((16, 128))
    in_first = (row16 == 0) | (row16 == 3) | ((row16 >= 6) & (row16 < 9))
    in_second = (row16 == 1) | (row16 == 4) | ((row16 >= 9) & (row16 < 12))
    half24 = lanes((24, 128)) < 64

    def face_of(along_y, along_z):
        row = row8[0 : along_y.shape[0]]
        turned = pltpu.roll(along_z, 7, axis=1)
        return jnp.where(row < 4, along_y, jnp.where(row < 7, along_z, turned))

    def passed_on(matrix):
        onward = jnp.concatenate([to_y, to_z, to_edge], axis=1)
        return jnp.concatenate([matrix, (0.5 * moved(matrix, onward)).astype(bf16)], axis=1)

    onto_low, onto_high = passed_on(from_before), passed_on(from_after)

    def thrice(x):
        return jnp.concatenate([x, x, x], axis=0)

    for k, at in enumerate((0, 64)):
        block = m_s[at : at + 16, :]
        top = split_three(block[0:8])
        faces = moved(top, spread)
        face = face_of(faces[:, 0:128].reshape(1, 8, 128), faces[:, 128:256].reshape(1, 8, 128))
        edge = moved(top, spread_edge)
        rate_s[k * 48 : k * 48 + 48, :] = -substep_length * thrice(block)
        rate_s[96 + k * 24 : 120 + k * 24, :] = -substep_length * thrice(face.reshape(8, 128))
        rate_s[144 + k * 24 : 168 + k * 24, :] = -substep_length * thrice(edge)

    def advance(first, size, mass, force):
        rows = pl.ds(first, size)
        speed = v_s[rows, :] - substep_length * mass * force
        v_s[rows, :] = speed
        u_s[rows, :] = u_s[rows, :] + substep_length * speed

    def summed(force, planes, first):
        force = force + pltpu.roll(force, 64, axis=1)
        main, faces = planes * 16, planes * 24
        moved_face = moved(split_two(force[main:faces]), collect)
        along_y = moved_face[:, 0:128].reshape(planes, 8, 128)
        along_z = moved_face[:, 128:256].reshape(planes, 8, 128)
        row = row8[0:planes]
        low = jnp.where(row < 4, along_y, jnp.where(row < 7, along_z, 0.0))
        low = low + jnp.where(row == 0, pltpu.roll(along_z, 1, axis=1), 0.0)
        both = force[0:main].reshape(planes, 2, 8, 128)
        both = jnp.concatenate([both[:, 0:1] + low[:, None], both[:, 1:2]], axis=1)
        f_s[first : first + main, :] = both.reshape(main, 128)
        edge = moved(split_two(force[faces:]), collect_edge)[0:planes]
        at = pl.ds(first, planes, stride=16)
        f_s[at, :] = f_s[at, :] + edge

    def unpacked(packed):
        turned = pltpu.roll(packed, 64, axis=1)
        return jnp.concatenate(
            [jnp.where(half24, packed, turned), jnp.where(half24, turned, packed)], axis=0
        )

    def weights(s):
        active = lax.rem(jnp.full((1, 128), s, jnp.int32), period) == 0
        weight = jnp.where(active, period.astype(f32), 0.0)
        return elem_s[2:3, :] * weight, elem_s[3:4, :] * weight

    def exchange(s):
        return [
            pltpu.make_async_remote_copy(
                src_ref=send_buf.at[s, way], dst_ref=recv_buf.at[s, way],
                send_sem=step_send.at[s, way], recv_sem=step_recv.at[s, way],
                device_id=other, device_id_type=MESH,
            )
            for way, other in enumerate((before_id, after_id))
        ]

    def worked(first, size, columns, x_ref):
        rows = slice(2 * first, 2 * (first + size))
        product = jnp.dot(oper_ref[rows, columns], x_ref[...], preferred_element_type=f32)
        return product[0:size] + product[size:]

    def know(s):
        u = u_s[0:MAIN, :].reshape(15, 16, 128)
        faces = moved(split_three(u[:, 0:8].reshape(FACE, 128)), spread)
        face = face_of(faces[:, 0:128].reshape(15, 8, 128), faces[:, 128:256].reshape(15, 8, 128))
        edge = moved(split_three(u_s[pl.ds(0, 16, stride=16), :]), spread_edge)
        centres = []
        for c in range(3):
            at = block_at(c, 2) + CENTRE
            centres.append(u_s[at : at + 1, :])
        edge = edge - jnp.where(in_first, centres[0], jnp.where(in_second, centres[1], centres[2]))
        edge = jnp.where(row16 < 15, edge, 0.0)
        main = [u[k] - centres[c] for k, (c, _) in enumerate(PLANES)]
        face = [face[k] - centres[c] for k, (c, _) in enumerate(PLANES)]
        values = jnp.concatenate(main + face + [edge, jnp.zeros((8, 128), f32)], axis=0)
        for k, weight in enumerate(weights(s)):
            x_s[k * TOTAL : (k + 1) * TOTAL, :] = split_two(values * weight)
        value_s[...] = values
        known_s[...] = worked(0, OUTER, slice(0, 2 * TOTAL), x_s)

    def arrived(s):
        for copy in exchange(s)[::-1]:
            copy.wait()
        both = [
            moved(split_two(unpacked(recv_buf[s, way])), matrix)
            for way, matrix in ((1, onto_low), (0, onto_high))
        ]
        main = jnp.concatenate([x[:, 0:128] for x in both], axis=0) * rate_s[0:96, :]
        v_s[0:96, :] = v_s[0:96, :] + main
        main = substep_length * main
        u_s[0:96, :] = u_s[0:96, :] + main
        tops = [
            jnp.concatenate(
                [x[:, k * 128 : k * 128 + 128].reshape(3, 16, 128)[:, 0:8] for x in both], axis=0
            )
            for k in (1, 2, 3)
        ]
        rest = jnp.concatenate(
            [face_of(tops[0], tops[1]).reshape(48, 128), tops[2].reshape(48, 128)], axis=0
        )
        return jnp.concatenate([main, substep_length * rest * rate_s[96:192, :]], axis=0)

    def substep(s, follow):
        if follow:
            change = arrived(s - 1)
            for k, weight in enumerate(weights(s)):
                change_s[k * DELTA : (k + 1) * DELTA, :] = split_two(change * weight)
        force = known_s[...]
        if follow:
            force = force + worked(0, OUTER, slice(2 * TOTAL, 2 * TOTAL + 2 * DELTA), change_s)
        summed(force, SHARED, 0)
        low_x, high_x = f_s[0:48, :], f_s[48:96, :]
        send_buf[s, 0] = jnp.where(half24, low_x[0:24], low_x[24:48])
        send_buf[s, 1] = jnp.where(half24, high_x[0:24], high_x[24:48])
        for copy in exchange(s)[::-1]:
            copy.start()
        if follow:
            edge_s[0:48, :] = change[144:192]
            edge = jnp.where(row16[0:8] < SHARED, edge_s[pl.ds(0, 8, stride=8), :], 0.0)
            none = jnp.zeros((8, 128), f32)
            last = jnp.concatenate([none, edge, none, none], axis=0)
            for at, part in ((0, change[0:96]), (MAIN, change[96:144]), (TOTAL - 32, last)):
                size = part.shape[0]
                full = value_s[at : at + size, :] + part
                for k, weight in enumerate(weights(s)):
                    x_s[k * TOTAL + at : k * TOTAL + at + size, :] = split_two(full * weight)
        summed(worked(OUTER, INNER, slice(0, 2 * TOTAL), x_s), 15 - SHARED, 96)
        low_sum = low_x + moved(split_two(high_x), to_low)
        high_sum = high_x + moved(split_two(low_x), to_high)
        advance(96, 144, thrice(m_s[16:64, :]), f_s[96:240, :])
        advance(0, 48, thrice(m_s[0:16, :]), low_sum)
        advance(48, 48, thrice(m_s[64:80, :]), high_sum)

    def follow_on(s, carry):
        substep(s, True)
        know(s + 1)
        return carry

    know(0)
    substep(0, False)
    know(1)
    lax.fori_loop(1, substeps - 1, follow_on, 0)
    substep(substeps - 1, True)

    def back(part):
        rows = slice(part * 96, part * 96 + 96)
        return bulk(back_out.at[rows], back_in.at[rows], 2 + part, home_id)

    for part, a in enumerate((1, 0)):
        if part == 1:
            arrived(substeps - 1)
        for k in range(6):
            ref, at = (u_s if k < 3 else v_s), part * 96 + k * 16
            one, two = block_at(k % 3, a), block_at(k % 3, a + 2)
            back_out[at : at + 16, :] = jnp.where(
                half16, ref[one : one + 16, :], ref[two : two + 16, :]
            )
        if folded:

            @pl.when(away)
            def _():
                back(part).start()

    if folded:

        @pl.when(away)
        def _():
            for part in range(2):
                back(part).wait()
            final_ref[...] = back_in[...]

        @pl.when(jnp.logical_not(away))
        def _():
            final_ref[...] = back_out[...]
    else:
        final_ref[...] = back_out[...]


def reorder(final_ref, place_ref, out_u_ref, out_v_ref):
    place_lane, place_row = place_ref[0:32, :], place_ref[32:64, :]

    def scatter_step(t, kept):
        here = place_row == t
        first = jnp.where(t < 16, t + 96, t - 16)
        new = []
        for k in range(6):
            row = final_ref[pl.ds(k * 16 + first, 1), :]
            got = jnp.take_along_axis(
                jnp.broadcast_to(row, (32, 128)), place_lane, axis=1, mode="promise_in_bounds"
            )
            new.append(jnp.where(here, got, kept[k]))
        return tuple(new)

    done = lax.fori_loop(
        0, 32, scatter_step, tuple(jnp.zeros((32, 128), f32) for _ in range(6)), unroll=32
    )
    for k in range(6):
        ref = out_u_ref if k < 3 else out_v_ref
        for t in range(32):
            ref[k % 3 : k % 3 + 1, t * 128 : t * 128 + 128] = done[k][t : t + 1]


def per_device(
    displacement, velocity, inverse_mass, levels, first_lame, shear_modulus, connectivity, owner_list
):
    operator = jnp.asarray(element_operator())
    nodes = displacement.shape[1]
    vmem = pl.BlockSpec(memory_space=pltpu.VMEM)
    hbm = pl.BlockSpec(memory_space=pltpu.HBM)
    shape = jax.ShapeDtypeStruct((3, nodes), f32)
    V, S = pltpu.VMEM, pltpu.SemaphoreType.DMA
    operands = (
        displacement, velocity, inverse_mass.reshape(32, 128),
        levels.reshape(1, 64), first_lame.reshape(1, 64), shear_modulus.reshape(1, 64),
        connectivity.T, owner_list.reshape(4, 128), operator,
    )
    folded = lax.axis_size("dom") == 8 and lax.axis_size("lvl") == 4
    held = (jax.ShapeDtypeStruct((192, 128), f32), jax.ShapeDtypeStruct((64, 128), jnp.int32))
    final, place = pl.pallas_call(
        functools.partial(kernel, folded),
        out_shape=held,
        in_specs=[hbm] * 9,
        out_specs=(vmem, vmem),
        scratch_shapes=[V(x.shape, x.dtype) for x in operands] + [S((9,))] + [
            V((128, 128), f32), V((128, 128), f32), V((32, 128), jnp.int32),
            V((64, 4096), bf16), V((128, 4096), bf16),
            V((256, 128), f32), V((256, 128), f32), V((80, 128), f32), V((256, 128), f32),
            V((2 * TOTAL, 128), bf16), V((8, 128), f32),
            V((OUTER, 128), f32), V((2 * DELTA, 128), bf16), V((DELTA, 128), f32),
            V((TOTAL, 128), f32), V((64, 128), f32),
            V((ROWS, 128), f32), V((ROWS, 128), f32), V((192, 128), f32), V((192, 128), f32),
            V((72, 128), f32), V((72, 128), f32), V((8, 128), f32), V((8, 128), f32),
            V((substeps, 2, 24, 128), f32), V((substeps, 2, 24, 128), f32),
            S((2,)), S((2,)), S((substeps, 2)), S((substeps, 2)), S((4,)), S((4,)),
        ],
        compiler_params=pltpu.CompilerParams(
            collective_id=0, has_side_effects=True, vmem_limit_bytes=63 * 1024 * 1024
        ),
    )(*operands)
    return pl.pallas_call(
        reorder,
        out_shape=(shape, shape),
        in_specs=[vmem] * 2,
        out_specs=(vmem, vmem),
        compiler_params=pltpu.CompilerParams(vmem_limit_bytes=63 * 1024 * 1024),
    )(final, place)


def solution(mesh):
    in_specs = (
        P(None, ("dom", "lvl")),
        P(None, ("dom", "lvl")),
        P(("dom", "lvl")),
        P(("dom", "lvl")),
        P(("dom", "lvl")),
        P(("dom", "lvl")),
        P(None, ("dom", "lvl")),
        P(("dom", "lvl")),
    )
    out_specs = (P(None, ("dom", "lvl")), P(None, ("dom", "lvl")))
    return jax.shard_map(
        per_device, mesh=mesh, in_specs=in_specs, out_specs=out_specs, check_vma=False
    )
```

```python
import functools

import jax
import jax.numpy as jnp
import numpy as np
from jax import lax
from jax.experimental import pallas as pl
from jax.experimental.pallas import tpu as pltpu
from jax.sharding import PartitionSpec as P

substep_length = 0.01
substeps = 8
MESH = pl.DeviceIdType.MESH
f32 = jnp.float32
bf16 = jnp.bfloat16

BLOCK = (
    [(0, 0), (0, 1), (0, 2), (0, 3), (1, 0), (2, 0), (3, 0)]
    + [(b, c) for b in (1, 2, 3) for c in (1, 2, 3)]
)
CENTRE = BLOCK.index((2, 2))
HIGH = [(4, 0), (4, 1), (4, 2), (4, 3), (1, 4), (2, 4), (3, 4), (0, 4)]
PLANES = [(c, a) for a in (0, 4) for c in range(3)] + [(c, a) for c in range(3) for a in (1, 2, 3)]
MAIN, FACE, TOTAL = 240, 120, 384
SHARED, OUTER, INNER, DELTA = 6, 192, 288, 192


def lobatto_tables():
    points = np.array([-1.0, -np.sqrt(3.0 / 7.0), 0.0, np.sqrt(3.0 / 7.0), 1.0])
    weights = np.array([0.1, 49.0 / 90.0, 32.0 / 45.0, 49.0 / 90.0, 0.1])
    factor = np.array(
        [np.prod([points[i] - points[k] for k in range(5) if k != i]) for i in range(5)]
    )
    matrix = np.zeros((5, 5))
    for i in range(5):
        for j in range(5):
            if i == j:
                matrix[i, j] = sum((1.0 / (points[i] - points[k]) for k in range(5) if k != i))
            else:
                matrix[i, j] = factor[i] / (factor[j] * (points[i] - points[j]))
    cube = weights[:, None, None] * weights[None, :, None] * weights[None, None, :]
    return matrix, cube


def element_operator():
    derivative, cube = lobatto_tables()
    one = np.eye(5)
    along = [
        np.kron(np.kron(derivative, one), one),
        np.kron(np.kron(one, derivative), one),
        np.kron(np.kron(one, one), derivative),
    ]
    weight = cube.reshape(125)
    lame = np.zeros((3, 125, 3, 125))
    shear = np.zeros((3, 125, 3, 125))
    for c in range(3):
        for a in range(3):
            lame[c, :, a, :] += along[c].T @ (weight[:, None] * along[a])
            shear[c, :, c, :] += along[a].T @ (weight[:, None] * along[a])
            shear[c, :, a, :] += along[a].T @ (weight[:, None] * along[c])

    def ordered(planes):
        rows = [c * 125 + a * 25 + b * 5 + k for c, a in planes for b, k in BLOCK]
        rows += [c * 125 + a * 25 + b * 5 + k for c, a in planes for b, k in HIGH]
        return np.array(rows + [c * 125 + a * 25 + 24 for c, a in planes])

    taken = ordered(PLANES)
    shared = ordered(PLANES[:SHARED])
    def spots(count):
        return np.concatenate([np.arange(count * 24), count * 24 + 8 * np.arange(count)])

    parts = []
    for planes, size in ((PLANES[:SHARED], OUTER), (PLANES[SHARED:], INNER)):
        given = ordered(planes)
        into = spots(len(planes))
        part = np.zeros((size, 2 * TOTAL + 2 * DELTA))
        for k, table in enumerate((lame.reshape(375, 375), shear.reshape(375, 375))):
            part[np.ix_(into, k * TOTAL + np.arange(len(taken)))] = table[np.ix_(given, taken)]
            at = 2 * TOTAL + k * DELTA
            part[np.ix_(into, at + spots(SHARED))] = table[np.ix_(given, shared)]
        high = part.astype(jnp.bfloat16)
        parts += [high, (part - high.astype(np.float64)).astype(jnp.bfloat16)]
    return np.concatenate(parts, axis=0)


def block_at(c, a):
    return PLANES.index((c, a)) * 16


def node_row(a, b, c):
    return a * 25 + b * 5 + c


NAMES = [
    node_row(2, 0, 2), node_row(2, 4, 2),
    node_row(2, 2, 0), node_row(2, 2, 4),
    node_row(2, 0, 0), node_row(2, 4, 4),
    node_row(0, 2, 2), node_row(4, 2, 2),
]


def lanes(shape):
    return lax.broadcasted_iota(jnp.int32, shape, len(shape) - 1)


def sublanes(shape):
    return lax.broadcasted_iota(jnp.int32, shape, len(shape) - 2)


def split_two(x):
    high = x.astype(bf16).astype(f32)
    return jnp.where(lanes(x.shape) < 64, high, x - high).astype(bf16)


def split_three(x):
    high = x.astype(bf16).astype(f32)
    rest = x - high
    middle = rest.astype(bf16).astype(f32)
    first = jnp.where(lanes(x.shape) < 64, high, middle).astype(bf16)
    second = jnp.where(lanes(x.shape) < 64, rest - middle, 0.0).astype(bf16)
    return jnp.concatenate([first, second], axis=1)


def moved(parts, matrix):
    return jnp.dot(parts, matrix, preferred_element_type=f32)


def same(column, row):
    return jnp.where(column == row, 1.0, 0.0).astype(bf16)


FOLDED = [5, 1, 3, 2, 0, 4, 6, 7, 11, 10, 14, 15, 13, 12, 8, 9]
NAMES_AT, PARAMS_AT, SPEED_AT, MASS_AT, ROWS = 96, 104, 112, 208, 240


def looked_up(index, table):
    found = jnp.int32(table[0])
    for k, value in enumerate(table[1:], 1):
        found = jnp.where(index == k, jnp.int32(value), found)
    return found


def kernel(
    folded, disp_hbm, vel_hbm, mass_hbm, level_hbm, lame_hbm, shear_hbm, conn_hbm, owner_hbm, oper_hbm,
    final_ref, place_ref,
    disp_ref, vel_ref, mass_ref, level_ref, lame_ref, shear_ref, conn_ref, owner_ref, oper_ref, load_sem,
    conn_s, tile_s, pick_s, hot_hi, hot_lo, u_s, v_s, m_s, x_s, elem_s, known_s, change_s, rate_s, value_s, edge_s,
    pack_out, pack_in, back_out, back_in,
    low_out, low_in, name_out, name_in, send_buf, recv_buf,
    init_send, init_recv, step_send, step_recv, bulk_send, bulk_recv,
):
    dom_size, lvl_size = lax.axis_size("dom"), lax.axis_size("lvl")
    count = dom_size * lvl_size
    me = lax.axis_index("dom") * lvl_size + lax.axis_index("lvl")

    loads = [
        pltpu.make_async_copy(src, dst, load_sem.at[k])
        for k, (src, dst) in enumerate([
            (conn_hbm, conn_ref), (disp_hbm, disp_ref), (vel_hbm, vel_ref), (mass_hbm, mass_ref),
            (owner_hbm, owner_ref), (level_hbm, level_ref), (lame_hbm, lame_ref),
            (shear_hbm, shear_ref), (oper_hbm, oper_ref),
        ])
    ]
    for load in loads:
        load.start()

    def device(index):
        return (index // lvl_size, lax.rem(index, lvl_size))

    def step(index, distance):
        return lax.rem(index + count + distance, count)

    if folded:
        order = [FOLDED.index(k) for k in range(count // 2)]

        def host_of(index):
            return looked_up(index // 2, FOLDED) * 2 + lax.rem(index, 2)

        home = looked_up(me // 2, order) * 2 + lax.rem(me, 2)
        host = host_of(me)
        away = host != me
        after, before = host_of(step(home, 1)), host_of(step(home, -1))
        low_to, name_to = host_of(step(me, -1)), host_of(step(me, 1))
        peers = [after, before, low_to, name_to, step(home, 1), step(home, -1)]
        host_id, home_id = device(host), device(home)
    else:
        after, before = step(me, 1), step(me, -1)
        low_to, name_to = before, after
        peers = [after, before]
    after_id, before_id = device(after), device(before)

    barrier = pltpu.get_barrier_semaphore()
    for other in peers:
        pl.semaphore_signal(barrier, inc=1, device_id=device(other), device_id_type=MESH)
    if folded:

        @pl.when(away)
        def _():
            for other in (host_id, home_id):
                pl.semaphore_signal(barrier, inc=1, device_id=other, device_id_type=MESH)

    def bulk(src, dst, k, other):
        return pltpu.make_async_remote_copy(
            src_ref=src, dst_ref=dst, send_sem=bulk_send.at[k], recv_sem=bulk_recv.at[k],
            device_id=other, device_id_type=MESH,
        )

    loads[0].wait()
    tile_s[...] = jnp.zeros((128, 128), f32)
    for k in range(2):
        tile_s[k * 64 : k * 64 + 64, 0:125] = conn_ref[...].astype(f32)
    conn_s[...] = jnp.transpose(tile_s[...])

    low_half = lanes((1, 128)) < 64
    for a in range(2):
        for j, (b, c) in enumerate(BLOCK):
            r0, r1 = node_row(a, b, c), node_row(a + 2, b, c)
            pick_s[a * 16 + j : a * 16 + j + 1, :] = jnp.where(
                low_half, conn_s[r0 : r0 + 1, :], conn_s[r1 : r1 + 1, :]
            ).astype(jnp.int32)
    pick = pick_s[...]
    pick_hi, pick_lo = lax.shift_right_logical(pick, 7), lax.bitwise_and(pick, 127)

    def gathered(refs, singles):
        def gather_step(t, kept):
            here = pick_hi == t
            cols = pl.ds(pl.multiple_of(t * 128, 128), 128)
            rows = [ref[c : c + 1, cols] for ref in refs for c in range(3)]
            rows += [ref[pl.ds(t, 1), :] for ref in singles]
            new = []
            for row, old in zip(rows, kept):
                got = jnp.take_along_axis(
                    jnp.broadcast_to(row, (32, 128)), pick_lo, axis=1, mode="promise_in_bounds"
                )
                new.append(jnp.where(here, got, old))
            return tuple(new)

        start = tuple(jnp.zeros((32, 128), f32) for _ in range(3 * len(refs) + len(singles)))
        return list(lax.fori_loop(0, 32, gather_step, start, unroll=32))

    for load in loads[1:8]:
        load.wait()
    got = gathered([disp_ref], [])
    half = lanes((32, 128)) < 64
    for k in range(3):
        pack_out[k * 32 : k * 32 + 32, :] = got[k]

    for k, r in enumerate(NAMES):
        pack_out[NAMES_AT + k : NAMES_AT + k + 1, :] = conn_s[r : r + 1, :]
    tile_s[0:8, :] = jnp.zeros((8, 128), f32)
    tile_s[0:4, :] = owner_ref[...].astype(f32)
    columns = jnp.transpose(tile_s[...])
    low_name = conn_s[NAMES[6] : NAMES[6] + 1, :]
    slot_low = jnp.full((1, 128), -9999.0, f32)
    for k in range(4):
        hit = columns[:, k : k + 1] == low_name
        number = sublanes((128, 128)).astype(f32) + (k * 128 + 9999)
        slot_low = slot_low + jnp.sum(jnp.where(hit, number, 0.0), axis=0, keepdims=True)
    pack_out[PARAMS_AT : PARAMS_AT + 8, :] = jnp.zeros((8, 128), f32)
    pack_out[PARAMS_AT : PARAMS_AT + 1, :] = slot_low
    for k, ref in enumerate((level_ref, lame_ref, shear_ref), 1):
        for at in (0, 64):
            pack_out[PARAMS_AT + k : PARAMS_AT + k + 1, at : at + 64] = ref[...].astype(f32)

    def first_move():
        return bulk(pack_out.at[0:SPEED_AT], pack_in.at[0:SPEED_AT], 0, host_id)

    def second_move():
        return bulk(pack_out.at[SPEED_AT:ROWS], pack_in.at[SPEED_AT:ROWS], 1, host_id)

    if folded:

        @pl.when(away)
        def _():
            pl.semaphore_wait(barrier, 8)
            first_move().start()

        @pl.when(jnp.logical_not(away))
        def _():
            pl.semaphore_wait(barrier, 6)
    else:
        pl.semaphore_wait(barrier, 2)
    got = got + gathered([vel_ref], [mass_ref])
    for k in range(3, 7):
        at = SPEED_AT + (k - 3) * 32
        pack_out[at : at + 32, :] = got[k]
    if folded:

        @pl.when(away)
        def _():
            second_move().start()

    half16 = lanes((16, 128)) < 64
    for k in range(4):
        other = got[min(2 * k + 1, 6)][0:16]
        low_out[k * 16 : k * 16 + 16, :] = jnp.where(
            half16, got[2 * k][0:16], pltpu.roll(other, 64, axis=1)
        )
    low_out[64:72, :] = jnp.broadcast_to(slot_low, (8, 128))
    owned = float(disp_ref.shape[1])
    name_out[...] = jnp.broadcast_to(conn_s[NAMES[7] : NAMES[7] + 1, :] - owned, (8, 128))
    low_copy = pltpu.make_async_remote_copy(
        src_ref=low_out, dst_ref=low_in, send_sem=init_send.at[0], recv_sem=init_recv.at[0],
        device_id=device(low_to), device_id_type=MESH,
    )
    name_copy = pltpu.make_async_remote_copy(
        src_ref=name_out, dst_ref=name_in, send_sem=init_send.at[1], recv_sem=init_recv.at[1],
        device_id=device(name_to), device_id_type=MESH,
    )
    low_copy.start()
    name_copy.start()

    def find_places():
        for r in range(32):
            cols = slice(r * 128, r * 128 + 128)
            hit = pick_hi[r : r + 1, :] == sublanes((32, 128))
            hot_hi[0:32, cols] = jnp.where(hit, lanes((32, 128)).astype(f32), 0.0).astype(bf16)
            hot_hi[32:64, cols] = jnp.where(hit, float(r), 0.0).astype(bf16)
            hot_lo[:, cols] = same(sublanes((128, 128)), pick_lo[r : r + 1, :])
        place = lax.dot_general(
            hot_hi[...], hot_lo[...], (((1,), (1,)), ((), ())), preferred_element_type=f32
        )
        return place[0:32].astype(jnp.int32), place[32:64].astype(jnp.int32)

    place_lane, place_row = find_places()
    place_ref[0:32, :] = place_lane
    place_ref[32:64, :] = place_row
    if folded:

        @pl.when(away)
        def _():
            first_move().wait()
            second_move().wait()

        @pl.when(jnp.logical_not(away))
        def _():
            pack_in[...] = pack_out[...]

    held = pack_in if folded else pack_out
    for k, ref in enumerate([u_s] * 3 + [v_s] * 3 + [m_s]):
        at = k * 32 if k < 3 else SPEED_AT + (k - 3) * 32
        packed = held[at : at + 32, :]
        turned = pltpu.roll(packed, 64, axis=1)
        low, high = jnp.where(half, packed, turned), jnp.where(half, turned, packed)
        for a in range(4):
            at = block_at(k % 3, a) if k < 6 else a * 16
            ref[at : at + 16, :] = (low if a < 2 else high)[a % 2 * 16 : a % 2 * 16 + 16]
    u_s[MAIN : MAIN + 16, :] = jnp.zeros((16, 128), f32)
    edge_s[...] = jnp.zeros((64, 128), f32)
    elem_s[...] = held[PARAMS_AT : PARAMS_AT + 8, :]
    slot_low = elem_s[0:1, :]
    name_row = [held[NAMES_AT + k : NAMES_AT + k + 1, :] for k in range(8)]
    slot_high = name_row[7] - owned

    tile_s[0:8, :] = held[NAMES_AT : NAMES_AT + 8, :]
    columns = jnp.transpose(tile_s[...])
    name_col = [columns[:, k : k + 1] for k in range(8)]
    to_y, to_z = same(name_col[0], name_row[1]), same(name_col[2], name_row[3])
    to_edge = same(name_col[4], name_row[5])
    spread = jnp.concatenate([to_y, to_z], axis=1)
    spread = jnp.concatenate([spread, spread], axis=0)
    spread_edge = jnp.concatenate([to_edge, to_edge], axis=0)
    collect = jnp.concatenate(
        [same(name_col[1], name_row[0]), same(name_col[3], name_row[2]), same(name_col[5], name_row[4])],
        axis=1,
    )
    collect = jnp.concatenate([collect, collect], axis=0)
    to_high = same(name_col[6], name_row[7])
    to_low = same(name_col[7], name_row[6])

    low_copy.wait()
    name_copy.wait()
    tile_s[0:8, :] = low_in[64:72, :]
    tile_s[8:16, :] = name_in[...]
    columns = jnp.transpose(tile_s[...])
    from_after = same(columns[:, 0:1], slot_high)
    from_before = same(columns[:, 8:9], slot_low)
    to_high_twice = jnp.concatenate([to_high, to_high], axis=0)
    from_after_twice = jnp.concatenate([from_after, from_after], axis=0)
    theirs = []
    for k in range(7):
        packed = low_in[k // 2 * 16 : k // 2 * 16 + 16, :]
        turned = pltpu.roll(packed, 64, axis=1)
        theirs.append(jnp.where(half16 if k % 2 == 0 else jnp.logical_not(half16), packed, turned))
    ours = jnp.concatenate([u_s[0:48, :], v_s[0:48, :], m_s[0:16, :]], axis=0)
    high = moved(split_three(ours), to_high_twice)
    high = high + moved(split_three(jnp.concatenate(theirs, axis=0)), from_after_twice)
    u_s[48:96, :] = high[0:48]
    v_s[48:96, :] = high[48:96]
    m_s[64:80, :] = high[96:112]
    loads[8].wait()

    level = elem_s[1:2, :]
    period = jnp.where(level == 0.0, 8, jnp.where(level == 1.0, 4, jnp.where(level == 2.0, 2, 1)))
    row8 = sublanes((15, 8, 128))
    row16 = sublanes((16, 128))
    in_first = (row16 == 0) | (row16 == 3) | ((row16 >= 6) & (row16 < 9))
    in_second = (row16 == 1) | (row16 == 4) | ((row16 >= 9) & (row16 < 12))
    half24 = lanes((24, 128)) < 64

    def face_of(along_y, along_z):
        row = row8[0 : along_y.shape[0]]
        turned = pltpu.roll(along_z, 7, axis=1)
        return jnp.where(row < 4, along_y, jnp.where(row < 7, along_z, turned))

    def passed_on(matrix):
        onward = jnp.concatenate([to_y, to_z, to_edge], axis=1)
        return jnp.concatenate([matrix, (0.5 * moved(matrix, onward)).astype(bf16)], axis=1)

    onto_low, onto_high = passed_on(from_before), passed_on(from_after)

    def thrice(x):
        return jnp.concatenate([x, x, x], axis=0)

    for k, at in enumerate((0, 64)):
        block = m_s[at : at + 16, :]
        top = split_three(block[0:8])
        faces = moved(top, spread)
        face = face_of(faces[:, 0:128].reshape(1, 8, 128), faces[:, 128:256].reshape(1, 8, 128))
        edge = moved(top, spread_edge)
        rate_s[k * 48 : k * 48 + 48, :] = -substep_length * thrice(block)
        rate_s[96 + k * 24 : 120 + k * 24, :] = -substep_length * thrice(face.reshape(8, 128))
        rate_s[144 + k * 24 : 168 + k * 24, :] = -substep_length * thrice(edge)

    def advance(first, size, mass, force):
        rows = pl.ds(first, size)
        speed = v_s[rows, :] - substep_length * mass * force
        v_s[rows, :] = speed
        u_s[rows, :] = u_s[rows, :] + substep_length * speed

    def summed(force, planes):
        main, faces = planes * 16, planes * 24
        high = force[main:].astype(bf16)
        rest = (force[main:] - high.astype(f32)).astype(bf16)
        given = moved(jnp.concatenate([high, rest], axis=1), collect)
        along_y = given[0 : faces - main, 0:128].reshape(planes, 8, 128)
        along_z = given[0 : faces - main, 128:256].reshape(planes, 8, 128)
        edge = given[faces - main :, 256:384].reshape(planes, 8, 128)
        row = row8[0:planes]
        low = edge + jnp.where(row < 4, along_y, jnp.where(row < 7, along_z, 0.0))
        low = low + jnp.where(row == 0, pltpu.roll(along_z, 1, axis=1), 0.0)
        both = force[0:main] + pltpu.roll(force[0:main], 64, axis=1)
        both = both.reshape(planes, 2, 8, 128)
        both = jnp.concatenate([both[:, 0:1] + low[:, None], both[:, 1:2]], axis=1)
        return both.reshape(main, 128)

    def unpacked(packed):
        turned = pltpu.roll(packed, 64, axis=1)
        return jnp.concatenate(
            [jnp.where(half24, packed, turned), jnp.where(half24, turned, packed)], axis=0
        )

    def weights(s):
        active = lax.rem(jnp.full((1, 128), s, jnp.int32), period) == 0
        weight = jnp.where(active, period.astype(f32), 0.0)
        return elem_s[2:3, :] * weight, elem_s[3:4, :] * weight

    def exchange(s):
        return [
            pltpu.make_async_remote_copy(
                src_ref=send_buf.at[s, way], dst_ref=recv_buf.at[s, way],
                send_sem=step_send.at[s, way], recv_sem=step_recv.at[s, way],
                device_id=other, device_id_type=MESH,
            )
            for way, other in enumerate((before_id, after_id))
        ]

    def worked(first, size, columns, x_ref):
        rows = slice(2 * first, 2 * (first + size))
        product = jnp.dot(oper_ref[rows, columns], x_ref[...], preferred_element_type=f32)
        return product[0:size] + product[size:]

    def know(s):
        u = u_s[0:MAIN, :].reshape(15, 16, 128)
        faces = moved(split_three(u[:, 0:8].reshape(FACE, 128)), spread)
        face = face_of(faces[:, 0:128].reshape(15, 8, 128), faces[:, 128:256].reshape(15, 8, 128))
        edge = moved(split_three(u_s[pl.ds(0, 16, stride=16), :]), spread_edge)
        centres = []
        for c in range(3):
            at = block_at(c, 2) + CENTRE
            centres.append(u_s[at : at + 1, :])
        edge = edge - jnp.where(in_first, centres[0], jnp.where(in_second, centres[1], centres[2]))
        edge = jnp.where(row16 < 15, edge, 0.0)
        main = [u[k] - centres[c] for k, (c, _) in enumerate(PLANES)]
        face = [face[k] - centres[c] for k, (c, _) in enumerate(PLANES)]
        values = jnp.concatenate(main + face + [edge, jnp.zeros((8, 128), f32)], axis=0)
        for k, weight in enumerate(weights(s)):
            x_s[k * TOTAL : (k + 1) * TOTAL, :] = split_two(values * weight)
        value_s[...] = values
        known_s[...] = worked(0, OUTER, slice(0, 2 * TOTAL), x_s)

    def arrived(s):
        for copy in exchange(s)[::-1]:
            copy.wait()
        both = [
            moved(split_two(unpacked(recv_buf[s, way])), matrix)
            for way, matrix in ((1, onto_low), (0, onto_high))
        ]
        main = jnp.concatenate([x[:, 0:128] for x in both], axis=0) * rate_s[0:96, :]
        v_s[0:96, :] = v_s[0:96, :] + main
        main = substep_length * main
        u_s[0:96, :] = u_s[0:96, :] + main
        tops = [
            jnp.concatenate(
                [x[:, k * 128 : k * 128 + 128].reshape(3, 16, 128)[:, 0:8] for x in both], axis=0
            )
            for k in (1, 2, 3)
        ]
        rest = jnp.concatenate(
            [face_of(tops[0], tops[1]).reshape(48, 128), tops[2].reshape(48, 128)], axis=0
        )
        return jnp.concatenate([main, substep_length * rest * rate_s[96:192, :]], axis=0)

    def substep(s, follow):
        if follow:
            change = arrived(s - 1)
            for k, weight in enumerate(weights(s)):
                change_s[k * DELTA : (k + 1) * DELTA, :] = split_two(change * weight)
        force = known_s[...]
        if follow:
            force = force + worked(0, OUTER, slice(2 * TOTAL, 2 * TOTAL + 2 * DELTA), change_s)
        force = summed(force, SHARED)
        low_x, high_x = force[0:48], force[48:96]
        send_buf[s, 0] = jnp.where(half24, low_x[0:24], low_x[24:48])
        send_buf[s, 1] = jnp.where(half24, high_x[0:24], high_x[24:48])
        for copy in exchange(s)[::-1]:
            copy.start()
        if follow:
            edge_s[0:48, :] = change[144:192]
            edge = jnp.where(row16[0:8] < SHARED, edge_s[pl.ds(0, 8, stride=8), :], 0.0)
            none = jnp.zeros((8, 128), f32)
            last = jnp.concatenate([none, edge, none, none], axis=0)
            for at, part in ((0, change[0:96]), (MAIN, change[96:144]), (TOTAL - 32, last)):
                size = part.shape[0]
                full = value_s[at : at + size, :] + part
                for k, weight in enumerate(weights(s)):
                    x_s[k * TOTAL + at : k * TOTAL + at + size, :] = split_two(full * weight)
        inner = summed(worked(OUTER, INNER, slice(0, 2 * TOTAL), x_s), 15 - SHARED)
        low_sum = low_x + moved(split_two(high_x), to_low)
        high_sum = high_x + moved(split_two(low_x), to_high)
        advance(96, 144, thrice(m_s[16:64, :]), inner)
        advance(0, 48, thrice(m_s[0:16, :]), low_sum)
        advance(48, 48, thrice(m_s[64:80, :]), high_sum)

    def follow_on(s, carry):
        substep(s, True)
        know(s + 1)
        return carry

    know(0)
    substep(0, False)
    know(1)
    lax.fori_loop(1, substeps - 1, follow_on, 0)
    substep(substeps - 1, True)

    def back(part):
        rows = slice(part * 96, part * 96 + 96)
        return bulk(back_out.at[rows], back_in.at[rows], 2 + part, home_id)

    for part, a in enumerate((1, 0)):
        if part == 1:
            arrived(substeps - 1)
        for k in range(6):
            ref, at = (u_s if k < 3 else v_s), part * 96 + k * 16
            one, two = block_at(k % 3, a), block_at(k % 3, a + 2)
            back_out[at : at + 16, :] = jnp.where(
                half16, ref[one : one + 16, :], ref[two : two + 16, :]
            )
        if folded:

            @pl.when(away)
            def _():
                back(part).start()

    if folded:

        @pl.when(away)
        def _():
            for part in range(2):
                back(part).wait()
            final_ref[...] = back_in[...]

        @pl.when(jnp.logical_not(away))
        def _():
            final_ref[...] = back_out[...]
    else:
        final_ref[...] = back_out[...]


def reorder(final_ref, place_ref, out_u_ref, out_v_ref):
    place_lane, place_row = place_ref[0:32, :], place_ref[32:64, :]

    def scatter_step(t, kept):
        here = place_row == t
        first = jnp.where(t < 16, t + 96, t - 16)
        new = []
        for k in range(6):
            row = final_ref[pl.ds(k * 16 + first, 1), :]
            got = jnp.take_along_axis(
                jnp.broadcast_to(row, (32, 128)), place_lane, axis=1, mode="promise_in_bounds"
            )
            new.append(jnp.where(here, got, kept[k]))
        return tuple(new)

    done = lax.fori_loop(
        0, 32, scatter_step, tuple(jnp.zeros((32, 128), f32) for _ in range(6)), unroll=32
    )
    for k in range(6):
        ref = out_u_ref if k < 3 else out_v_ref
        for t in range(32):
            ref[k % 3 : k % 3 + 1, t * 128 : t * 128 + 128] = done[k][t : t + 1]


def per_device(
    displacement, velocity, inverse_mass, levels, first_lame, shear_modulus, connectivity, owner_list
):
    operator = jnp.asarray(element_operator())
    nodes = displacement.shape[1]
    vmem = pl.BlockSpec(memory_space=pltpu.VMEM)
    hbm = pl.BlockSpec(memory_space=pltpu.HBM)
    shape = jax.ShapeDtypeStruct((3, nodes), f32)
    V, S = pltpu.VMEM, pltpu.SemaphoreType.DMA
    operands = (
        displacement, velocity, inverse_mass.reshape(32, 128),
        levels.reshape(1, 64), first_lame.reshape(1, 64), shear_modulus.reshape(1, 64),
        connectivity.T, owner_list.reshape(4, 128), operator,
    )
    folded = lax.axis_size("dom") == 8 and lax.axis_size("lvl") == 4
    held = (jax.ShapeDtypeStruct((192, 128), f32), jax.ShapeDtypeStruct((64, 128), jnp.int32))
    final, place = pl.pallas_call(
        functools.partial(kernel, folded),
        out_shape=held,
        in_specs=[hbm] * 9,
        out_specs=(vmem, vmem),
        scratch_shapes=[V(x.shape, x.dtype) for x in operands] + [S((9,))] + [
            V((128, 128), f32), V((128, 128), f32), V((32, 128), jnp.int32),
            V((64, 4096), bf16), V((128, 4096), bf16),
            V((256, 128), f32), V((256, 128), f32), V((80, 128), f32),
            V((2 * TOTAL, 128), bf16), V((8, 128), f32),
            V((OUTER, 128), f32), V((2 * DELTA, 128), bf16), V((DELTA, 128), f32),
            V((TOTAL, 128), f32), V((64, 128), f32),
            V((ROWS, 128), f32), V((ROWS, 128), f32), V((192, 128), f32), V((192, 128), f32),
            V((72, 128), f32), V((72, 128), f32), V((8, 128), f32), V((8, 128), f32),
            V((substeps, 2, 24, 128), f32), V((substeps, 2, 24, 128), f32),
            S((2,)), S((2,)), S((substeps, 2)), S((substeps, 2)), S((4,)), S((4,)),
        ],
        compiler_params=pltpu.CompilerParams(
            collective_id=0, has_side_effects=True, vmem_limit_bytes=63 * 1024 * 1024
        ),
    )(*operands)
    return pl.pallas_call(
        reorder,
        out_shape=(shape, shape),
        in_specs=[vmem] * 2,
        out_specs=(vmem, vmem),
        compiler_params=pltpu.CompilerParams(vmem_limit_bytes=63 * 1024 * 1024),
    )(final, place)


def solution(mesh):
    in_specs = (
        P(None, ("dom", "lvl")),
        P(None, ("dom", "lvl")),
        P(("dom", "lvl")),
        P(("dom", "lvl")),
        P(("dom", "lvl")),
        P(("dom", "lvl")),
        P(None, ("dom", "lvl")),
        P(("dom", "lvl")),
    )
    out_specs = (P(None, ("dom", "lvl")), P(None, ("dom", "lvl")))
    return jax.shard_map(
        per_device, mesh=mesh, in_specs=in_specs, out_specs=out_specs, check_vma=False
    )
```

```python
import functools

import jax
import jax.numpy as jnp
import numpy as np
from jax import lax
from jax.experimental import pallas as pl
from jax.experimental.pallas import tpu as pltpu
from jax.sharding import PartitionSpec as P

substep_length = 0.01
substeps = 8
MESH = pl.DeviceIdType.MESH
f32 = jnp.float32
bf16 = jnp.bfloat16

BLOCK = (
    [(0, 0), (0, 1), (0, 2), (0, 3), (1, 0), (2, 0), (3, 0)]
    + [(b, c) for b in (1, 2, 3) for c in (1, 2, 3)]
)
CENTRE = BLOCK.index((2, 2))
HIGH = [(4, 0), (4, 1), (4, 2), (4, 3), (1, 4), (2, 4), (3, 4), (0, 4)]
PLANES = [(c, a) for a in (0, 4) for c in range(3)] + [(c, a) for c in range(3) for a in (1, 2, 3)]
MAIN, FACE, TOTAL = 240, 120, 384
SHARED, OUTER, INNER, DELTA = 6, 192, 288, 192


def lobatto_tables():
    points = np.array([-1.0, -np.sqrt(3.0 / 7.0), 0.0, np.sqrt(3.0 / 7.0), 1.0])
    weights = np.array([0.1, 49.0 / 90.0, 32.0 / 45.0, 49.0 / 90.0, 0.1])
    factor = np.array(
        [np.prod([points[i] - points[k] for k in range(5) if k != i]) for i in range(5)]
    )
    matrix = np.zeros((5, 5))
    for i in range(5):
        for j in range(5):
            if i == j:
                matrix[i, j] = sum((1.0 / (points[i] - points[k]) for k in range(5) if k != i))
            else:
                matrix[i, j] = factor[i] / (factor[j] * (points[i] - points[j]))
    cube = weights[:, None, None] * weights[None, :, None] * weights[None, None, :]
    return matrix, cube


def element_operator():
    derivative, cube = lobatto_tables()
    one = np.eye(5)
    along = [
        np.kron(np.kron(derivative, one), one),
        np.kron(np.kron(one, derivative), one),
        np.kron(np.kron(one, one), derivative),
    ]
    weight = cube.reshape(125)
    lame = np.zeros((3, 125, 3, 125))
    shear = np.zeros((3, 125, 3, 125))
    for c in range(3):
        for a in range(3):
            lame[c, :, a, :] += along[c].T @ (weight[:, None] * along[a])
            shear[c, :, c, :] += along[a].T @ (weight[:, None] * along[a])
            shear[c, :, a, :] += along[a].T @ (weight[:, None] * along[c])

    def ordered(planes):
        rows = [c * 125 + a * 25 + b * 5 + k for c, a in planes for b, k in BLOCK]
        rows += [c * 125 + a * 25 + b * 5 + k for c, a in planes for b, k in HIGH]
        return np.array(rows + [c * 125 + a * 25 + 24 for c, a in planes])

    taken = ordered(PLANES)
    shared = ordered(PLANES[:SHARED])
    def spots(count):
        return np.concatenate([np.arange(count * 24), count * 24 + 8 * np.arange(count)])

    parts = []
    for planes, size in ((PLANES[:SHARED], OUTER), (PLANES[SHARED:], INNER)):
        given = ordered(planes)
        into = spots(len(planes))
        part = np.zeros((size, 2 * TOTAL + 2 * DELTA))
        for k, table in enumerate((lame.reshape(375, 375), shear.reshape(375, 375))):
            part[np.ix_(into, k * TOTAL + np.arange(len(taken)))] = table[np.ix_(given, taken)]
            at = 2 * TOTAL + k * DELTA
            part[np.ix_(into, at + spots(SHARED))] = table[np.ix_(given, shared)]
        high = part.astype(jnp.bfloat16)
        parts += [high, (part - high.astype(np.float64)).astype(jnp.bfloat16)]
    return np.concatenate(parts, axis=0)


def block_at(c, a):
    return PLANES.index((c, a)) * 16


def node_row(a, b, c):
    return a * 25 + b * 5 + c


NAMES = [
    node_row(2, 0, 2), node_row(2, 4, 2),
    node_row(2, 2, 0), node_row(2, 2, 4),
    node_row(2, 0, 0), node_row(2, 4, 4),
    node_row(0, 2, 2), node_row(4, 2, 2),
]


def lanes(shape):
    return lax.broadcasted_iota(jnp.int32, shape, len(shape) - 1)


def sublanes(shape):
    return lax.broadcasted_iota(jnp.int32, shape, len(shape) - 2)


def split_two(x):
    high = x.astype(bf16).astype(f32)
    return jnp.where(lanes(x.shape) < 64, high, x - high).astype(bf16)


def split_three(x):
    high = x.astype(bf16).astype(f32)
    rest = x - high
    middle = rest.astype(bf16).astype(f32)
    first = jnp.where(lanes(x.shape) < 64, high, middle).astype(bf16)
    second = jnp.where(lanes(x.shape) < 64, rest - middle, 0.0).astype(bf16)
    return jnp.concatenate([first, second], axis=1)


def moved(parts, matrix):
    return jnp.dot(parts, matrix, preferred_element_type=f32)


def same(column, row):
    return jnp.where(column == row, 1.0, 0.0).astype(bf16)


FOLDED = [5, 1, 3, 2, 0, 4, 6, 7, 11, 10, 14, 15, 13, 12, 8, 9]
NAMES_AT, PARAMS_AT, SPEED_AT, MASS_AT, ROWS = 96, 104, 112, 208, 240


def looked_up(index, table):
    found = jnp.int32(table[0])
    for k, value in enumerate(table[1:], 1):
        found = jnp.where(index == k, jnp.int32(value), found)
    return found


def kernel(
    folded, disp_hbm, vel_hbm, mass_hbm, level_hbm, lame_hbm, shear_hbm, conn_hbm, owner_hbm, oper_hbm,
    final_ref, place_ref,
    disp_ref, vel_ref, mass_ref, level_ref, lame_ref, shear_ref, conn_ref, owner_ref, oper_ref, load_sem,
    conn_s, tile_s, pick_s, hot_hi, hot_lo, u_s, v_s, m_s, x_s, elem_s, known_s, change_s, rate_s, value_s, edge_s,
    pack_out, pack_in, back_out, back_in,
    low_out, low_in, name_out, name_in, send_buf, recv_buf,
    init_send, init_recv, step_send, step_recv, bulk_send, bulk_recv,
):
    dom_size, lvl_size = lax.axis_size("dom"), lax.axis_size("lvl")
    count = dom_size * lvl_size
    me = lax.axis_index("dom") * lvl_size + lax.axis_index("lvl")

    loads = [
        pltpu.make_async_copy(src, dst, load_sem.at[k])
        for k, (src, dst) in enumerate([
            (conn_hbm, conn_ref), (disp_hbm, disp_ref), (vel_hbm, vel_ref), (mass_hbm, mass_ref),
            (owner_hbm, owner_ref), (level_hbm, level_ref), (lame_hbm, lame_ref),
            (shear_hbm, shear_ref), (oper_hbm, oper_ref),
        ])
    ]
    for load in loads:
        load.start()

    def device(index):
        return (index // lvl_size, lax.rem(index, lvl_size))

    def step(index, distance):
        return lax.rem(index + count + distance, count)

    if folded:
        order = [FOLDED.index(k) for k in range(count // 2)]

        def host_of(index):
            return looked_up(index // 2, FOLDED) * 2 + lax.rem(index, 2)

        home = looked_up(me // 2, order) * 2 + lax.rem(me, 2)
        host = host_of(me)
        away = host != me
        after, before = host_of(step(home, 1)), host_of(step(home, -1))
        low_to, name_to = host_of(step(me, -1)), host_of(step(me, 1))
        peers = [after, before, low_to, name_to, step(home, 1), step(home, -1)]
        host_id, home_id = device(host), device(home)
    else:
        after, before = step(me, 1), step(me, -1)
        low_to, name_to = before, after
        peers = [after, before]
    after_id, before_id = device(after), device(before)

    barrier = pltpu.get_barrier_semaphore()
    for other in peers:
        pl.semaphore_signal(barrier, inc=1, device_id=device(other), device_id_type=MESH)
    if folded:

        @pl.when(away)
        def _():
            for other in (host_id, home_id):
                pl.semaphore_signal(barrier, inc=1, device_id=other, device_id_type=MESH)

    def bulk(src, dst, k, other):
        return pltpu.make_async_remote_copy(
            src_ref=src, dst_ref=dst, send_sem=bulk_send.at[k], recv_sem=bulk_recv.at[k],
            device_id=other, device_id_type=MESH,
        )

    loads[0].wait()
    tile_s[...] = jnp.zeros((128, 128), f32)
    for k in range(2):
        tile_s[k * 64 : k * 64 + 64, 0:125] = conn_ref[...].astype(f32)
    conn_s[...] = jnp.transpose(tile_s[...])

    low_half = lanes((1, 128)) < 64
    for a in range(2):
        for j, (b, c) in enumerate(BLOCK):
            r0, r1 = node_row(a, b, c), node_row(a + 2, b, c)
            pick_s[a * 16 + j : a * 16 + j + 1, :] = jnp.where(
                low_half, conn_s[r0 : r0 + 1, :], conn_s[r1 : r1 + 1, :]
            ).astype(jnp.int32)
    pick = pick_s[...]
    pick_hi, pick_lo = lax.shift_right_logical(pick, 7), lax.bitwise_and(pick, 127)

    def gathered(refs, singles):
        def gather_step(t, kept):
            here = pick_hi == t
            cols = pl.ds(pl.multiple_of(t * 128, 128), 128)
            rows = [ref[c : c + 1, cols] for ref in refs for c in range(3)]
            rows += [ref[pl.ds(t, 1), :] for ref in singles]
            new = []
            for row, old in zip(rows, kept):
                got = jnp.take_along_axis(
                    jnp.broadcast_to(row, (32, 128)), pick_lo, axis=1, mode="promise_in_bounds"
                )
                new.append(jnp.where(here, got, old))
            return tuple(new)

        start = tuple(jnp.zeros((32, 128), f32) for _ in range(3 * len(refs) + len(singles)))
        return list(lax.fori_loop(0, 32, gather_step, start, unroll=32))

    for load in loads[1:8]:
        load.wait()
    got = gathered([disp_ref], [])
    half = lanes((32, 128)) < 64
    for k in range(3):
        pack_out[k * 32 : k * 32 + 32, :] = got[k]

    for k, r in enumerate(NAMES):
        pack_out[NAMES_AT + k : NAMES_AT + k + 1, :] = conn_s[r : r + 1, :]
    tile_s[0:8, :] = jnp.zeros((8, 128), f32)
    tile_s[0:4, :] = owner_ref[...].astype(f32)
    columns = jnp.transpose(tile_s[...])
    low_name = conn_s[NAMES[6] : NAMES[6] + 1, :]
    slot_low = jnp.full((1, 128), -9999.0, f32)
    for k in range(4):
        hit = columns[:, k : k + 1] == low_name
        number = sublanes((128, 128)).astype(f32) + (k * 128 + 9999)
        slot_low = slot_low + jnp.sum(jnp.where(hit, number, 0.0), axis=0, keepdims=True)
    pack_out[PARAMS_AT : PARAMS_AT + 8, :] = jnp.zeros((8, 128), f32)
    pack_out[PARAMS_AT : PARAMS_AT + 1, :] = slot_low
    for k, ref in enumerate((level_ref, lame_ref, shear_ref), 1):
        for at in (0, 64):
            pack_out[PARAMS_AT + k : PARAMS_AT + k + 1, at : at + 64] = ref[...].astype(f32)

    def first_move():
        return bulk(pack_out.at[0:SPEED_AT], pack_in.at[0:SPEED_AT], 0, host_id)

    def second_move():
        return bulk(pack_out.at[SPEED_AT:ROWS], pack_in.at[SPEED_AT:ROWS], 1, host_id)

    if folded:

        @pl.when(away)
        def _():
            pl.semaphore_wait(barrier, 8)
            first_move().start()

        @pl.when(jnp.logical_not(away))
        def _():
            pl.semaphore_wait(barrier, 6)
    else:
        pl.semaphore_wait(barrier, 2)
    got = got + gathered([vel_ref], [mass_ref])
    for k in range(3, 7):
        at = SPEED_AT + (k - 3) * 32
        pack_out[at : at + 32, :] = got[k]
    if folded:

        @pl.when(away)
        def _():
            second_move().start()

    half16 = lanes((16, 128)) < 64
    for k in range(4):
        other = got[min(2 * k + 1, 6)][0:16]
        low_out[k * 16 : k * 16 + 16, :] = jnp.where(
            half16, got[2 * k][0:16], pltpu.roll(other, 64, axis=1)
        )
    low_out[64:72, :] = jnp.broadcast_to(slot_low, (8, 128))
    owned = float(disp_ref.shape[1])
    name_out[...] = jnp.broadcast_to(conn_s[NAMES[7] : NAMES[7] + 1, :] - owned, (8, 128))
    low_copy = pltpu.make_async_remote_copy(
        src_ref=low_out, dst_ref=low_in, send_sem=init_send.at[0], recv_sem=init_recv.at[0],
        device_id=device(low_to), device_id_type=MESH,
    )
    name_copy = pltpu.make_async_remote_copy(
        src_ref=name_out, dst_ref=name_in, send_sem=init_send.at[1], recv_sem=init_recv.at[1],
        device_id=device(name_to), device_id_type=MESH,
    )
    low_copy.start()
    name_copy.start()

    def find_places():
        for r in range(32):
            cols = slice(r * 128, r * 128 + 128)
            hit = pick_hi[r : r + 1, :] == sublanes((32, 128))
            hot_hi[0:32, cols] = jnp.where(hit, lanes((32, 128)).astype(f32), 0.0).astype(bf16)
            hot_hi[32:64, cols] = jnp.where(hit, float(r), 0.0).astype(bf16)
            hot_lo[:, cols] = same(sublanes((128, 128)), pick_lo[r : r + 1, :])
        place = lax.dot_general(
            hot_hi[...], hot_lo[...], (((1,), (1,)), ((), ())), preferred_element_type=f32
        )
        return place[0:32].astype(jnp.int32), place[32:64].astype(jnp.int32)

    place_lane, place_row = find_places()
    place_ref[0:32, :] = place_lane
    place_ref[32:64, :] = place_row
    if folded:

        @pl.when(away)
        def _():
            first_move().wait()
            second_move().wait()

        @pl.when(jnp.logical_not(away))
        def _():
            pack_in[...] = pack_out[...]

    held = pack_in if folded else pack_out
    for k, ref in enumerate([u_s] * 3 + [v_s] * 3 + [m_s]):
        at = k * 32 if k < 3 else SPEED_AT + (k - 3) * 32
        packed = held[at : at + 32, :]
        turned = pltpu.roll(packed, 64, axis=1)
        low, high = jnp.where(half, packed, turned), jnp.where(half, turned, packed)
        for a in range(4):
            at = block_at(k % 3, a) if k < 6 else a * 16
            ref[at : at + 16, :] = (low if a < 2 else high)[a % 2 * 16 : a % 2 * 16 + 16]
    u_s[MAIN : MAIN + 16, :] = jnp.zeros((16, 128), f32)
    edge_s[...] = jnp.zeros((64, 128), f32)
    elem_s[...] = held[PARAMS_AT : PARAMS_AT + 8, :]
    slot_low = elem_s[0:1, :]
    name_row = [held[NAMES_AT + k : NAMES_AT + k + 1, :] for k in range(8)]
    slot_high = name_row[7] - owned

    tile_s[0:8, :] = held[NAMES_AT : NAMES_AT + 8, :]
    columns = jnp.transpose(tile_s[...])
    name_col = [columns[:, k : k + 1] for k in range(8)]
    to_y, to_z = same(name_col[0], name_row[1]), same(name_col[2], name_row[3])
    to_edge = same(name_col[4], name_row[5])
    spread = jnp.concatenate([to_y, to_z], axis=1)
    spread = jnp.concatenate([spread, spread], axis=0)
    spread_edge = jnp.concatenate([to_edge, to_edge], axis=0)
    collect = jnp.concatenate(
        [same(name_col[1], name_row[0]), same(name_col[3], name_row[2]), same(name_col[5], name_row[4])],
        axis=1,
    )
    collect = jnp.concatenate([collect, collect], axis=0)
    to_high = same(name_col[6], name_row[7])
    to_low = same(name_col[7], name_row[6])

    low_copy.wait()
    name_copy.wait()
    tile_s[0:8, :] = low_in[64:72, :]
    tile_s[8:16, :] = name_in[...]
    columns = jnp.transpose(tile_s[...])
    from_after = same(columns[:, 0:1], slot_high)
    from_before = same(columns[:, 8:9], slot_low)
    to_high_twice = jnp.concatenate([to_high, to_high], axis=0)
    from_after_twice = jnp.concatenate([from_after, from_after], axis=0)
    theirs = []
    for k in range(7):
        packed = low_in[k // 2 * 16 : k // 2 * 16 + 16, :]
        turned = pltpu.roll(packed, 64, axis=1)
        theirs.append(jnp.where(half16 if k % 2 == 0 else jnp.logical_not(half16), packed, turned))
    ours = jnp.concatenate([u_s[0:48, :], v_s[0:48, :], m_s[0:16, :]], axis=0)
    high = moved(split_three(ours), to_high_twice)
    high = high + moved(split_three(jnp.concatenate(theirs, axis=0)), from_after_twice)
    u_s[48:96, :] = high[0:48]
    v_s[48:96, :] = high[48:96]
    m_s[64:80, :] = high[96:112]
    loads[8].wait()

    level = elem_s[1:2, :]
    period = jnp.where(level == 0.0, 8, jnp.where(level == 1.0, 4, jnp.where(level == 2.0, 2, 1)))
    row8 = sublanes((15, 8, 128))
    row16 = sublanes((16, 128))
    in_first = (row16 == 0) | (row16 == 3) | ((row16 >= 6) & (row16 < 9))
    in_second = (row16 == 1) | (row16 == 4) | ((row16 >= 9) & (row16 < 12))
    half24 = lanes((24, 128)) < 64

    def face_of(along_y, along_z):
        row = row8[0 : along_y.shape[0]]
        turned = pltpu.roll(along_z, 7, axis=1)
        return jnp.where(row < 4, along_y, jnp.where(row < 7, along_z, turned))

    def passed_on(matrix):
        onward = jnp.concatenate([to_y, to_z, to_edge], axis=1)
        return jnp.concatenate([matrix, (0.5 * moved(matrix, onward)).astype(bf16)], axis=1)

    onto_low, onto_high = passed_on(from_before), passed_on(from_after)

    def thrice(x):
        return jnp.concatenate([x, x, x], axis=0)

    for k, at in enumerate((0, 64)):
        block = m_s[at : at + 16, :]
        top = split_three(block[0:8])
        faces = moved(top, spread)
        face = face_of(faces[:, 0:128].reshape(1, 8, 128), faces[:, 128:256].reshape(1, 8, 128))
        edge = moved(top, spread_edge)
        rate_s[k * 48 : k * 48 + 48, :] = -substep_length * thrice(block)
        rate_s[96 + k * 24 : 120 + k * 24, :] = -substep_length * thrice(face.reshape(8, 128))
        rate_s[144 + k * 24 : 168 + k * 24, :] = -substep_length * thrice(edge)

    def advance(first, size, mass, force):
        rows = pl.ds(first, size)
        speed = v_s[rows, :] - substep_length * mass * force
        v_s[rows, :] = speed
        u_s[rows, :] = u_s[rows, :] + substep_length * speed

    def summed(force, planes):
        main, faces = planes * 16, planes * 24
        high = force[main:].astype(bf16)
        rest = (force[main:] - high.astype(f32)).astype(bf16)
        given = moved(jnp.concatenate([high, rest], axis=1), collect)
        along_y = given[0 : faces - main, 0:128].reshape(planes, 8, 128)
        along_z = given[0 : faces - main, 128:256].reshape(planes, 8, 128)
        edge = given[faces - main :, 256:384].reshape(planes, 8, 128)
        row = row8[0:planes]
        low = edge + jnp.where(row < 4, along_y, jnp.where(row < 7, along_z, 0.0))
        low = low + jnp.where(row == 0, pltpu.roll(along_z, 1, axis=1), 0.0)
        both = force[0:main] + pltpu.roll(force[0:main], 64, axis=1)
        both = both.reshape(planes, 2, 8, 128)
        both = jnp.concatenate([both[:, 0:1] + low[:, None], both[:, 1:2]], axis=1)
        return both.reshape(main, 128)

    def unpacked(packed):
        turned = pltpu.roll(packed, 64, axis=1)
        return jnp.concatenate(
            [jnp.where(half24, packed, turned), jnp.where(half24, turned, packed)], axis=0
        )

    def weights(s):
        active = lax.rem(jnp.full((1, 128), s, jnp.int32), period) == 0
        weight = jnp.where(active, period.astype(f32), 0.0)
        return elem_s[2:3, :] * weight, elem_s[3:4, :] * weight

    def exchange(s):
        return [
            pltpu.make_async_remote_copy(
                src_ref=send_buf.at[s, way], dst_ref=recv_buf.at[s, way],
                send_sem=step_send.at[s, way], recv_sem=step_recv.at[s, way],
                device_id=other, device_id_type=MESH,
            )
            for way, other in enumerate((before_id, after_id))
        ]

    def worked(first, size, columns, x_ref):
        rows = slice(2 * first, 2 * (first + size))
        product = jnp.dot(oper_ref[rows, columns], x_ref[...], preferred_element_type=f32)
        return product[0:size] + product[size:]

    def know(s):
        u = u_s[0:MAIN, :].reshape(15, 16, 128)
        faces = moved(split_three(u[:, 0:8].reshape(FACE, 128)), spread)
        face = face_of(faces[:, 0:128].reshape(15, 8, 128), faces[:, 128:256].reshape(15, 8, 128))
        edge = moved(split_three(u_s[pl.ds(0, 16, stride=16), :]), spread_edge)
        centres = []
        for c in range(3):
            at = block_at(c, 2) + CENTRE
            centres.append(u_s[at : at + 1, :])
        edge = edge - jnp.where(in_first, centres[0], jnp.where(in_second, centres[1], centres[2]))
        edge = jnp.where(row16 < 15, edge, 0.0)
        main = [u[k] - centres[c] for k, (c, _) in enumerate(PLANES)]
        face = [face[k] - centres[c] for k, (c, _) in enumerate(PLANES)]
        values = jnp.concatenate(main + face + [edge, jnp.zeros((8, 128), f32)], axis=0)
        for k, weight in enumerate(weights(s)):
            x_s[k * TOTAL : (k + 1) * TOTAL, :] = split_two(values * weight)
        value_s[...] = values
        known_s[...] = worked(0, OUTER, slice(0, 2 * TOTAL), x_s)

    def arrived(s):
        for copy in exchange(s)[::-1]:
            copy.wait()
        both = [
            moved(split_two(unpacked(recv_buf[s, way])), matrix)
            for way, matrix in ((1, onto_low), (0, onto_high))
        ]
        main = jnp.concatenate([x[:, 0:128] for x in both], axis=0) * rate_s[0:96, :]
        v_s[0:96, :] = v_s[0:96, :] + main
        main = substep_length * main
        u_s[0:96, :] = u_s[0:96, :] + main
        tops = [
            jnp.concatenate(
                [x[:, k * 128 : k * 128 + 128].reshape(3, 16, 128)[:, 0:8] for x in both], axis=0
            )
            for k in (1, 2, 3)
        ]
        rest = jnp.concatenate(
            [face_of(tops[0], tops[1]).reshape(48, 128), tops[2].reshape(48, 128)], axis=0
        )
        return jnp.concatenate([main, substep_length * rest * rate_s[96:192, :]], axis=0)

    def substep(s, follow):
        if follow:
            change = arrived(s - 1)
            for k, weight in enumerate(weights(s)):
                change_s[k * DELTA : (k + 1) * DELTA, :] = split_two(change * weight)
        force = known_s[...]
        if follow:
            force = force + worked(0, OUTER, slice(2 * TOTAL, 2 * TOTAL + 2 * DELTA), change_s)
        force = summed(force, SHARED)
        low_x, high_x = force[0:48], force[48:96]
        send_buf[s, 0] = jnp.where(half24, low_x[0:24], low_x[24:48])
        send_buf[s, 1] = jnp.where(half24, high_x[0:24], high_x[24:48])
        for copy in exchange(s)[::-1]:
            copy.start()
        if follow:
            edge_s[0:48, :] = change[144:192]
            edge = jnp.where(row16[0:8] < SHARED, edge_s[pl.ds(0, 8, stride=8), :], 0.0)
            none = jnp.zeros((8, 128), f32)
            last = jnp.concatenate([none, edge, none, none], axis=0)
            for at, part in ((0, change[0:96]), (MAIN, change[96:144]), (TOTAL - 32, last)):
                size = part.shape[0]
                full = value_s[at : at + size, :] + part
                for k, weight in enumerate(weights(s)):
                    x_s[k * TOTAL + at : k * TOTAL + at + size, :] = split_two(full * weight)
        inner = summed(worked(OUTER, INNER, slice(0, 2 * TOTAL), x_s), 15 - SHARED)
        low_sum = low_x + moved(split_two(high_x), to_low)
        high_sum = high_x + moved(split_two(low_x), to_high)
        advance(96, 144, thrice(m_s[16:64, :]), inner)
        advance(0, 48, thrice(m_s[0:16, :]), low_sum)
        advance(48, 48, thrice(m_s[64:80, :]), high_sum)

    def follow_on(s, carry):
        substep(s, True)
        know(s + 1)
        return carry

    know(0)
    substep(0, False)
    know(1)
    lax.fori_loop(1, substeps - 1, follow_on, 0, unroll=2)
    substep(substeps - 1, True)

    def back(part):
        rows = slice(part * 96, part * 96 + 96)
        return bulk(back_out.at[rows], back_in.at[rows], 2 + part, home_id)

    for part, a in enumerate((1, 0)):
        if part == 1:
            arrived(substeps - 1)
        for k in range(6):
            ref, at = (u_s if k < 3 else v_s), part * 96 + k * 16
            one, two = block_at(k % 3, a), block_at(k % 3, a + 2)
            back_out[at : at + 16, :] = jnp.where(
                half16, ref[one : one + 16, :], ref[two : two + 16, :]
            )
        if folded:

            @pl.when(away)
            def _():
                back(part).start()

    if folded:

        @pl.when(away)
        def _():
            for part in range(2):
                back(part).wait()
            final_ref[...] = back_in[...]

        @pl.when(jnp.logical_not(away))
        def _():
            final_ref[...] = back_out[...]
    else:
        final_ref[...] = back_out[...]


def reorder(final_ref, place_ref, out_u_ref, out_v_ref):
    place_lane, place_row = place_ref[0:32, :], place_ref[32:64, :]

    def scatter_step(t, kept):
        here = place_row == t
        first = jnp.where(t < 16, t + 96, t - 16)
        new = []
        for k in range(6):
            row = final_ref[pl.ds(k * 16 + first, 1), :]
            got = jnp.take_along_axis(
                jnp.broadcast_to(row, (32, 128)), place_lane, axis=1, mode="promise_in_bounds"
            )
            new.append(jnp.where(here, got, kept[k]))
        return tuple(new)

    done = lax.fori_loop(
        0, 32, scatter_step, tuple(jnp.zeros((32, 128), f32) for _ in range(6)), unroll=32
    )
    for k in range(6):
        ref = out_u_ref if k < 3 else out_v_ref
        for t in range(32):
            ref[k % 3 : k % 3 + 1, t * 128 : t * 128 + 128] = done[k][t : t + 1]


def per_device(
    displacement, velocity, inverse_mass, levels, first_lame, shear_modulus, connectivity, owner_list
):
    operator = jnp.asarray(element_operator())
    nodes = displacement.shape[1]
    vmem = pl.BlockSpec(memory_space=pltpu.VMEM)
    hbm = pl.BlockSpec(memory_space=pltpu.HBM)
    shape = jax.ShapeDtypeStruct((3, nodes), f32)
    V, S = pltpu.VMEM, pltpu.SemaphoreType.DMA
    operands = (
        displacement, velocity, inverse_mass.reshape(32, 128),
        levels.reshape(1, 64), first_lame.reshape(1, 64), shear_modulus.reshape(1, 64),
        connectivity.T, owner_list.reshape(4, 128), operator,
    )
    folded = lax.axis_size("dom") == 8 and lax.axis_size("lvl") == 4
    held = (jax.ShapeDtypeStruct((192, 128), f32), jax.ShapeDtypeStruct((64, 128), jnp.int32))
    final, place = pl.pallas_call(
        functools.partial(kernel, folded),
        out_shape=held,
        in_specs=[hbm] * 9,
        out_specs=(vmem, vmem),
        scratch_shapes=[V(x.shape, x.dtype) for x in operands] + [S((9,))] + [
            V((128, 128), f32), V((128, 128), f32), V((32, 128), jnp.int32),
            V((64, 4096), bf16), V((128, 4096), bf16),
            V((256, 128), f32), V((256, 128), f32), V((80, 128), f32),
            V((2 * TOTAL, 128), bf16), V((8, 128), f32),
            V((OUTER, 128), f32), V((2 * DELTA, 128), bf16), V((DELTA, 128), f32),
            V((TOTAL, 128), f32), V((64, 128), f32),
            V((ROWS, 128), f32), V((ROWS, 128), f32), V((192, 128), f32), V((192, 128), f32),
            V((72, 128), f32), V((72, 128), f32), V((8, 128), f32), V((8, 128), f32),
            V((substeps, 2, 24, 128), f32), V((substeps, 2, 24, 128), f32),
            S((2,)), S((2,)), S((substeps, 2)), S((substeps, 2)), S((4,)), S((4,)),
        ],
        compiler_params=pltpu.CompilerParams(
            collective_id=0, has_side_effects=True, vmem_limit_bytes=63 * 1024 * 1024
        ),
    )(*operands)
    return pl.pallas_call(
        reorder,
        out_shape=(shape, shape),
        in_specs=[vmem] * 2,
        out_specs=(vmem, vmem),
        compiler_params=pltpu.CompilerParams(vmem_limit_bytes=63 * 1024 * 1024),
    )(final, place)


def solution(mesh):
    in_specs = (
        P(None, ("dom", "lvl")),
        P(None, ("dom", "lvl")),
        P(("dom", "lvl")),
        P(("dom", "lvl")),
        P(("dom", "lvl")),
        P(("dom", "lvl")),
        P(None, ("dom", "lvl")),
        P(("dom", "lvl")),
    )
    out_specs = (P(None, ("dom", "lvl")), P(None, ("dom", "lvl")))
    return jax.shard_map(
        per_device, mesh=mesh, in_specs=in_specs, out_specs=out_specs, check_vma=False
    )
```
